256 devices in a mesh: ep: 64 (over z, x, core), kv: 4 (over y).
Axes of the slice: x: 4, y: 4, z: 8, core: 2. Of those that a mesh axis runs over, the one named last changes fastest.
Arguments:
- tokens: bfloat16 [8192, 4096], P('ep', 'kv'), may hold values from -6 to 6
- routes: int32 [8192, 8], P('ep'), may hold values from 0 to 63, all different within a row; in each aligned block of 128 rows (0 to 127, 128 to 255, ...) at most 20 rows name the same one
- combine_weight: float32 [8192, 8], P('ep'), may hold values from 0.1 to 0.5
- gate_weight: bfloat16 [64, 4096, 1536], P('ep', 'kv'), may hold values from -0.09375 to 0.09375
- up_weight: bfloat16 [64, 4096, 1536], P('ep', 'kv'), may hold values from -0.09375 to 0.09375
- down_weight: bfloat16 [64, 1536, 4096], P('ep', None, 'kv'), may hold values from -0.15625 to 0.15625
Outputs:
- moe_out: bfloat16 [8192, 4096], P('ep', 'kv')
The draws below stay inside these ranges and needn't reach their ends.
Inputs may be any that keep to these rules, and one draw needn't show every extreme that they name: `routes`: each row names 8 different experts; within the rows of one device no expert is named more than 20 times, a bound that some block reaches.
All inputs are finite; a program needn't handle non-finite values.
Results may differ from the reference program's by a relative error of at most 0.0057.
Values may be sent and summed in bfloat16 or wider, within the bound.
A program may use at most 128 MiB of HBM per device.

```python
import math
import jax
import jax.numpy as jnp
import numpy as np
from jax import lax

D = 4096
FF = 1536
TOPK = 8
TOK_DEV = 128
EXPERTS = 64
TOKENS = 8192
CAP = 20
N_EP = 64


def level_of(key, extent, pieces, least, largest):
    gain, own = 1.0, jax.random.fold_in(key, 6)
    for position, shards_of in pieces:
        steps = jnp.exp(jax.random.uniform(jax.random.fold_in(own, position), (shards_of,), jnp.float32, least / len(pieces), largest / len(pieces)))
        gain = gain * jnp.repeat(steps, extent[position] // shards_of).reshape([-1 if axis == position else 1 for axis in range(len(extent))])
    return gain


def deal_out(own_key, own, number, rows, count, top, bound, lean):
    sequence = jax.random.permutation(own_key, count)
    heavy_load, usual = shares(count, rows * top, bound, lean, True), shares(count, rows * top, bound, lean, False)
    places = jnp.arange(count)

    def named(lengths, offset_by):
        used = int((lengths > 0).sum())
        fixed = max(1, used // 4)
        shifted = fixed + (places - fixed + offset_by * (used - fixed)) % max(1, count - fixed)
        return jnp.zeros((count,), jnp.int32).at[sequence[jnp.where(places < fixed, places, shifted)]].set(jnp.asarray(lengths, jnp.int32))

    lengths = jnp.where(number % 4 == 0, named(heavy_load, number // 4), named(usual, number - number // 4 - 1))
    mixed = jax.random.permutation(jax.random.fold_in(own, 3), count)
    giver, receiver = mixed[0:count // 2 * 2:2], mixed[1:count // 2 * 2:2]
    slack = jnp.minimum(lengths[giver] - 1, bound - lengths[receiver]) // 2
    slack = jnp.where((giver == sequence[0]) | (receiver == sequence[0]) | (lengths[receiver] == 0), 0, jnp.maximum(slack, 0))
    shifted = jax.random.randint(jax.random.fold_in(own, 4), (count // 2,), 0, 1 << 20) % (slack + 1)
    lengths = lengths.at[giver].add(-shifted).at[receiver].add(shifted)
    members = jnp.searchsorted(jnp.cumsum(lengths), jnp.arange(rows * top), side="right").astype(jnp.int32)
    grid = members.reshape(top, rows).T
    grid = grid[jax.random.permutation(jax.random.fold_in(own, 1), rows)]
    offset_by = jax.random.randint(jax.random.fold_in(own, 2), (rows, 1), 0, top)
    return jnp.take_along_axis(grid, (jnp.arange(top)[None, :] + offset_by) % top, axis=1)


def shares(amount, total, bound, slope, full):
    weights = [(1 << 20) // math.isqrt(rank ** slope) + 1 for rank in range(1, amount + 1)]
    largest = bound if full else min(bound, max(-(-total // amount), total * weights[0] // sum(weights)))
    least = 1 if total - largest >= amount - 1 else 0
    holding, surplus = [largest] + [least] * (amount - 1), total - largest - least * (amount - 1)
    while surplus > 0:
        movable = [i for i in range(1, amount) if holding[i] < largest] or [i for i in range(1, amount) if holding[i] < bound]
        mass, remaining = sum([weights[i] for i in movable]), surplus
        for i in movable:
            extra = min(bound - holding[i], max(1, remaining * weights[i] // mass), surplus)
            holding[i] = holding[i] + extra
            surplus = surplus - extra
    return np.array(holding)


def gaussian(key, extent, width, reach, split=(), kind=jnp.bfloat16):
    gain = level_of(key, extent, split, -0.22, 0.18) if split else 1.0
    drawn = jax.random.normal(key, extent, jnp.float32) * width * gain
    return jnp.minimum(jnp.maximum(drawn, -reach), reach).astype(kind)


def setup_inputs(seed: int = 0) -> dict:
    arg_keys = jax.random.split(jax.random.key(seed), 7)
    tokens = gaussian(arg_keys[0], (TOKENS, D), 1.0, 6.0, ((0, 64), (1, 4)))
    routes_keys = jax.random.split(jax.random.fold_in(arg_keys[1], 1), TOKENS // TOK_DEV)
    routes_turns = jax.random.permutation(jax.random.fold_in(arg_keys[1], 3), TOKENS // TOK_DEV)
    routes = jax.vmap(lambda own, number: deal_out(jax.random.fold_in(arg_keys[1], 2), own, number, TOK_DEV, EXPERTS, TOPK, CAP, 2))(routes_keys, routes_turns).reshape((TOKENS, TOPK))
    combine_weight = jnp.clip(0.1 + 0.4 * jax.random.uniform(arg_keys[2], (TOKENS, TOPK), jnp.float32) ** level_of(arg_keys[2], (TOKENS, TOPK), ((0, 64),), -0.2, 0.2), 0.1, 0.5)
    gate_weight = gaussian(arg_keys[3], (EXPERTS, D, FF), D ** -0.5, 0.09375, ((0, 64), (1, 4)))
    up_weight = gaussian(arg_keys[4], (EXPERTS, D, FF), D ** -0.5, 0.09375, ((0, 64), (1, 4)))
    down_weight = gaussian(arg_keys[5], (EXPERTS, FF, D), FF ** -0.5, 0.15625, ((0, 64), (2, 4)))
    return dict(tokens=tokens, routes=routes, combine_weight=combine_weight, gate_weight=gate_weight, up_weight=up_weight, down_weight=down_weight)


def slot_targets(block_routes):
    flattened = block_routes.reshape(-1)
    one_hot = (flattened[:, None] == jnp.arange(EXPERTS, dtype=jnp.int32)[None, :]).astype(jnp.int32)
    earlier = jnp.cumsum(one_hot, axis=0) - one_hot
    return flattened * CAP + jnp.sum(earlier * one_hot, axis=1)


def place_block(target_row, owner_row, weight_row):
    token_slot = jnp.zeros((EXPERTS * CAP,), jnp.int32).at[target_row].set(owner_row)
    occupied = jnp.zeros((EXPERTS * CAP,), jnp.float32).at[target_row].set(1.0)
    route_share = jnp.zeros((EXPERTS * CAP,), jnp.float32).at[target_row].set(weight_row)
    return token_slot, occupied, route_share


def by_expert(table):
    return table.reshape(N_EP, EXPERTS, CAP).transpose(1, 0, 2).reshape(EXPERTS, N_EP * CAP)


def reference(tokens, routes, combine_weight, gate_weight, up_weight, down_weight):
    targets = jax.vmap(slot_targets)(routes.reshape(N_EP, TOK_DEV, TOPK))
    local_token = jnp.arange(TOK_DEV * TOPK, dtype=jnp.int32) // TOPK
    owners = jnp.arange(N_EP, dtype=jnp.int32)[:, None] * TOK_DEV + local_token[None, :]
    token_slot, occupied, route_share = jax.vmap(place_block)(targets, owners, combine_weight.reshape(N_EP, TOK_DEV * TOPK))

    def one_expert(running, items):
        slot_rows, slot_used, slot_share, w_gate, w_up, w_down = items
        arrived = tokens[slot_rows] * slot_used[:, None].astype(jnp.bfloat16)
        gate_sum = jnp.dot(arrived, w_gate, preferred_element_type=jnp.float32)
        up_sum = jnp.dot(arrived, w_up, preferred_element_type=jnp.float32)
        hidden = (jax.nn.silu(gate_sum) * up_sum).astype(jnp.bfloat16)
        expert_rows = jnp.dot(hidden, w_down, preferred_element_type=jnp.float32).astype(jnp.bfloat16)
        return running.at[slot_rows].add(expert_rows.astype(jnp.float32) * slot_share[:, None]), None

    start_sum = jnp.zeros((TOKENS, D), jnp.float32)
    running = lax.scan(one_expert, start_sum, (by_expert(token_slot), by_expert(occupied), by_expert(route_share), gate_weight, up_weight, down_weight))[0]
    return running.astype(jnp.bfloat16)
```

```python
import jax
import jax.numpy as jnp
from jax import lax
from jax.experimental import pallas as pl
from jax.experimental.pallas import tpu as pltpu
from jax.sharding import PartitionSpec as P

MESH = pl.DeviceIdType.MESH
F32, BF16 = jnp.float32, jnp.bfloat16
NZ, NX, NC, NY = 8, 4, 2, 4
PLANE = NX * NC
TOPK = 8
QUAD = 4

OFFSETS = (0, -1, 1, -2, 2, -3, 3, -4)
RIGHT_IN = ((0, 1), (1, 3), (3, 5), (5, 7))
LEFT_IN = ((0, 2), (2, 4), (4, 6))
LEFT_OUT = (7, 5, 3, 1)
RIGHT_OUT = (6, 4, 2)

ORDER = ((0, 0), (0, 1), (0, 2), (1, 0), (1, 2), (1, 1), (1, 3), (0, 3))
CHUNKS = len(ORDER)
POS = {key: i for i, key in enumerate(ORDER)}


def body(
    meta_ref, tok_ref, wg_ref, wu_ref, wd_ref, out_ref,
    tok_all, meta_all, vv, ww, wgu, wdn, sel, xrows, hop_s, hop_r, qf, qs, qr, own, hid, erow, back,
    zp, zs, zr,
    w_sem, zt_ss, zt_rs, zm_ss, zm_rs, x_ss, x_rs, hop_ss, hop_rs, q_ss, q_rs, ag_ss, ag_rs,
    fw_ss, fw_rs, b_ss, b_rs, z_ss, z_rs,
):
    tok, width = tok_ref.shape
    ff = wg_ref.shape[1]
    fq = ff // NY
    rows = xrows.shape[1] // 2
    cap = rows // QUAD
    ep, y = lax.axis_index("ep"), lax.axis_index("kv")
    z, x, c = ep // PLANE, lax.rem(ep // NC, NX), lax.rem(ep, NC)

    def dev(dz=0, dx=0, dc=0, dy=0):
        zz, xx, cc = lax.rem(z + dz + NZ, NZ), lax.rem(x + dx, NX), lax.rem(c + dc, NC)
        return {"ep": (zz * NX + xx) * NC + cc, "kv": lax.rem(y + dy + NY, NY)}

    def remote(src, dst, ss, rs, to):
        return pltpu.make_async_remote_copy(
            src_ref=src, dst_ref=dst, send_sem=ss, recv_sem=rs, device_id=to, device_id_type=MESH
        )

    up_y, down_y = dev(dy=1), dev(dy=-1)
    up_z, down_z = dev(dz=1), dev(dz=-1)

    def arrived(dst, rs):
        remote(dst, dst, rs, rs, up_y).wait_recv()

    def sent(src, ss):
        remote(src, src, ss, ss, up_y).wait_send()

    loads = []
    for r in range(NY):
        cols = pl.ds(pl.multiple_of(lax.rem(y + r, NY) * fq, 128), fq)
        loads += [
            pltpu.make_async_copy(wg_ref.at[:, cols], wgu.at[:, pl.ds(2 * r * fq, fq)], w_sem.at[3 * r]),
            pltpu.make_async_copy(wu_ref.at[:, cols], wgu.at[:, pl.ds((2 * r + 1) * fq, fq)], w_sem.at[3 * r + 1]),
            pltpu.make_async_copy(wd_ref.at[cols], wdn.at[pl.ds(r * fq, fq)], w_sem.at[3 * r + 2]),
        ]
    for load in loads:
        load.start()

    plane = [(dx, dc) for dx in range(NX) for dc in range(NC)]
    barrier = pltpu.get_barrier_semaphore()
    partners = [up_y, down_y, up_z, down_z] + [dev(dx=dx, dc=dc) for dx, dc in plane[1:]]
    for partner in partners:
        pl.semaphore_signal(barrier, inc=1, device_id=partner, device_id_type=MESH)
    tok_all[0] = tok_ref[...]
    meta_all[0] = meta_ref[...]
    pl.semaphore_wait(barrier, len(partners))

    def z_send(pair, to):
        src, dst = pair
        remote(meta_all.at[src], meta_all.at[dst], zm_ss.at[dst - 1], zm_rs.at[dst - 1], to).start()
        remote(tok_all.at[src], tok_all.at[dst], zt_ss.at[dst - 1], zt_rs.at[dst - 1], to).start()

    def z_arrived(dst):
        arrived(meta_all.at[dst], zm_rs.at[dst - 1])
        arrived(tok_all.at[dst], zt_rs.at[dst - 1])

    def prepare(slot):
        rt, wt = meta_all[slot, 0:TOPK, :], meta_all[slot, TOPK : 2 * TOPK, :]
        j = lax.broadcasted_iota(jnp.int32, (PLANE, tok), 0)
        expert = (z * NX + lax.rem(x + j // NC, NX)) * NC + lax.rem(c + lax.rem(j, NC), NC)
        expert = expert.astype(F32)
        hit = jnp.zeros((PLANE, tok), F32)
        share = jnp.zeros((PLANE, tok), F32)
        for k in range(TOPK):
            same = rt[k : k + 1, :] == expert
            hit += jnp.where(same, 1.0, 0.0)
            share += jnp.where(same, wt[k : k + 1, :], 0.0)
        earlier = lax.broadcasted_iota(jnp.int32, (tok, tok), 0) < lax.broadcasted_iota(jnp.int32, (tok, tok), 1)
        rank = jnp.dot(hit.astype(BF16), jnp.where(earlier, 1.0, 0.0).astype(BF16), preferred_element_type=F32)
        vv[slot] = jnp.where(hit > 0.5, rank, -1000.0)
        ww[slot] = share

    slot_row = lax.broadcasted_iota(jnp.int32, (rows, tok), 0).astype(F32)

    def select(quad, dx):
        parts = []
        for dc in range(NC):
            j = dx * NC + dc
            parts.append(
                jnp.concatenate(
                    [
                        jnp.where(slot_row - cap * q == vv[quad * QUAD + q, j : j + 1, :], 1.0, 0.0).astype(BF16)
                        for q in range(QUAD)
                    ],
                    axis=1,
                )
            )
        source = tok_all[quad * QUAD : (quad + 1) * QUAD].reshape(QUAD * tok, width)
        picked = jnp.dot(jnp.concatenate(parts, axis=0), source, preferred_element_type=F32)
        at = quad * NX + dx
        sel[at] = picked.astype(BF16)
        pos = POS[quad, (NX - dx) % NX]
        for dc in range(NC):
            src, dst = sel.at[at, pl.ds(dc * rows, rows)], xrows.at[pos, pl.ds(dc * rows, rows)]
            if dx == 0 and dc == 0:
                pltpu.make_async_copy(src, dst, x_rs.at[pos, dc]).start()
            else:
                remote(src, dst, x_ss.at[at, dc], x_rs.at[pos, dc], dev(dx=dx, dc=dc)).start()

    z_send(RIGHT_IN[0], up_z)
    z_send(LEFT_IN[0], down_z)
    prepare(0)
    z_arrived(1)
    z_send(RIGHT_IN[1], up_z)
    z_arrived(2)
    z_send(LEFT_IN[1], down_z)
    prepare(1)
    prepare(2)
    z_arrived(3)
    z_send(RIGHT_IN[2], up_z)
    prepare(3)
    for dx in (0, 3, 2, 1):
        select(0, dx)
    for load in loads:
        load.wait()

    def partials(i):
        for dc in range(NC):
            arrived(xrows.at[i, pl.ds(dc * rows, rows)], x_rs.at[i, dc])

        def part(r):
            return jnp.dot(xrows[i], wgu[:, 2 * r * fq : 2 * (r + 1) * fq], preferred_element_type=F32)

        far = part(2)
        hop_s[0, i] = far[:, :fq].astype(BF16)
        hop_s[1, i] = far[:, fq:].astype(BF16)
        remote(hop_s.at[0, i], hop_r.at[0, i], hop_ss.at[0, i], hop_rs.at[0, i], up_y).start()
        remote(hop_s.at[1, i], hop_r.at[1, i], hop_ss.at[1, i], hop_rs.at[1, i], down_y).start()
        above = part(1)
        qf[0, i] = above[:, :fq]
        qs[0, i, :, fq:] = above[:, fq:].astype(BF16)
        below = part(3)
        qs[1, i, :, :fq] = below[:, :fq].astype(BF16)
        qf[1, i] = below[:, fq:]
        own[i] = part(0)

    def middle(i):
        arrived(hop_r.at[0, i], hop_rs.at[0, i])
        qs[0, i, :, :fq] = (qf[0, i] + hop_r[0, i].astype(F32)).astype(BF16)
        remote(qs.at[0, i], qr.at[0, i], q_ss.at[0, i], q_rs.at[0, i], up_y).start()
        arrived(hop_r.at[1, i], hop_rs.at[1, i])
        qs[1, i, :, fq:] = (qf[1, i] + hop_r[1, i].astype(F32)).astype(BF16)
        remote(qs.at[1, i], qr.at[1, i], q_ss.at[1, i], q_rs.at[1, i], down_y).start()

    def quarter(i, r):
        return hid.at[i, :, pl.ds(r * fq, fq)]

    def half(i, r, h):
        return hid.at[i, pl.ds(h * rows, rows), pl.ds(r * fq, fq)]

    def activate(i):
        arrived(qr.at[0, i], q_rs.at[0, i])
        arrived(qr.at[1, i], q_rs.at[1, i])
        total = own[i] + qr[0, i].astype(F32) + qr[1, i].astype(F32)
        gate, up = total[:, :fq], total[:, fq:]
        hid[i, :, :fq] = (gate / (1.0 + jnp.exp(-gate)) * up).astype(BF16)
        remote(quarter(i, 0), quarter(i, 3), ag_ss.at[0, i], ag_rs.at[0, i], up_y).start()
        remote(quarter(i, 0), quarter(i, 1), ag_ss.at[1, i], ag_rs.at[1, i], down_y).start()

    def forward(i):
        arrived(quarter(i, 3), ag_rs.at[0, i])
        remote(half(i, 3, 0), half(i, 2, 0), fw_ss.at[0, i], fw_rs.at[0, i], up_y).start()
        arrived(quarter(i, 1), ag_rs.at[1, i])
        remote(half(i, 1, 1), half(i, 2, 1), fw_ss.at[1, i], fw_rs.at[1, i], down_y).start()

    def back_to(k):
        quad, dx = ORDER[k]
        copies = []
        for dc in range(NC):
            j = ((NX - dx) % NX) * NC + dc
            src, dst = erow.at[k, pl.ds(dc * rows, rows)], back.at[quad, pl.ds(j * rows, rows)]
            if dx == 0 and dc == 0:
                copies.append(pltpu.make_async_copy(src, dst, b_rs.at[quad, j]))
            else:
                copies.append(remote(src, dst, b_ss.at[k, dc], b_rs.at[quad, j], dev(dx=dx, dc=dc)))
        return copies

    def down(i):
        arrived(half(i, 2, 0), fw_rs.at[0, i])
        arrived(half(i, 2, 1), fw_rs.at[1, i])
        erow[i] = jnp.dot(hid[i], wdn[...], preferred_element_type=F32).astype(BF16)
        for k in range(CHUNKS):

            @pl.when(i == k)
            def _():
                for copy in back_to(k):
                    copy.start()

    def step(s, carry):
        @pl.when(s == 1)
        def _():
            z_arrived(5)
            z_send(RIGHT_IN[3], up_z)
            z_arrived(4)
            z_send(LEFT_IN[2], down_z)

        for lag, stage in enumerate((partials, middle, activate, forward, down)):

            @pl.when(jnp.logical_and(s >= lag, s < CHUNKS + lag))
            def _():
                stage(s - lag)

        @pl.when(s == 2)
        def _():
            z_arrived(6)
            z_arrived(7)
            for slot in range(QUAD, 2 * QUAD):
                prepare(slot)
            for dx in (0, 2, 3, 1):
                select(1, dx)

        return carry

    lax.fori_loop(0, CHUNKS + 4, step, 0)

    def combine(quad):
        for j in range(PLANE):
            arrived(back.at[quad, pl.ds(j * rows, rows)], b_rs.at[quad, j])

        def one(q, carry):
            slot = quad * QUAD + q
            row = slot_row - (cap * q).astype(F32)
            share = jnp.concatenate(
                [
                    jnp.where(row == vv[slot, j : j + 1, :], ww[slot, j : j + 1, :], 0.0)
                    for j in range(PLANE)
                ],
                axis=0,
            )
            high = share.astype(BF16)
            low = (share - high.astype(F32)).astype(BF16)
            both = lax.dot_general(
                jnp.concatenate([high, low], axis=1), back[quad], (((0,), (0,)), ((), ())), preferred_element_type=F32
            )
            zp[slot] = both[:tok] + both[tok:]
            return carry

        lax.fori_loop(0, QUAD, one, 0)

    nleft = len(LEFT_OUT)

    def z_out(out, base, h, to):
        total = zp[out[h]]
        if h > 0:
            arrived(zr.at[base + h - 1], z_rs.at[base + h - 1])
            total = total + zr[base + h - 1].astype(F32)
        zs[base + h] = total.astype(BF16)
        remote(zs.at[base + h], zr.at[base + h], z_ss.at[base + h], z_rs.at[base + h], to).start()

    combine(1)
    z_out(LEFT_OUT, 0, 0, down_z)
    z_out(RIGHT_OUT, nleft, 0, up_z)
    z_out(LEFT_OUT, 0, 1, down_z)
    z_out(RIGHT_OUT, nleft, 1, up_z)
    combine(0)
    z_out(LEFT_OUT, 0, 2, down_z)
    z_out(RIGHT_OUT, nleft, 2, up_z)
    z_out(LEFT_OUT, 0, 3, down_z)
    last_left, last_right = nleft - 1, nleft + len(RIGHT_OUT) - 1
    arrived(zr.at[last_right], z_rs.at[last_right])
    arrived(zr.at[last_left], z_rs.at[last_left])
    out_ref[...] = (zp[0] + zr[last_left].astype(F32) + zr[last_right].astype(F32)).astype(BF16)

    for slot in range(1, 2 * QUAD):
        sent(meta_all.at[slot], zm_ss.at[slot - 1])
        sent(tok_all.at[slot], zt_ss.at[slot - 1])
        sent(zs.at[slot - 1], z_ss.at[slot - 1])

    def drain(i, carry):
        for d in range(2):
            sent(hop_s.at[d, i], hop_ss.at[d, i])
            sent(qs.at[d, i], q_ss.at[d, i])
            sent(quarter(i, 0), ag_ss.at[d, i])
            sent(half(i, 0, 0), fw_ss.at[d, i])
        return carry

    lax.fori_loop(0, CHUNKS, drain, 0)
    for k in range(CHUNKS):
        for dc in range(NC):
            if (k % NX, dc) != (0, 0):
                sent(sel.at[k, pl.ds(0, rows)], x_ss.at[k, dc])
            if (ORDER[k][1], dc) != (0, 0):
                sent(erow.at[k, pl.ds(0, rows)], b_ss.at[k, dc])


def shards(tokens, routes, combine_weight, gate_weight, up_weight, down_weight):
    tok, width = tokens.shape
    experts = lax.axis_size("ep")
    ff = gate_weight.shape[2]
    fq = ff // NY
    cap = min(tok, 5 * tok * TOPK // (4 * experts))
    rows = QUAD * cap
    n = CHUNKS
    meta = jnp.concatenate([routes.astype(F32).T, combine_weight.T], axis=0)
    vm = pltpu.VMEM
    dma = pltpu.SemaphoreType.DMA
    any_space = pl.BlockSpec(memory_space=pl.ANY)
    return pl.pallas_call(
        body,
        out_shape=jax.ShapeDtypeStruct((tok, width), BF16),
        in_specs=[pl.BlockSpec(memory_space=vm)] * 2 + [any_space] * 3,
        out_specs=pl.BlockSpec(memory_space=vm),
        scratch_shapes=[
            vm((2 * QUAD, tok, width), BF16),
            vm((2 * QUAD, 2 * TOPK, tok), F32),
            vm((2 * QUAD, PLANE, tok), F32),
            vm((2 * QUAD, PLANE, tok), F32),
            vm((width, 2 * ff), BF16),
            vm((ff, width), BF16),
            vm((n, 2 * rows, width), BF16),
            vm((n, 2 * rows, width), BF16),
            vm((2, n, 2 * rows, fq), BF16),
            vm((2, n, 2 * rows, fq), BF16),
            vm((2, n, 2 * rows, fq), F32),
            vm((2, n, 2 * rows, 2 * fq), BF16),
            vm((2, n, 2 * rows, 2 * fq), BF16),
            vm((n, 2 * rows, 2 * fq), F32),
            vm((n, 2 * rows, ff), BF16),
            vm((n, 2 * rows, width), BF16),
            vm((2, PLANE * rows, width), BF16),
            vm((2 * QUAD, tok, width), F32),
            vm((2 * QUAD - 1, tok, width), BF16),
            vm((2 * QUAD - 1, tok, width), BF16),
            dma((3 * NY,)),
            dma((2 * QUAD - 1,)),
            dma((2 * QUAD - 1,)),
            dma((2 * QUAD - 1,)),
            dma((2 * QUAD - 1,)),
            dma((n, NC)),
            dma((n, NC)),
            dma((2, n)),
            dma((2, n)),
            dma((2, n)),
            dma((2, n)),
            dma((2, n)),
            dma((2, n)),
            dma((2, n)),
            dma((2, n)),
            dma((n, NC)),
            dma((2, PLANE)),
            dma((2 * QUAD - 1,)),
            dma((2 * QUAD - 1,)),
        ],
        compiler_params=pltpu.CompilerParams(
            collective_id=0, has_side_effects=True, vmem_limit_bytes=63 * 1024 * 1024
        ),
        cost_estimate=pl.CostEstimate(flops=12 * 10**9, bytes_accessed=10 * 10**6, transcendentals=0),
    )(meta, tokens, gate_weight[0], up_weight[0], down_weight[0])


def solution(mesh):
    return jax.shard_map(
        shards,
        mesh=mesh,
        in_specs=(
            P("ep", "kv"),
            P("ep", None),
            P("ep", None),
            P("ep", "kv", None),
            P("ep", "kv", None),
            P("ep", None, "kv"),
        ),
        out_specs=P("ep", "kv"),
        check_vma=False,
    )
```

```python
import jax
import jax.numpy as jnp
from jax import lax
from jax.experimental import pallas as pl
from jax.experimental.pallas import tpu as pltpu
from jax.sharding import PartitionSpec as P

MESH = pl.DeviceIdType.MESH
F32, BF16 = jnp.float32, jnp.bfloat16
NZ, NX, NC, NY = 8, 4, 2, 4
PLANE = NX * NC
TOPK = 8

OFFSETS = (0, -1, 1, -2, 2, -3, 3, -4)
NEXT_HOP = {0: (1, 2), 1: (3,), 2: (4,), 3: (5,), 4: (6,), 5: (7,), 6: (), 7: ()}
LEFT_OUT = (7, 5, 3, 1)
RIGHT_OUT = (6, 4, 2)

MAIN, TAIL, CUT = 16, 4, 4

ORDER = tuple(
    tuple(divmod(unit, 10) for unit in chunk)
    for chunk in (
        (3, 1),
        (20, 10),
        (12, 21, 11, 13),
        (50, 31, 32, 33),
        (61, 71, 51, 53),
        (70, 52, 73, 72),
        (62, 63, 60, 42),
        (30, 43, 41, 40),
        (23, 22),
        (2, 0),
    )
)
CHUNKS, SMALL, LARGE = len(ORDER), 2, 4
LOW, HIGH = 2, CHUNKS - 2
POS = {unit: (k, a) for k, units in enumerate(ORDER) for a, unit in enumerate(units)}
UROWS = NC * MAIN
UNIT = NC * (MAIN + TAIL)
ROWS = LARGE * UNIT

PLANE_IN, COMBINE, LEAVE = 0, 1, 2
FIRST = ()
AFTER_P = {0: ((PLANE_IN, 1), (PLANE_IN, 2),), 3: ((PLANE_IN, 7),), 8: ((COMBINE, 5), (COMBINE, 7), (LEAVE, 7),), 9: ((LEAVE, 5),)}
AFTER_A = {9: ((COMBINE, 6), (LEAVE, 6),), 10: ((LEAVE, 4),)}
AFTER_D = {2: ((PLANE_IN, 5), (PLANE_IN, 6),), 5: ((COMBINE, 1),)}
AFTER_M = {1: ((PLANE_IN, 3), (PLANE_IN, 4),)}
AFTER_F = {9: ((COMBINE, 3), (COMBINE, 4), (LEAVE, 3),)}
LAST = ((LEAVE, 1), (COMBINE, 2), (LEAVE, 2), (COMBINE, 0),)

def body(
    rt_ref, wt_ref, tok_ref, wg_ref, wu_ref, wd_ref, out_ref,
    tok_all, meta_all, vv, ww, wgu, wdn, sel, xin, xrows, hop_s, hop_r, qf, qs, qr, own, hid, erow, eout, back,
    zp, zs, zr,
    w_sem, zt_ss, zt_rs, zm_ss, zm_rs, x_ss, x_rs, hop_ss, hop_rs, q_ss, q_rs, ag_ss, ag_rs,
    fw_ss, fw_rs, b_ss, b_rs, z_ss, z_rs,
):
    tok, width = tok_ref.shape
    ff = wg_ref.shape[1]
    fq = ff // NY
    block = width // CUT
    ep, y = lax.axis_index("ep"), lax.axis_index("kv")
    z, x, c = ep // PLANE, lax.rem(ep // NC, NX), lax.rem(ep, NC)

    def dev(dz=0, dx=0, dc=0, dy=0):
        zz, xx, cc = lax.rem(z + dz + NZ, NZ), lax.rem(x + dx, NX), lax.rem(c + dc, NC)
        return {"ep": (zz * NX + xx) * NC + cc, "kv": lax.rem(y + dy + NY, NY)}

    def remote(src, dst, ss, rs, to):
        return pltpu.make_async_remote_copy(
            src_ref=src, dst_ref=dst, send_sem=ss, recv_sem=rs, device_id=to, device_id_type=MESH
        )

    up_y, down_y = dev(dy=1), dev(dy=-1)
    up_z, down_z = dev(dz=1), dev(dz=-1)

    def arrived(dst, rs):
        remote(dst, dst, rs, rs, up_y).wait_recv()

    def sent(src, ss):
        remote(src, src, ss, ss, up_y).wait_send()

    plane = [(dx, dc) for dx in range(NX) for dc in range(NC)]
    barrier = pltpu.get_barrier_semaphore()
    partners = [up_y, down_y, up_z, down_z] + [dev(dx=dx, dc=dc) for dx, dc in plane[1:]]
    for partner in partners:
        pl.semaphore_signal(barrier, inc=1, device_id=partner, device_id_type=MESH)

    loads = []
    for r in range(NY):
        cols = pl.ds(pl.multiple_of(lax.rem(y + r, NY) * fq, 128), fq)
        loads += [
            pltpu.make_async_copy(wg_ref.at[:, cols], wgu.at[:, pl.ds(2 * r * fq, fq)], w_sem.at[3 * r]),
            pltpu.make_async_copy(wu_ref.at[:, cols], wgu.at[:, pl.ds((2 * r + 1) * fq, fq)], w_sem.at[3 * r + 1]),
            pltpu.make_async_copy(wd_ref.at[cols], wdn.at[pl.ds(r * fq, fq)], w_sem.at[3 * r + 2]),
        ]
    for load in loads:
        load.start()

    place = lax.rem(lax.broadcasted_iota(jnp.int32, (PLANE * MAIN, tok), 0), MAIN)
    main_slot = place.astype(F32)
    tail_slot = [
        jnp.where(lax.rem(place, CUT) == b, MAIN + place // CUT, -1).astype(F32) for b in range(CUT)
    ]

    def spread(rows):
        return jnp.concatenate([jnp.broadcast_to(rows[j : j + 1, :], (MAIN, tok)) for j in range(PLANE)], axis=0)

    def prepare(p):
        rt, wt = meta_all[p, 0:TOPK, :], meta_all[p, TOPK : 2 * TOPK, :]
        j = lax.broadcasted_iota(jnp.int32, (PLANE, tok), 0)
        expert = (z * NX + lax.rem(x + j // NC, NX)) * NC + lax.rem(c + lax.rem(j, NC), NC)
        expert = expert.astype(F32)
        hit = jnp.zeros((PLANE, tok), F32)
        share = jnp.zeros((PLANE, tok), F32)
        for k in range(TOPK):
            same = rt[k : k + 1, :] == expert
            hit += jnp.where(same, 1.0, 0.0)
            share += jnp.where(same, wt[k : k + 1, :], 0.0)
        earlier = lax.broadcasted_iota(jnp.int32, (tok, tok), 0) < lax.broadcasted_iota(jnp.int32, (tok, tok), 1)
        rank = jnp.dot(hit.astype(BF16), jnp.where(earlier, 1.0, 0.0).astype(BF16), preferred_element_type=F32)
        vv[p] = jnp.where(hit > 0.5, rank, -1000.0)
        ww[p] = share

    def select(p):
        slot = spread(vv[p])

        def rows(of, cols):
            return jnp.dot(jnp.where(slot == of, 1.0, 0.0).astype(BF16), tok_all[p, :, cols], preferred_element_type=F32)

        sel[p, :, :width] = rows(main_slot, slice(0, width)).astype(BF16)
        tail = rows(tail_slot[0], slice(0, block))
        for b in range(1, CUT):
            tail += rows(tail_slot[b], slice(b * block, (b + 1) * block))
        sel[p, :, width:] = tail.astype(BF16)

    def dispatch(p):
        todo = []
        for dx, dc in plane:
            k, a = POS[p, (NX - dx) % NX]
            todo.append((k, dx != 2, dx, dc, a))
        for k, _, dx, dc, a in sorted(todo):
            src = sel.at[p, pl.ds((dx * NC + dc) * MAIN, MAIN)]
            dst = xin.at[k, pl.ds(a * UROWS + dc * MAIN, MAIN)]
            if dx == 0 and dc == 0:
                pltpu.make_async_copy(src, dst, x_rs.at[k, a]).start()
            else:
                remote(src, dst, x_ss, x_rs.at[k, a], dev(dx=dx, dc=dc)).start()

    def z_send(p):
        for q in NEXT_HOP[p]:
            to = up_z if OFFSETS[q] < 0 else down_z
            remote(meta_all.at[p], meta_all.at[q], zm_ss, zm_rs.at[q - 1], to).start()
            remote(tok_all.at[p], tok_all.at[q], zt_ss, zt_rs.at[q - 1], to).start()

    def z_arrived(p):
        arrived(meta_all.at[p], zm_rs.at[p - 1])
        arrived(tok_all.at[p], zt_rs.at[p - 1])
        z_send(p)
        prepare(p)
        select(p)
        dispatch(p)

    def picks(n, b, axis):
        shape = (n * UROWS // CUT, n * UROWS) if axis == 0 else (n * UROWS, n * UROWS // CUT)
        few, many = lax.broadcasted_iota(jnp.int32, shape, axis), lax.broadcasted_iota(jnp.int32, shape, 1 - axis)
        return jnp.where(many == few * CUT + b, 1.0, 0.0).astype(BF16)

    def send_y(ref, recv, i, n, ss, rs):
        for d, to in enumerate((up_y, down_y)):
            part = pl.ds(0, n * UNIT)
            remote(ref.at[d, i, part], recv.at[d, i, part], ss, rs.at[d, i], to).start()

    def partials(i, n):
        for a in range(n):
            arrived(xin.at[i, pl.ds(a * UROWS, UROWS)], x_rs.at[i, a])
        rows, whole = n * UNIT, n * UROWS
        xrows[:whole] = xin[i, :whole, :width]
        for b in range(CUT):
            tail = jnp.dot(picks(n, b, 0), xin[i, :whole, width:], preferred_element_type=F32)
            xrows[whole:rows, b * block : (b + 1) * block] = tail.astype(BF16)

        def part(r):
            return jnp.dot(xrows[:rows], wgu[:, 2 * r * fq : 2 * (r + 1) * fq], preferred_element_type=F32)

        far = part(2)
        hop_s[0, i, :rows] = far[:, :fq].astype(BF16)
        hop_s[1, i, :rows] = far[:, fq:].astype(BF16)
        send_y(hop_s, hop_r, i, n, hop_ss, hop_rs)
        above = part(1)
        qf[0, :rows] = above[:, :fq]
        qs[0, i, :rows, fq:] = above[:, fq:].astype(BF16)
        below = part(3)
        qs[1, i, :rows, :fq] = below[:, :fq].astype(BF16)
        qf[1, :rows] = below[:, fq:]
        own[lax.rem(i, 2), :rows] = part(0)

    def middle(i, n):
        rows = n * UNIT
        for d, to in enumerate((up_y, down_y)):
            arrived(hop_r.at[d, i, pl.ds(0, rows)], hop_rs.at[d, i])
            total = qf[d, :rows] + hop_r[d, i, :rows].astype(F32)
            qs[d, i, :rows, d * fq : (d + 1) * fq] = total.astype(BF16)
            part = pl.ds(0, rows)
            remote(qs.at[d, i, part], qr.at[d, i, part], q_ss, q_rs.at[d, i], to).start()

    def quarter(i, n, r):
        return hid.at[i, pl.ds(0, n * UNIT), pl.ds(r * fq, fq)]

    def half(i, n, r, h):
        first = -(-n * UNIT // 32) * 16
        at = pl.ds(0, first) if h == 0 else pl.ds(first, n * UNIT - first)
        return hid.at[i, at, pl.ds(r * fq, fq)]

    def activate(i, n):
        rows = n * UNIT
        for d in range(2):
            arrived(qr.at[d, i, pl.ds(0, rows)], q_rs.at[d, i])
        total = own[lax.rem(i, 2), :rows] + qr[0, i, :rows].astype(F32) + qr[1, i, :rows].astype(F32)
        gate, up = total[:, :fq], total[:, fq:]
        hid[i, :rows, :fq] = (gate / (1.0 + jnp.exp(-gate)) * up).astype(BF16)
        remote(quarter(i, n, 0), quarter(i, n, 3), ag_ss, ag_rs.at[0, i], up_y).start()
        remote(quarter(i, n, 0), quarter(i, n, 1), ag_ss, ag_rs.at[1, i], down_y).start()

    def forward(i, n):
        arrived(quarter(i, n, 3), ag_rs.at[0, i])
        remote(half(i, n, 3, 0), half(i, n, 2, 0), fw_ss, fw_rs.at[0, i], up_y).start()
        arrived(quarter(i, n, 1), ag_rs.at[1, i])
        remote(half(i, n, 1, 1), half(i, n, 2, 1), fw_ss, fw_rs.at[1, i], down_y).start()

    def send_back(k):
        todo = sorted((dx != 2, a, p, dx, dc) for a, (p, dx) in enumerate(ORDER[k]) for dc in range(NC))
        for _, a, p, dx, dc in todo:
            d = (NX - dx) % NX
            src = eout.at[k, pl.ds(a * UROWS + dc * MAIN, MAIN)]
            dst = back.at[p, pl.ds((d * NC + dc) * MAIN, MAIN)]
            if dx == 0 and dc == 0:
                pltpu.make_async_copy(src, dst, b_rs.at[p, d]).start()
            else:
                remote(src, dst, b_ss, b_rs.at[p, d], dev(dx=dx, dc=dc)).start()

    def down(i, n):
        arrived(half(i, n, 2, 0), fw_rs.at[0, i])
        arrived(half(i, n, 2, 1), fw_rs.at[1, i])
        rows, whole = n * UNIT, n * UROWS
        erow[:rows] = jnp.dot(hid[i, :rows], wdn[...], preferred_element_type=F32).astype(BF16)
        eout[i, :whole, :width] = erow[:whole]
        tail = jnp.zeros((whole, block), F32)
        for b in range(CUT):
            last = erow[whole:rows, b * block : (b + 1) * block]
            tail += jnp.dot(picks(n, b, 1), last, preferred_element_type=F32)
        eout[i, :whole, width:] = tail.astype(BF16)
        for k in range(CHUNKS):
            if len(ORDER[k]) == n:
                pl.when(i == k)(lambda k=k: send_back(k))

    def combine(p):
        for d in range(NX):
            arrived(back.at[p, pl.ds(d * UROWS, UROWS)], b_rs.at[p, d])
        slot, share = spread(vv[p]), spread(ww[p])

        def weighted(of, cols):
            exact = jnp.where(slot == of, share, 0.0)
            high = exact.astype(BF16)
            low = (exact - high.astype(F32)).astype(BF16)
            both = lax.dot_general(
                jnp.concatenate([high, low], axis=1), back[p, :, cols], (((0,), (0,)), ((), ())),
                preferred_element_type=F32,
            )
            return both[:tok] + both[tok:]

        zp[p] = weighted(main_slot, slice(0, width))
        for b in range(CUT):
            zp[p, :, b * block : (b + 1) * block] += weighted(tail_slot[b], slice(width, width + block))

    def leave(p):
        out, base, to = (LEFT_OUT, 0, down_z) if p in LEFT_OUT else (RIGHT_OUT, len(LEFT_OUT), up_z)
        h = base + out.index(p)
        total = zp[p]
        if h > base:
            arrived(zr.at[h - 1], z_rs.at[h - 1])
            total = total + zr[h - 1].astype(F32)
        zs[h] = total.astype(BF16)
        remote(zs.at[h], zr.at[h], z_ss, z_rs.at[h], to).start()

    ops = {0: z_arrived, 1: combine, 2: leave}

    def perform(todo):
        for op, p in todo:
            ops[op](p)

    tok_all[0] = tok_ref[...]
    meta_all[0, 0:TOPK, :] = rt_ref[...].astype(F32)
    meta_all[0, TOPK : 2 * TOPK, :] = wt_ref[...]
    prepare(0)
    select(0)
    pl.semaphore_wait(barrier, len(partners))
    z_send(0)
    dispatch(0)
    perform(FIRST)
    for load in loads:
        load.wait()

    def step(s, carry):
        for run, lag, table in (
            (partials, 0, AFTER_P),
            (activate, 1, AFTER_A),
            (down, 2, AFTER_D),
            (middle, 0, AFTER_M),
            (forward, 1, AFTER_F),
        ):
            i = s - lag
            large = jnp.logical_and(i >= LOW, i < HIGH)
            small = jnp.logical_or(
                jnp.logical_and(i >= 0, i < LOW), jnp.logical_and(i >= HIGH, i < CHUNKS)
            )
            pl.when(large)(lambda run=run, i=i: run(i, LARGE))
            pl.when(small)(lambda run=run, i=i: run(i, SMALL))
            for at, todo in table.items():
                pl.when(s == at)(lambda todo=todo: perform(todo))
        return carry

    lax.fori_loop(0, CHUNKS + 2, step, 0)
    perform(LAST)
    last_left, last_right = len(LEFT_OUT) - 1, len(LEFT_OUT) + len(RIGHT_OUT) - 1
    arrived(zr.at[last_right], z_rs.at[last_right])
    arrived(zr.at[last_left], z_rs.at[last_left])
    out_ref[...] = (zp[0] + zr[last_left].astype(F32) + zr[last_right].astype(F32)).astype(BF16)

    sent(meta_all.at[pl.ds(1, NZ - 1)], zm_ss)
    sent(tok_all.at[pl.ds(1, NZ - 1)], zt_ss)
    sent(sel.at[:, pl.ds(MAIN, (PLANE - 1) * MAIN)], x_ss)
    sent(hop_s.at[:, pl.ds(0, NZ)], hop_ss)
    sent(qs.at[:, pl.ds(0, NZ)], q_ss)
    sent(hop_s.at[:, pl.ds(0, NZ)], ag_ss)
    sent(hop_s.at[0, pl.ds(0, NZ)], fw_ss)
    sent(sel.at[:, pl.ds(MAIN, (PLANE - 1) * MAIN)], b_ss)
    sent(zs, z_ss)


def shards(tokens, routes, combine_weight, gate_weight, up_weight, down_weight):
    tok, width = tokens.shape
    ff = gate_weight.shape[2]
    fq = ff // NY
    n = CHUNKS
    wide = width + width // CUT
    vm = pltpu.VMEM
    dma = pltpu.SemaphoreType.DMA
    any_space = pl.BlockSpec(memory_space=pl.ANY)
    return pl.pallas_call(
        body,
        out_shape=jax.ShapeDtypeStruct((tok, width), BF16),
        in_specs=[pl.BlockSpec(memory_space=vm)] * 3 + [any_space] * 3,
        out_specs=pl.BlockSpec(memory_space=vm),
        scratch_shapes=[
            vm((NZ, tok, width), BF16),
            vm((NZ, 2 * TOPK, tok), F32),
            vm((NZ, PLANE, tok), F32),
            vm((NZ, PLANE, tok), F32),
            vm((width, 2 * ff), BF16),
            vm((ff, width), BF16),
            vm((NZ, PLANE * MAIN, wide), BF16),
            vm((n, LARGE * UROWS, wide), BF16),
            vm((ROWS, width), BF16),
            vm((2, n, ROWS, fq), BF16),
            vm((2, n, ROWS, fq), BF16),
            vm((2, ROWS, fq), F32),
            vm((2, n, ROWS, 2 * fq), BF16),
            vm((2, n, ROWS, 2 * fq), BF16),
            vm((2, ROWS, 2 * fq), F32),
            vm((n, ROWS, ff), BF16),
            vm((ROWS, width), BF16),
            vm((n, LARGE * UROWS, wide), BF16),
            vm((NZ, PLANE * MAIN, wide), BF16),
            vm((NZ, tok, width), F32),
            vm((NZ - 1, tok, width), BF16),
            vm((NZ - 1, tok, width), BF16),
            dma((3 * NY,)),
            dma,
            dma((NZ - 1,)),
            dma,
            dma((NZ - 1,)),
            dma,
            dma((n, LARGE)),
            dma,
            dma((2, n)),
            dma,
            dma((2, n)),
            dma,
            dma((2, n)),
            dma,
            dma((2, n)),
            dma,
            dma((NZ, NX)),
            dma,
            dma((NZ - 1,)),
        ],
        compiler_params=pltpu.CompilerParams(
            collective_id=0, has_side_effects=True, vmem_limit_bytes=62 * 1024 * 1024
        ),
        cost_estimate=pl.CostEstimate(flops=13 * 10**9, bytes_accessed=10 * 10**6, transcendentals=0),
    )(routes.T, combine_weight.T, tokens, gate_weight[0], up_weight[0], down_weight[0])


def solution(mesh):
    return jax.shard_map(
        shards,
        mesh=mesh,
        in_specs=(
            P("ep", "kv"),
            P("ep", None),
            P("ep", None),
            P("ep", "kv", None),
            P("ep", "kv", None),
            P("ep", None, "kv"),
        ),
        out_specs=P("ep", "kv"),
        check_vma=False,
    )
```

```python
import jax
import jax.numpy as jnp
from jax import lax
from jax.experimental import pallas as pl
from jax.experimental.pallas import tpu as pltpu
from jax.sharding import PartitionSpec as P

MESH = pl.DeviceIdType.MESH
F32, BF16 = jnp.float32, jnp.bfloat16
NZ, NX, NC, NY = 8, 4, 2, 4
PLANE = NX * NC
TOPK = 8

OFFSETS = (0, -1, 1, -2, 2, -3, 3, -4)
NEXT_HOP = {0: (1, 2), 1: (3,), 2: (4,), 3: (5,), 4: (6,), 5: (7,), 6: (), 7: ()}
LEFT_OUT = (7, 5, 3, 1)
RIGHT_OUT = (6, 4, 2)

MAIN, TAIL, CUT = 16, 4, 4

ORDER = tuple(
    tuple(divmod(unit, 10) for unit in chunk)
    for chunk in (
        (1, 0),
        (20, 10),
        (11, 30, 12, 13),
        (22, 61, 51, 32),
        (42, 62, 33, 70),
        (73, 71, 63, 72),
        (53, 52, 60, 50),
        (43, 40, 41, 31),
        (21, 23),
        (2, 3),
    )
)
CHUNKS, SMALL, LARGE = len(ORDER), 2, 4
LOW, HIGH = 2, CHUNKS - 2
POS = {unit: (k, a) for k, units in enumerate(ORDER) for a, unit in enumerate(units)}
UROWS = NC * MAIN
UNIT = NC * (MAIN + TAIL)
ROWS = LARGE * UNIT

PLANE_IN, COMBINE, LEAVE, SHARE = 0, 1, 2, 3
FIRST = ()
AFTER_P = {0: ((PLANE_IN, 1), (PLANE_IN, 2),), 3: ((PLANE_IN, 7),), 5: ((COMBINE, 1),), 8: ((COMBINE, 7), (LEAVE, 7),)}
AFTER_A = {1: ((PLANE_IN, 3), (PLANE_IN, 4),), 2: ((PLANE_IN, 5), (PLANE_IN, 6),), 9: ((COMBINE, 5), (LEAVE, 5),), 10: ((COMBINE, 3), (LEAVE, 3),)}
AFTER_D = {}
AFTER_M = {8: ((COMBINE, 6), (LEAVE, 6),)}
AFTER_F = {4: ((SHARE, 1), (SHARE, 7),), 5: ((SHARE, 6), (SHARE, 5),), 6: ((SHARE, 4), (SHARE, 3),), 7: ((SHARE, 2), (SHARE, 0),), 9: ((COMBINE, 4), (LEAVE, 4),)}
LAST = ((COMBINE, 2), (LEAVE, 2), (LEAVE, 1), (COMBINE, 0),)

def body(
    rt_ref, wt_ref, tok_ref, wg_ref, wu_ref, wd_ref, out_ref,
    rt_own, tok_all, meta_all, vv, ww, shares_all, wgu, wdn, sel, xin, xrows, hop_s, hop_r, qf, qs, qr, own, hid, erow, eout, back,
    zp, zs, zr,
    in_sem, w_sem, zt_ss, zt_rs, zm_ss, zm_rs, x_ss, x_rs, hop_ss, hop_rs, q_ss, q_rs, ag_ss, ag_rs,
    fw_ss, fw_rs, b_ss, b_rs, z_ss, z_rs,
):
    tok, width = tok_ref.shape
    ff = wg_ref.shape[1]
    fq = ff // NY
    block = width // CUT
    ep, y = lax.axis_index("ep"), lax.axis_index("kv")
    z, x, c = ep // PLANE, lax.rem(ep // NC, NX), lax.rem(ep, NC)

    def dev(dz=0, dx=0, dc=0, dy=0):
        zz, xx, cc = lax.rem(z + dz + NZ, NZ), lax.rem(x + dx, NX), lax.rem(c + dc, NC)
        return {"ep": (zz * NX + xx) * NC + cc, "kv": lax.rem(y + dy + NY, NY)}

    def remote(src, dst, ss, rs, to):
        return pltpu.make_async_remote_copy(
            src_ref=src, dst_ref=dst, send_sem=ss, recv_sem=rs, device_id=to, device_id_type=MESH
        )

    up_y, down_y = dev(dy=1), dev(dy=-1)
    up_z, down_z = dev(dz=1), dev(dz=-1)
    plane = [(dx, dc) for dx in range(NX) for dc in range(NC)]
    mate = {at: dev(dx=at[0], dc=at[1]) for at in plane}

    def arrived(dst, rs):
        remote(dst, dst, rs, rs, up_y).wait_recv()

    def sent(src, ss):
        remote(src, src, ss, ss, up_y).wait_send()

    barrier = pltpu.get_barrier_semaphore()
    partners = [up_y, down_y, up_z, down_z] + [mate[at] for at in plane[1:]]
    for partner in partners:
        pl.semaphore_signal(barrier, inc=1, device_id=partner, device_id_type=MESH)

    inputs = [
        pltpu.make_async_copy(rt_ref, rt_own, in_sem.at[0]),
        pltpu.make_async_copy(wt_ref, meta_all.at[0, pl.ds(TOPK, TOPK)], in_sem.at[1]),
        pltpu.make_async_copy(tok_ref, tok_all.at[0], in_sem.at[2]),
    ]
    for load in inputs:
        load.start()

    loads = []
    for r in range(NY):
        cols = pl.ds(pl.multiple_of(lax.rem(y + r, NY) * fq, 128), fq)
        loads += [
            pltpu.make_async_copy(wg_ref.at[:, cols], wgu.at[:, pl.ds(2 * r * fq, fq)], w_sem.at[3 * r]),
            pltpu.make_async_copy(wu_ref.at[:, cols], wgu.at[:, pl.ds((2 * r + 1) * fq, fq)], w_sem.at[3 * r + 1]),
            pltpu.make_async_copy(wd_ref.at[cols], wdn.at[pl.ds(r * fq, fq)], w_sem.at[3 * r + 2]),
        ]
    for load in loads:
        load.start()

    place = lax.rem(lax.broadcasted_iota(jnp.int32, (PLANE * MAIN, tok), 0), MAIN)
    main_slot = place.astype(F32)
    tail_slot = [
        jnp.where(lax.rem(place, CUT) == b, MAIN + place // CUT, -1).astype(F32) for b in range(CUT)
    ]

    def spread(rows):
        return jnp.concatenate([jnp.broadcast_to(rows[j : j + 1, :], (MAIN, tok)) for j in range(PLANE)], axis=0)

    def prepare(p):
        rt, wt = meta_all[p, 0:TOPK, :], meta_all[p, TOPK : 2 * TOPK, :]
        j = lax.broadcasted_iota(jnp.int32, (PLANE, tok), 0)
        expert = (z * NX + lax.rem(x + j // NC, NX)) * NC + lax.rem(c + lax.rem(j, NC), NC)
        expert = expert.astype(F32)
        hit = jnp.zeros((PLANE, tok), F32)
        share = jnp.zeros((PLANE, tok), F32)
        for k in range(TOPK):
            same = rt[k : k + 1, :] == expert
            hit += jnp.where(same, 1.0, 0.0)
            share += jnp.where(same, wt[k : k + 1, :], 0.0)
        earlier = lax.broadcasted_iota(jnp.int32, (tok, tok), 0) < lax.broadcasted_iota(jnp.int32, (tok, tok), 1)
        rank = jnp.dot(hit.astype(BF16), jnp.where(earlier, 1.0, 0.0).astype(BF16), preferred_element_type=F32)
        vv[p] = jnp.where(hit > 0.5, rank, -64.0)
        ww[p] = share

    def select(p):
        slot = spread(vv[p])
        tail = jnp.zeros((PLANE * MAIN, block), F32)
        first = jnp.where(slot == main_slot, 1.0, 0.0).astype(BF16)
        for b in range(CUT):
            cols = slice(b * block, (b + 1) * block)
            last = jnp.where(slot == tail_slot[b], 1.0, 0.0).astype(BF16)
            both = jnp.dot(jnp.concatenate([first, last], axis=0), tok_all[p, :, cols], preferred_element_type=F32)
            sel[p, :, cols] = both[: PLANE * MAIN].astype(BF16)
            tail += both[PLANE * MAIN :]
        sel[p, :, width:] = tail.astype(BF16)

    def share(p):
        expand = lax.broadcasted_iota(jnp.int32, (PLANE, PLANE * MAIN), 1) // MAIN
        expand = jnp.where(expand == lax.broadcasted_iota(jnp.int32, (PLANE, PLANE * MAIN), 0), 1.0, 0.0)

        def by_token(rows):
            return lax.dot_general(rows, expand, (((0,), (0,)), ((), ())), preferred_element_type=F32)

        weight = ww[p]
        high = weight.astype(BF16).astype(F32)
        slot, high, low = by_token(vv[p]), by_token(high), by_token(weight - high)
        lane = lax.rem(lax.broadcasted_iota(jnp.int32, (tok, PLANE * MAIN), 1), MAIN)
        wants = [lane] + [jnp.where(lax.rem(lane, CUT) == b, MAIN + lane // CUT, -1) for b in range(CUT)]
        for n, want in enumerate(wants):
            same = slot == want.astype(F32)
            both = jnp.concatenate([jnp.where(same, high, 0.0), jnp.where(same, low, 0.0)], axis=1)
            shares_all[p, :, 2 * n * PLANE * MAIN : 2 * (n + 1) * PLANE * MAIN] = both.astype(BF16)

    def dispatch(p):
        todo = []
        for dx, dc in plane:
            k, a = POS[p, (NX - dx) % NX]
            todo.append((k, dx != 2, dx, dc, a))
        for k, _, dx, dc, a in sorted(todo):
            src = sel.at[p, pl.ds((dx * NC + dc) * MAIN, MAIN)]
            dst = xin.at[k, pl.ds(a * UROWS + dc * MAIN, MAIN)]
            if dx == 0 and dc == 0:
                pltpu.make_async_copy(src, dst, x_rs.at[k, a]).start()
            else:
                remote(src, dst, x_ss, x_rs.at[k, a], mate[dx, dc]).start()

    def z_send(p):
        for q in NEXT_HOP[p]:
            to = up_z if OFFSETS[q] < 0 else down_z
            remote(meta_all.at[p], meta_all.at[q], zm_ss, zm_rs.at[q - 1], to).start()
            remote(tok_all.at[p], tok_all.at[q], zt_ss, zt_rs.at[q - 1], to).start()

    def z_arrived(p):
        arrived(meta_all.at[p], zm_rs.at[p - 1])
        arrived(tok_all.at[p], zt_rs.at[p - 1])
        z_send(p)
        prepare(p)
        select(p)
        dispatch(p)

    def picks(n, b, axis):
        shape = (n * UROWS // CUT, n * UROWS) if axis == 0 else (n * UROWS, n * UROWS // CUT)
        few, many = lax.broadcasted_iota(jnp.int32, shape, axis), lax.broadcasted_iota(jnp.int32, shape, 1 - axis)
        return jnp.where(many == few * CUT + b, 1.0, 0.0).astype(BF16)

    def send_y(ref, recv, i, n, ss, rs):
        for d, to in enumerate((up_y, down_y)):
            part = pl.ds(0, n * UNIT)
            remote(ref.at[d, i, part], recv.at[d, i, part], ss, rs.at[d, i], to).start()

    def partials(i, n):
        for a in range(n):
            arrived(xin.at[i, pl.ds(a * UROWS, UROWS)], x_rs.at[i, a])
        rows, whole = n * UNIT, n * UROWS
        xrows[:whole] = xin[i, :whole, :width]
        for b in range(CUT):
            tail = jnp.dot(picks(n, b, 0), xin[i, :whole, width:], preferred_element_type=F32)
            xrows[whole:rows, b * block : (b + 1) * block] = tail.astype(BF16)

        def part(r):
            return jnp.dot(xrows[:rows], wgu[:, 2 * r * fq : 2 * (r + 1) * fq], preferred_element_type=F32)

        far = part(2)
        hop_s[0, i, :rows] = far[:, :fq].astype(BF16)
        hop_s[1, i, :rows] = far[:, fq:].astype(BF16)
        send_y(hop_s, hop_r, i, n, hop_ss, hop_rs)
        above = part(1)
        qf[0, :rows] = above[:, :fq]
        qs[0, i, :rows, fq:] = above[:, fq:].astype(BF16)
        below = part(3)
        qs[1, i, :rows, :fq] = below[:, :fq].astype(BF16)
        qf[1, :rows] = below[:, fq:]
        own[lax.rem(i, 2), :rows] = part(0)

    def middle(i, n):
        rows = n * UNIT
        for d, to in enumerate((up_y, down_y)):
            arrived(hop_r.at[d, i, pl.ds(0, rows)], hop_rs.at[d, i])
            total = qf[d, :rows] + hop_r[d, i, :rows].astype(F32)
            qs[d, i, :rows, d * fq : (d + 1) * fq] = total.astype(BF16)
            part = pl.ds(0, rows)
            remote(qs.at[d, i, part], qr.at[d, i, part], q_ss, q_rs.at[d, i], to).start()

    def quarter(i, n, r):
        return hid.at[i, pl.ds(0, n * UNIT), pl.ds(r * fq, fq)]

    def half(i, n, r, h):
        first = -(-n * UNIT // 32) * 16
        at = pl.ds(0, first) if h == 0 else pl.ds(first, n * UNIT - first)
        return hid.at[i, at, pl.ds(r * fq, fq)]

    def activate(i, n):
        rows = n * UNIT
        for d in range(2):
            arrived(qr.at[d, i, pl.ds(0, rows)], q_rs.at[d, i])
        total = own[lax.rem(i, 2), :rows] + qr[0, i, :rows].astype(F32) + qr[1, i, :rows].astype(F32)
        gate, up = total[:, :fq], total[:, fq:]
        hid[i, :rows, :fq] = (gate / (1.0 + jnp.exp(-gate)) * up).astype(BF16)
        remote(quarter(i, n, 0), quarter(i, n, 3), ag_ss, ag_rs.at[0, i], up_y).start()
        remote(quarter(i, n, 0), quarter(i, n, 1), ag_ss, ag_rs.at[1, i], down_y).start()

    def forward(i, n):
        arrived(quarter(i, n, 3), ag_rs.at[0, i])
        remote(half(i, n, 3, 0), half(i, n, 2, 0), fw_ss, fw_rs.at[0, i], up_y).start()
        arrived(quarter(i, n, 1), ag_rs.at[1, i])
        remote(half(i, n, 1, 1), half(i, n, 2, 1), fw_ss, fw_rs.at[1, i], down_y).start()

    def send_back(k):
        todo = sorted((dx != 2, a, p, dx, dc) for a, (p, dx) in enumerate(ORDER[k]) for dc in range(NC))
        for _, a, p, dx, dc in todo:
            d = (NX - dx) % NX
            src = eout.at[k, pl.ds(a * UROWS + dc * MAIN, MAIN)]
            dst = back.at[p, pl.ds((d * NC + dc) * MAIN, MAIN)]
            if dx == 0 and dc == 0:
                pltpu.make_async_copy(src, dst, b_rs.at[p, d]).start()
            else:
                remote(src, dst, b_ss, b_rs.at[p, d], mate[dx, dc]).start()

    def down(i, n):
        arrived(half(i, n, 2, 0), fw_rs.at[0, i])
        arrived(half(i, n, 2, 1), fw_rs.at[1, i])
        rows, whole = n * UNIT, n * UROWS
        erow[:rows] = jnp.dot(hid[i, :rows], wdn[...], preferred_element_type=F32).astype(BF16)
        eout[i, :whole, :width] = erow[:whole]
        tail = jnp.zeros((whole, block), F32)
        for b in range(CUT):
            last = erow[whole:rows, b * block : (b + 1) * block]
            tail += jnp.dot(picks(n, b, 1), last, preferred_element_type=F32)
        eout[i, :whole, width:] = tail.astype(BF16)
        for k in range(CHUNKS):
            if len(ORDER[k]) == n:
                pl.when(i == k)(lambda k=k: send_back(k))

    def combine(p):
        for d in range(NX):
            arrived(back.at[p, pl.ds(d * UROWS, UROWS)], b_rs.at[p, d])
        span = 2 * PLANE * MAIN
        last = back[p, :, width:]
        for b in range(CUT):
            cols = slice(b * block, (b + 1) * block)
            first = back[p, :, cols]
            weights = jnp.concatenate(
                [shares_all[p, :, :span], shares_all[p, :, (b + 1) * span : (b + 2) * span]], axis=1
            )
            rows = jnp.concatenate([first, first, last, last], axis=0)
            zp[p, :, cols] = jnp.dot(weights, rows, preferred_element_type=F32)

    def leave(p):
        out, base, to = (LEFT_OUT, 0, down_z) if p in LEFT_OUT else (RIGHT_OUT, len(LEFT_OUT), up_z)
        h = base + out.index(p)
        total = zp[p]
        if h > base:
            arrived(zr.at[h - 1], z_rs.at[h - 1])
            total = total + zr[h - 1].astype(F32)
        zs[h] = total.astype(BF16)
        remote(zs.at[h], zr.at[h], z_ss, z_rs.at[h], to).start()

    ops = {PLANE_IN: z_arrived, COMBINE: combine, LEAVE: leave, SHARE: share}

    def perform(todo):
        for op, p in todo:
            ops[op](p)

    for load in inputs:
        load.wait()
    meta_all[0, 0:TOPK, :] = rt_own[...].astype(F32)
    prepare(0)
    select(0)
    pl.semaphore_wait(barrier, len(partners))
    z_send(0)
    dispatch(0)
    perform(FIRST)
    for load in loads:
        load.wait()

    def step(s, carry):
        for run, lag, table in (
            (partials, 0, AFTER_P),
            (activate, 1, AFTER_A),
            (down, 2, AFTER_D),
            (middle, 0, AFTER_M),
            (forward, 1, AFTER_F),
        ):
            i = s - lag
            large = jnp.logical_and(i >= LOW, i < HIGH)
            small = jnp.logical_or(
                jnp.logical_and(i >= 0, i < LOW), jnp.logical_and(i >= HIGH, i < CHUNKS)
            )
            pl.when(large)(lambda run=run, i=i: run(i, LARGE))
            pl.when(small)(lambda run=run, i=i: run(i, SMALL))
            for at, todo in table.items():
                pl.when(s == at)(lambda todo=todo: perform(todo))
        return carry

    lax.fori_loop(0, CHUNKS + 2, step, 0)
    perform(LAST)
    last_left, last_right = len(LEFT_OUT) - 1, len(LEFT_OUT) + len(RIGHT_OUT) - 1
    arrived(zr.at[last_right], z_rs.at[last_right])
    arrived(zr.at[last_left], z_rs.at[last_left])
    out_ref[...] = (zp[0] + zr[last_left].astype(F32) + zr[last_right].astype(F32)).astype(BF16)

    sent(meta_all.at[pl.ds(1, NZ - 1)], zm_ss)
    sent(tok_all.at[pl.ds(1, NZ - 1)], zt_ss)
    sent(sel.at[:, pl.ds(MAIN, (PLANE - 1) * MAIN)], x_ss)
    sent(hop_s.at[:, pl.ds(0, NZ)], hop_ss)
    sent(qs.at[:, pl.ds(0, NZ)], q_ss)
    sent(hop_s.at[:, pl.ds(0, NZ)], ag_ss)
    sent(hop_s.at[0, pl.ds(0, NZ)], fw_ss)
    sent(sel.at[:, pl.ds(MAIN, (PLANE - 1) * MAIN)], b_ss)
    sent(zs, z_ss)


def shards(tokens, routes, combine_weight, gate_weight, up_weight, down_weight):
    tok, width = tokens.shape
    ff = gate_weight.shape[2]
    fq = ff // NY
    n = CHUNKS
    wide = width + width // CUT
    vm = pltpu.VMEM
    dma = pltpu.SemaphoreType.DMA
    any_space = pl.BlockSpec(memory_space=pl.ANY)
    return pl.pallas_call(
        body,
        out_shape=jax.ShapeDtypeStruct((tok, width), BF16),
        in_specs=[any_space] * 6,
        out_specs=pl.BlockSpec(memory_space=vm),
        scratch_shapes=[
            vm((TOPK, tok), jnp.int32),
            vm((NZ, tok, width), BF16),
            vm((NZ, 2 * TOPK, tok), F32),
            vm((NZ, PLANE, tok), F32),
            vm((NZ, PLANE, tok), F32),
            vm((NZ, tok, 2 * (1 + CUT) * PLANE * MAIN), BF16),
            vm((width, 2 * ff), BF16),
            vm((ff, width), BF16),
            vm((NZ, PLANE * MAIN, wide), BF16),
            vm((n, LARGE * UROWS, wide), BF16),
            vm((ROWS, width), BF16),
            vm((2, n, ROWS, fq), BF16),
            vm((2, n, ROWS, fq), BF16),
            vm((2, ROWS, fq), F32),
            vm((2, n, ROWS, 2 * fq), BF16),
            vm((2, n, ROWS, 2 * fq), BF16),
            vm((2, ROWS, 2 * fq), F32),
            vm((n, ROWS, ff), BF16),
            vm((ROWS, width), BF16),
            vm((n, LARGE * UROWS, wide), BF16),
            vm((NZ, PLANE * MAIN, wide), BF16),
            vm((NZ, tok, width), F32),
            vm((NZ - 1, tok, width), BF16),
            vm((NZ - 1, tok, width), BF16),
            dma((3,)),
            dma((3 * NY,)),
            dma,
            dma((NZ - 1,)),
            dma,
            dma((NZ - 1,)),
            dma,
            dma((n, LARGE)),
            dma,
            dma((2, n)),
            dma,
            dma((2, n)),
            dma,
            dma((2, n)),
            dma,
            dma((2, n)),
            dma,
            dma((NZ, NX)),
            dma,
            dma((NZ - 1,)),
        ],
        compiler_params=pltpu.CompilerParams(
            collective_id=0, has_side_effects=True, vmem_limit_bytes=62 * 1024 * 1024
        ),
        cost_estimate=pl.CostEstimate(flops=13 * 10**9, bytes_accessed=10 * 10**6, transcendentals=0),
    )(routes.T, combine_weight.T, tokens, gate_weight[0], up_weight[0], down_weight[0])


def solution(mesh):
    return jax.shard_map(
        shards,
        mesh=mesh,
        in_specs=(
            P("ep", "kv"),
            P("ep", None),
            P("ep", None),
            P("ep", "kv", None),
            P("ep", "kv", None),
            P("ep", None, "kv"),
        ),
        out_specs=P("ep", "kv"),
        check_vma=False,
    )
```

```python
import jax
import jax.numpy as jnp
from jax import lax
from jax.experimental import pallas as pl
from jax.experimental.pallas import tpu as pltpu
from jax.sharding import PartitionSpec as P

MESH = pl.DeviceIdType.MESH
F32, BF16 = jnp.float32, jnp.bfloat16
NZ, NX, NC, NY = 8, 4, 2, 4
PLANE = NX * NC
TOPK = 8

OFFSETS = (0, -1, 1, -2, 2, -3, 3, -4)
NEXT_HOP = {0: (1, 2), 1: (3,), 2: (4,), 3: (5,), 4: (6,), 5: (7,), 6: (), 7: ()}
LEFT_OUT = (7, 5, 3, 1)
RIGHT_OUT = (6, 4, 2)

MAIN, TAIL, CUT = 16, 4, 4

ORDER = tuple(
    tuple(divmod(unit, 10) for unit in chunk)
    for chunk in (
        (0, 3),
        (1, 10),
        (13, 11, 21, 12),
        (41, 60, 50, 51),
        (70, 63, 71, 61),
        (62, 53, 72, 73),
        (52, 31, 42, 43),
        (32, 40, 30, 33),
        (23, 22),
        (2, 20),
    )
)
CHUNKS, SMALL, LARGE = len(ORDER), 2, 4
POS = {unit: (k, a) for k, units in enumerate(ORDER) for a, unit in enumerate(units)}
UROWS = NC * MAIN
UNIT = NC * (MAIN + TAIL)
ROWS = LARGE * UNIT

PLANE_IN, COMBINE, LEAVE, SHARE = 0, 1, 2, 3
FIRST = ()
ALL_STEPS = tuple(range(CHUNKS + 2))
EARLY_A = (1, 2, 3, 4, 5, 6, 7, 8, 9, 10)
EARLY_M = (0, 1, 2, 3, 5, 8, 9)
EARLY_F = (1,)
LATE_A = ()
LATE_M = (4, 6, 7)
LATE_F = (2, 3, 4, 5, 6, 7, 8, 9, 10)
AFTER_P = {0: ((PLANE_IN, 1),), 6: ((SHARE, 3),), 7: ((SHARE, 7),), 8: ((COMBINE, 6),)}
AFTER_EARLY_A = {2: ((PLANE_IN, 5),), 3: ((SHARE, 2), (PLANE_IN, 7)), 8: ((COMBINE, 7), (LEAVE, 6), (LEAVE, 7)), 9: ((COMBINE, 5), (LEAVE, 5)), 10: ((LEAVE, 4),)}
AFTER_EARLY_M = {0: ((PLANE_IN, 2),), 1: ((PLANE_IN, 3), (PLANE_IN, 4)), 2: ((PLANE_IN, 6),), 5: ((SHARE, 1),)}
AFTER_EARLY_F = {}
AFTER_D = {10: ((COMBINE, 3), (LEAVE, 3))}
AFTER_A = {}
AFTER_M = {4: ((SHARE, 5),), 7: ((SHARE, 4), (SHARE, 6), (SHARE, 0))}
AFTER_F = {6: ((COMBINE, 1),), 9: ((COMBINE, 4),)}
LAST = ((COMBINE, 2), (LEAVE, 2), (LEAVE, 1), (COMBINE, 0))

def body(
    rt_ref, wt_ref, tok_ref, wg_ref, wu_ref, wd_ref, out_ref,
    rt_own, tok_all, meta_all, vv, ww, shares_all, wgu, wdn, sel, xin, xrows, hop_s, hop_r, qf, qs, qr, own, hid, erow, eout, back,
    zp, zs, zr,
    in_sem, w_sem, zt_ss, zt_rs, zm_ss, zm_rs, x_ss, x_rs, hop_ss, hop_rs, q_ss, q_rs, ag_ss, ag_rs,
    fw_ss, fw_rs, b_ss, b_rs, z_ss, z_rs,
):
    tok, width = tok_ref.shape
    ff = wg_ref.shape[1]
    fq = ff // NY
    block = width // CUT
    ep, y = lax.axis_index("ep"), lax.axis_index("kv")
    z, x, c = ep // PLANE, lax.rem(ep // NC, NX), lax.rem(ep, NC)

    def dev(dz=0, dx=0, dc=0, dy=0):
        zz, xx, cc = lax.rem(z + dz + NZ, NZ), lax.rem(x + dx, NX), lax.rem(c + dc, NC)
        return {"ep": (zz * NX + xx) * NC + cc, "kv": lax.rem(y + dy + NY, NY)}

    def remote(src, dst, ss, rs, to):
        return pltpu.make_async_remote_copy(
            src_ref=src, dst_ref=dst, send_sem=ss, recv_sem=rs, device_id=to, device_id_type=MESH
        )

    up_y, down_y = dev(dy=1), dev(dy=-1)
    up_z, down_z = dev(dz=1), dev(dz=-1)
    plane = [(dx, dc) for dx in range(NX) for dc in range(NC)]
    mate = {at: dev(dx=at[0], dc=at[1]) for at in plane}

    def arrived(dst, rs):
        remote(dst, dst, rs, rs, up_y).wait_recv()

    def sent(src, ss):
        remote(src, src, ss, ss, up_y).wait_send()

    barrier = pltpu.get_barrier_semaphore()
    partners = [up_y, down_y, up_z, down_z] + [mate[at] for at in plane[1:]]
    for partner in partners:
        pl.semaphore_signal(barrier, inc=1, device_id=partner, device_id_type=MESH)

    inputs = [
        pltpu.make_async_copy(rt_ref, rt_own, in_sem.at[0]),
        pltpu.make_async_copy(wt_ref, meta_all.at[0, pl.ds(TOPK, TOPK)], in_sem.at[1]),
        pltpu.make_async_copy(tok_ref, tok_all.at[0], in_sem.at[2]),
    ]
    for load in inputs:
        load.start()

    loads = []
    for r in range(NY):
        cols = pl.ds(pl.multiple_of(lax.rem(y + r, NY) * fq, 128), fq)
        loads += [
            pltpu.make_async_copy(wg_ref.at[:, cols], wgu.at[:, pl.ds(2 * r * fq, fq)], w_sem.at[3 * r]),
            pltpu.make_async_copy(wu_ref.at[:, cols], wgu.at[:, pl.ds((2 * r + 1) * fq, fq)], w_sem.at[3 * r + 1]),
            pltpu.make_async_copy(wd_ref.at[cols], wdn.at[pl.ds(r * fq, fq)], w_sem.at[3 * r + 2]),
        ]
    for load in loads:
        load.start()

    place = lax.rem(lax.broadcasted_iota(jnp.int32, (PLANE * MAIN, tok), 0), MAIN)
    main_slot = place.astype(F32)
    tail_slot = [
        jnp.where(lax.rem(place, CUT) == b, MAIN + place // CUT, -1).astype(F32) for b in range(CUT)
    ]

    def spread(rows):
        return jnp.concatenate([jnp.broadcast_to(rows[j : j + 1, :], (MAIN, tok)) for j in range(PLANE)], axis=0)

    def prepare(p):
        rt, wt = meta_all[p, 0:TOPK, :], meta_all[p, TOPK : 2 * TOPK, :]
        j = lax.broadcasted_iota(jnp.int32, (PLANE, tok), 0)
        expert = (z * NX + lax.rem(x + j // NC, NX)) * NC + lax.rem(c + lax.rem(j, NC), NC)
        expert = expert.astype(F32)
        hit = jnp.zeros((PLANE, tok), F32)
        share = jnp.zeros((PLANE, tok), F32)
        for k in range(TOPK):
            same = rt[k : k + 1, :] == expert
            hit += jnp.where(same, 1.0, 0.0)
            share += jnp.where(same, wt[k : k + 1, :], 0.0)
        earlier = lax.broadcasted_iota(jnp.int32, (tok, tok), 0) < lax.broadcasted_iota(jnp.int32, (tok, tok), 1)
        rank = jnp.dot(hit.astype(BF16), jnp.where(earlier, 1.0, 0.0).astype(BF16), preferred_element_type=F32)
        vv[p] = jnp.where(hit > 0.5, rank, -64.0)
        ww[p] = share

    def select(p):
        slot = spread(vv[p])
        tail = jnp.zeros((PLANE * MAIN, block), F32)
        first = jnp.where(slot == main_slot, 1.0, 0.0).astype(BF16)
        for b in range(CUT):
            cols = slice(b * block, (b + 1) * block)
            last = jnp.where(slot == tail_slot[b], 1.0, 0.0).astype(BF16)
            both = jnp.dot(jnp.concatenate([first, last], axis=0), tok_all[p, :, cols], preferred_element_type=F32)
            sel[p, :, cols] = both[: PLANE * MAIN].astype(BF16)
            tail += both[PLANE * MAIN :]
        sel[p, :, width:] = tail.astype(BF16)

    def share(p):
        expand = lax.broadcasted_iota(jnp.int32, (PLANE, PLANE * MAIN), 1) // MAIN
        expand = jnp.where(expand == lax.broadcasted_iota(jnp.int32, (PLANE, PLANE * MAIN), 0), 1.0, 0.0)

        def by_token(rows):
            return lax.dot_general(rows, expand, (((0,), (0,)), ((), ())), preferred_element_type=F32)

        weight = ww[p]
        high = weight.astype(BF16).astype(F32)
        slot, high, low = by_token(vv[p]), by_token(high), by_token(weight - high)
        lane = lax.rem(lax.broadcasted_iota(jnp.int32, (tok, PLANE * MAIN), 1), MAIN)
        wants = [lane] + [jnp.where(lax.rem(lane, CUT) == b, MAIN + lane // CUT, -1) for b in range(CUT)]
        for n, want in enumerate(wants):
            same = slot == want.astype(F32)
            both = jnp.concatenate([jnp.where(same, high, 0.0), jnp.where(same, low, 0.0)], axis=1)
            shares_all[p, :, 2 * n * PLANE * MAIN : 2 * (n + 1) * PLANE * MAIN] = both.astype(BF16)

    def dispatch(p):
        todo = []
        for dx, dc in plane:
            k, a = POS[p, (NX - dx) % NX]
            todo.append((k, dx != 2, dx, dc, a))
        for k, _, dx, dc, a in sorted(todo):
            src = sel.at[p, pl.ds((dx * NC + dc) * MAIN, MAIN)]
            dst = xin.at[k, pl.ds(a * UROWS + dc * MAIN, MAIN)]
            if dx == 0 and dc == 0:
                pltpu.make_async_copy(src, dst, x_rs.at[k, a]).start()
            else:
                remote(src, dst, x_ss, x_rs.at[k, a], mate[dx, dc]).start()

    def z_send(p):
        for q in NEXT_HOP[p]:
            to = up_z if OFFSETS[q] < 0 else down_z
            remote(meta_all.at[p], meta_all.at[q], zm_ss, zm_rs.at[q - 1], to).start()
            remote(tok_all.at[p], tok_all.at[q], zt_ss, zt_rs.at[q - 1], to).start()

    def z_arrived(p):
        arrived(meta_all.at[p], zm_rs.at[p - 1])
        arrived(tok_all.at[p], zt_rs.at[p - 1])
        z_send(p)
        prepare(p)
        select(p)
        dispatch(p)

    def picks(n, b, axis):
        shape = (n * UROWS // CUT, n * UROWS) if axis == 0 else (n * UROWS, n * UROWS // CUT)
        few, many = lax.broadcasted_iota(jnp.int32, shape, axis), lax.broadcasted_iota(jnp.int32, shape, 1 - axis)
        return jnp.where(many == few * CUT + b, 1.0, 0.0).astype(BF16)

    def send_y(ref, recv, i, n, ss, rs):
        for d, to in enumerate((up_y, down_y)):
            part = pl.ds(0, n * UNIT)
            remote(ref.at[d, i, part], recv.at[d, i, part], ss, rs.at[d, i], to).start()

    def partials(i, n):
        for a in range(n):
            arrived(xin.at[i, pl.ds(a * UROWS, UROWS)], x_rs.at[i, a])
        rows, whole = n * UNIT, n * UROWS
        xrows[:whole] = xin[i, :whole, :width]
        for b in range(CUT):
            tail = jnp.dot(picks(n, b, 0), xin[i, :whole, width:], preferred_element_type=F32)
            xrows[whole:rows, b * block : (b + 1) * block] = tail.astype(BF16)

        def part(r):
            return jnp.dot(xrows[:rows], wgu[:, 2 * r * fq : 2 * (r + 1) * fq], preferred_element_type=F32)

        far = part(2)
        hop_s[0, i, :rows] = far[:, :fq].astype(BF16)
        hop_s[1, i, :rows] = far[:, fq:].astype(BF16)
        send_y(hop_s, hop_r, i, n, hop_ss, hop_rs)
        above = part(1)
        qf[0, :rows] = above[:, :fq]
        qs[0, i, :rows, fq:] = above[:, fq:].astype(BF16)
        below = part(3)
        qs[1, i, :rows, :fq] = below[:, :fq].astype(BF16)
        qf[1, :rows] = below[:, fq:]
        own[lax.rem(i, 2), :rows] = part(0)

    def middle(i, n):
        rows = n * UNIT
        for d, to in enumerate((up_y, down_y)):
            arrived(hop_r.at[d, i, pl.ds(0, rows)], hop_rs.at[d, i])
            total = qf[d, :rows] + hop_r[d, i, :rows].astype(F32)
            qs[d, i, :rows, d * fq : (d + 1) * fq] = total.astype(BF16)
            part = pl.ds(0, rows)
            remote(qs.at[d, i, part], qr.at[d, i, part], q_ss, q_rs.at[d, i], to).start()

    def quarter(i, n, r):
        return hid.at[i, pl.ds(0, n * UNIT), pl.ds(r * fq, fq)]

    def half(i, n, r, h):
        first = -(-n * UNIT // 32) * 16
        at = pl.ds(0, first) if h == 0 else pl.ds(first, n * UNIT - first)
        return hid.at[i, at, pl.ds(r * fq, fq)]

    def activate(i, n):
        rows = n * UNIT
        for d in range(2):
            arrived(qr.at[d, i, pl.ds(0, rows)], q_rs.at[d, i])
        total = own[lax.rem(i, 2), :rows] + qr[0, i, :rows].astype(F32) + qr[1, i, :rows].astype(F32)
        gate, up = total[:, :fq], total[:, fq:]
        hid[i, :rows, :fq] = (gate / (1.0 + jnp.exp(-gate)) * up).astype(BF16)
        remote(quarter(i, n, 0), quarter(i, n, 3), ag_ss, ag_rs.at[0, i], up_y).start()
        remote(quarter(i, n, 0), quarter(i, n, 1), ag_ss, ag_rs.at[1, i], down_y).start()

    def forward(i, n):
        arrived(quarter(i, n, 3), ag_rs.at[0, i])
        remote(half(i, n, 3, 0), half(i, n, 2, 0), fw_ss, fw_rs.at[0, i], up_y).start()
        arrived(quarter(i, n, 1), ag_rs.at[1, i])
        remote(half(i, n, 1, 1), half(i, n, 2, 1), fw_ss, fw_rs.at[1, i], down_y).start()

    def send_back(k):
        todo = sorted((dx != 2, a, p, dx, dc) for a, (p, dx) in enumerate(ORDER[k]) for dc in range(NC))
        for _, a, p, dx, dc in todo:
            d = (NX - dx) % NX
            src = eout.at[k, pl.ds(a * UROWS + dc * MAIN, MAIN)]
            dst = back.at[p, pl.ds((d * NC + dc) * MAIN, MAIN)]
            if dx == 0 and dc == 0:
                pltpu.make_async_copy(src, dst, b_rs.at[p, d]).start()
            else:
                remote(src, dst, b_ss, b_rs.at[p, d], mate[dx, dc]).start()

    def down(i, n):
        arrived(half(i, n, 2, 0), fw_rs.at[0, i])
        arrived(half(i, n, 2, 1), fw_rs.at[1, i])
        rows, whole = n * UNIT, n * UROWS
        erow[:rows] = jnp.dot(hid[i, :rows], wdn[...], preferred_element_type=F32).astype(BF16)
        eout[i, :whole, :width] = erow[:whole]
        tail = jnp.zeros((whole, block), F32)
        for b in range(CUT):
            last = erow[whole:rows, b * block : (b + 1) * block]
            tail += jnp.dot(picks(n, b, 1), last, preferred_element_type=F32)
        eout[i, :whole, width:] = tail.astype(BF16)
        for k in range(CHUNKS):
            if len(ORDER[k]) == n:
                pl.when(i == k)(lambda k=k: send_back(k))

    def combine(p):
        for d in range(NX):
            arrived(back.at[p, pl.ds(d * UROWS, UROWS)], b_rs.at[p, d])
        span = 2 * PLANE * MAIN
        last = back[p, :, width:]
        for b in range(CUT):
            cols = slice(b * block, (b + 1) * block)
            first = back[p, :, cols]
            weights = jnp.concatenate(
                [shares_all[p, :, :span], shares_all[p, :, (b + 1) * span : (b + 2) * span]], axis=1
            )
            rows = jnp.concatenate([first, first, last, last], axis=0)
            zp[p, :, cols] = jnp.dot(weights, rows, preferred_element_type=F32)

    def leave(p):
        out, base, to = (LEFT_OUT, 0, down_z) if p in LEFT_OUT else (RIGHT_OUT, len(LEFT_OUT), up_z)
        h = base + out.index(p)
        total = zp[p]
        if h > base:
            arrived(zr.at[h - 1], z_rs.at[h - 1])
            total = total + zr[h - 1].astype(F32)
        zs[h] = total.astype(BF16)
        remote(zs.at[h], zr.at[h], z_ss, z_rs.at[h], to).start()

    ops = {PLANE_IN: z_arrived, COMBINE: combine, LEAVE: leave, SHARE: share}

    def one_of(s, steps):
        hit = s == steps[0]
        for t in steps[1:]:
            hit = jnp.logical_or(hit, s == t)
        return hit

    def perform(todo):
        for op, p in todo:
            ops[op](p)

    for load in inputs:
        load.wait()
    meta_all[0, 0:TOPK, :] = rt_own[...].astype(F32)
    prepare(0)
    select(0)
    pl.semaphore_wait(barrier, len(partners))
    z_send(0)
    dispatch(0)
    perform(FIRST)
    for load in loads:
        load.wait()

    def step(s, carry):
        for run, lag, steps, table in (
            (partials, 0, ALL_STEPS, AFTER_P),
            (activate, 1, EARLY_A, AFTER_EARLY_A),
            (middle, 0, EARLY_M, AFTER_EARLY_M),
            (forward, 1, EARLY_F, AFTER_EARLY_F),
            (down, 2, ALL_STEPS, AFTER_D),
            (activate, 1, LATE_A, AFTER_A),
            (middle, 0, LATE_M, AFTER_M),
            (forward, 1, LATE_F, AFTER_F),
        ):
            i = s - lag
            for n in (LARGE, SMALL):
                at = [t for t in steps if 0 <= t - lag < CHUNKS and len(ORDER[t - lag]) == n]
                if at:
                    pl.when(one_of(s, at))(lambda run=run, i=i, n=n: run(i, n))
            for at, todo in table.items():
                pl.when(s == at)(lambda todo=todo: perform(todo))
        return carry

    lax.fori_loop(0, CHUNKS + 2, step, 0)
    perform(LAST)
    last_left, last_right = len(LEFT_OUT) - 1, len(LEFT_OUT) + len(RIGHT_OUT) - 1
    arrived(zr.at[last_right], z_rs.at[last_right])
    arrived(zr.at[last_left], z_rs.at[last_left])
    out_ref[...] = (zp[0] + zr[last_left].astype(F32) + zr[last_right].astype(F32)).astype(BF16)

    sent(meta_all.at[pl.ds(1, NZ - 1)], zm_ss)
    sent(tok_all.at[pl.ds(1, NZ - 1)], zt_ss)
    sent(sel.at[:, pl.ds(MAIN, (PLANE - 1) * MAIN)], x_ss)
    sent(hop_s.at[:, pl.ds(0, NZ)], hop_ss)
    sent(qs.at[:, pl.ds(0, NZ)], q_ss)
    sent(hop_s.at[:, pl.ds(0, NZ)], ag_ss)
    sent(hop_s.at[0, pl.ds(0, NZ)], fw_ss)
    sent(sel.at[:, pl.ds(MAIN, (PLANE - 1) * MAIN)], b_ss)
    sent(zs, z_ss)


def shards(tokens, routes, combine_weight, gate_weight, up_weight, down_weight):
    tok, width = tokens.shape
    ff = gate_weight.shape[2]
    fq = ff // NY
    n = CHUNKS
    wide = width + width // CUT
    vm = pltpu.VMEM
    dma = pltpu.SemaphoreType.DMA
    any_space = pl.BlockSpec(memory_space=pl.ANY)
    return pl.pallas_call(
        body,
        out_shape=vm((tok, width), BF16),
        in_specs=[any_space] * 6,
        out_specs=pl.BlockSpec(memory_space=vm),
        scratch_shapes=[
            vm((TOPK, tok), jnp.int32),
            vm((NZ, tok, width), BF16),
            vm((NZ, 2 * TOPK, tok), F32),
            vm((NZ, PLANE, tok), F32),
            vm((NZ, PLANE, tok), F32),
            vm((NZ, tok, 2 * (1 + CUT) * PLANE * MAIN), BF16),
            vm((width, 2 * ff), BF16),
            vm((ff, width), BF16),
            vm((NZ, PLANE * MAIN, wide), BF16),
            vm((n, LARGE * UROWS, wide), BF16),
            vm((ROWS, width), BF16),
            vm((2, n, ROWS, fq), BF16),
            vm((2, n, ROWS, fq), BF16),
            vm((2, ROWS, fq), F32),
            vm((2, n, ROWS, 2 * fq), BF16),
            vm((2, n, ROWS, 2 * fq), BF16),
            vm((2, ROWS, 2 * fq), F32),
            vm((n, ROWS, ff), BF16),
            vm((ROWS, width), BF16),
            vm((n, LARGE * UROWS, wide), BF16),
            vm((NZ, PLANE * MAIN, wide), BF16),
            vm((NZ, tok, width), F32),
            vm((NZ - 1, tok, width), BF16),
            vm((NZ - 1, tok, width), BF16),
            dma((3,)),
            dma((3 * NY,)),
            dma,
            dma((NZ - 1,)),
            dma,
            dma((NZ - 1,)),
            dma,
            dma((n, LARGE)),
            dma,
            dma((2, n)),
            dma,
            dma((2, n)),
            dma,
            dma((2, n)),
            dma,
            dma((2, n)),
            dma,
            dma((NZ, NX)),
            dma,
            dma((NZ - 1,)),
        ],
        compiler_params=pltpu.CompilerParams(
            collective_id=0, has_side_effects=True, vmem_limit_bytes=60 * 1024 * 1024
        ),
        cost_estimate=pl.CostEstimate(flops=13 * 10**9, bytes_accessed=10 * 10**6, transcendentals=0),
    )(routes.T, combine_weight.T, tokens, gate_weight[0], up_weight[0], down_weight[0])


def solution(mesh):
    return jax.shard_map(
        shards,
        mesh=mesh,
        in_specs=(
            P("ep", "kv"),
            P("ep", None),
            P("ep", None),
            P("ep", "kv", None),
            P("ep", "kv", None),
            P("ep", None, "kv"),
        ),
        out_specs=P("ep", "kv"),
        check_vma=False,
    )
```

```python
import jax
import jax.numpy as jnp
from jax import lax
from jax.experimental import pallas as pl
from jax.experimental.pallas import tpu as pltpu
from jax.sharding import PartitionSpec as P

MESH = pl.DeviceIdType.MESH
F32, BF16 = jnp.float32, jnp.bfloat16
NZ, NX, NC, NY = 8, 4, 2, 4
PLANE = NX * NC
TOPK = 8

OFFSETS = (0, -1, 1, -2, 2, -3, 3, -4)
NEXT_HOP = {0: (1, 2), 1: (3,), 2: (4,), 3: (5,), 4: (6,), 5: (7,), 6: (), 7: ()}
LEFT_OUT = (7, 5, 3, 1)
RIGHT_OUT = (6, 4, 2)

MAIN, TAIL, CUT = 16, 4, 4
TILE = 256

ORDER = tuple(
    tuple(divmod(unit, 10) for unit in chunk)
    for chunk in (
        (0, 3),
        (1, 10),
        (13, 11, 21, 12),
        (41, 60, 50, 51),
        (70, 63, 71, 61),
        (62, 53, 72, 73),
        (52, 31, 42, 43),
        (32, 40, 30, 33),
        (23, 22),
        (2, 20),
    )
)
CHUNKS, SMALL, LARGE = len(ORDER), 2, 4
POS = {unit: (k, a) for k, units in enumerate(ORDER) for a, unit in enumerate(units)}
UROWS = NC * MAIN
UNIT = NC * (MAIN + TAIL)
ROWS = LARGE * UNIT

PLANE_IN, COMBINE, LEAVE, SHARE = 0, 1, 2, 3
FIRST = ()
ALL_STEPS = tuple(range(CHUNKS + 2))
EARLY_A = (1, 2, 3, 4, 5, 6, 7, 8, 9, 10)
EARLY_M = (0, 1, 2, 3, 5, 8, 9)
EARLY_F = (1,)
LATE_A = ()
LATE_M = (4, 6, 7)
LATE_F = (2, 3, 4, 5, 6, 7, 8, 9, 10)
AFTER_P = {0: ((PLANE_IN, 1),), 6: ((SHARE, 3),), 7: ((SHARE, 7),), 8: ((COMBINE, 6),)}
AFTER_EARLY_A = {2: ((PLANE_IN, 5),), 3: ((SHARE, 2), (PLANE_IN, 7)), 8: ((COMBINE, 7), (LEAVE, 6), (LEAVE, 7)), 9: ((COMBINE, 5), (LEAVE, 5)), 10: ((LEAVE, 4),)}
AFTER_EARLY_M = {0: ((PLANE_IN, 2),), 1: ((PLANE_IN, 3), (PLANE_IN, 4)), 2: ((PLANE_IN, 6),), 5: ((SHARE, 1),)}
AFTER_EARLY_F = {}
AFTER_D = {10: ((COMBINE, 3), (LEAVE, 3))}
AFTER_A = {}
AFTER_M = {4: ((SHARE, 5),), 7: ((SHARE, 4), (SHARE, 6), (SHARE, 0))}
AFTER_F = {6: ((COMBINE, 1),), 9: ((COMBINE, 4),)}
LAST = ((COMBINE, 2), (LEAVE, 2), (LEAVE, 1), (COMBINE, 0))

def body(
    rt_ref, wt_ref, tok_ref, wg_ref, wu_ref, wd_ref, out_ref,
    rt_own, tok_all, meta_all, vv, ww, shares_all, wgu, wdn, sel, xin, xrows, hop_s, hop_r, qf, qs, qr, own, hid, eout, back,
    zp, zs, zr,
    in_sem, w_sem, zt_ss, zt_rs, zm_ss, zm_rs, x_ss, x_rs, hop_ss, hop_rs, q_ss, q_rs, ag_ss, ag_rs,
    fw_ss, fw_rs, b_ss, b_rs, z_ss, z_rs,
):
    tok, width = tok_ref.shape
    ff = wg_ref.shape[1]
    fq = ff // NY
    block = width // CUT
    ep, y = lax.axis_index("ep"), lax.axis_index("kv")
    z, x, c = ep // PLANE, lax.rem(ep // NC, NX), lax.rem(ep, NC)

    def dev(dz=0, dx=0, dc=0, dy=0):
        zz, xx, cc = lax.rem(z + dz + NZ, NZ), lax.rem(x + dx, NX), lax.rem(c + dc, NC)
        return {"ep": (zz * NX + xx) * NC + cc, "kv": lax.rem(y + dy + NY, NY)}

    def remote(src, dst, ss, rs, to):
        return pltpu.make_async_remote_copy(
            src_ref=src, dst_ref=dst, send_sem=ss, recv_sem=rs, device_id=to, device_id_type=MESH
        )

    up_y, down_y = dev(dy=1), dev(dy=-1)
    up_z, down_z = dev(dz=1), dev(dz=-1)
    plane = [(dx, dc) for dx in range(NX) for dc in range(NC)]
    mate = {at: dev(dx=at[0], dc=at[1]) for at in plane}

    def arrived(dst, rs):
        remote(dst, dst, rs, rs, up_y).wait_recv()

    def sent(src, ss):
        remote(src, src, ss, ss, up_y).wait_send()

    barrier = pltpu.get_barrier_semaphore()
    partners = [up_y, down_y, up_z, down_z] + [mate[at] for at in plane[1:]]
    for partner in partners:
        pl.semaphore_signal(barrier, inc=1, device_id=partner, device_id_type=MESH)

    inputs = [
        pltpu.make_async_copy(rt_ref, rt_own, in_sem.at[0]),
        pltpu.make_async_copy(wt_ref, meta_all.at[0, pl.ds(TOPK, TOPK)], in_sem.at[1]),
        pltpu.make_async_copy(tok_ref, tok_all.at[0], in_sem.at[2]),
    ]
    for load in inputs:
        load.start()

    loads = []
    for r in range(NY):
        cols = pl.ds(pl.multiple_of(lax.rem(y + r, NY) * fq, 128), fq)
        loads += [
            pltpu.make_async_copy(wg_ref.at[:, cols], wgu.at[:, pl.ds(2 * r * fq, fq)], w_sem.at[3 * r]),
            pltpu.make_async_copy(wu_ref.at[:, cols], wgu.at[:, pl.ds((2 * r + 1) * fq, fq)], w_sem.at[3 * r + 1]),
            pltpu.make_async_copy(wd_ref.at[cols], wdn.at[pl.ds(r * fq, fq)], w_sem.at[3 * r + 2]),
        ]
    for load in loads:
        load.start()

    place = lax.rem(lax.broadcasted_iota(jnp.int32, (PLANE * MAIN, tok), 0), MAIN)
    main_slot = place.astype(F32)
    tail_slot = [
        jnp.where(lax.rem(place, CUT) == b, MAIN + place // CUT, -1).astype(F32) for b in range(CUT)
    ]

    def spread(rows):
        return jnp.concatenate([jnp.broadcast_to(rows[j : j + 1, :], (MAIN, tok)) for j in range(PLANE)], axis=0)

    def prepare(p):
        rt, wt = meta_all[p, 0:TOPK, :], meta_all[p, TOPK : 2 * TOPK, :]
        j = lax.broadcasted_iota(jnp.int32, (PLANE, tok), 0)
        expert = (z * NX + lax.rem(x + j // NC, NX)) * NC + lax.rem(c + lax.rem(j, NC), NC)
        expert = expert.astype(F32)
        hit = jnp.zeros((PLANE, tok), F32)
        share = jnp.zeros((PLANE, tok), F32)
        for k in range(TOPK):
            same = rt[k : k + 1, :] == expert
            hit += jnp.where(same, 1.0, 0.0)
            share += jnp.where(same, wt[k : k + 1, :], 0.0)
        earlier = lax.broadcasted_iota(jnp.int32, (tok, tok), 0) < lax.broadcasted_iota(jnp.int32, (tok, tok), 1)
        rank = jnp.dot(hit.astype(BF16), jnp.where(earlier, 1.0, 0.0).astype(BF16), preferred_element_type=F32)
        vv[p] = jnp.where(hit > 0.5, rank, -64.0)
        ww[p] = share

    def select(p):
        slot = spread(vv[p])
        tail = jnp.zeros((PLANE * MAIN, block), F32)
        first = jnp.where(slot == main_slot, 1.0, 0.0).astype(BF16)
        for b in range(CUT):
            cols = slice(b * block, (b + 1) * block)
            last = jnp.where(slot == tail_slot[b], 1.0, 0.0).astype(BF16)
            both = jnp.dot(jnp.concatenate([first, last], axis=0), tok_all[p, :, cols], preferred_element_type=F32)
            sel[p, :, cols] = both[: PLANE * MAIN].astype(BF16)
            tail += both[PLANE * MAIN :]
        sel[p, :, width:] = tail.astype(BF16)

    def share(p):
        expand = lax.broadcasted_iota(jnp.int32, (PLANE, PLANE * MAIN), 1) // MAIN
        expand = jnp.where(expand == lax.broadcasted_iota(jnp.int32, (PLANE, PLANE * MAIN), 0), 1.0, 0.0)

        def by_token(rows):
            return lax.dot_general(rows, expand, (((0,), (0,)), ((), ())), preferred_element_type=F32)

        weight = ww[p]
        high = weight.astype(BF16).astype(F32)
        slot, high, low = by_token(vv[p]), by_token(high), by_token(weight - high)
        lane = lax.rem(lax.broadcasted_iota(jnp.int32, (tok, PLANE * MAIN), 1), MAIN)
        wants = [lane] + [jnp.where(lax.rem(lane, CUT) == b, MAIN + lane // CUT, -1) for b in range(CUT)]
        for n, want in enumerate(wants):
            same = slot == want.astype(F32)
            both = jnp.concatenate([jnp.where(same, high, 0.0), jnp.where(same, low, 0.0)], axis=1)
            shares_all[p, :, 2 * n * PLANE * MAIN : 2 * (n + 1) * PLANE * MAIN] = both.astype(BF16)

    def dispatch(p):
        todo = []
        for dx, dc in plane:
            k, a = POS[p, (NX - dx) % NX]
            todo.append((k, dx != 2, dx, dc, a))
        for k, _, dx, dc, a in sorted(todo):
            src = sel.at[p, pl.ds((dx * NC + dc) * MAIN, MAIN)]
            dst = xin.at[k, pl.ds(a * UROWS + dc * MAIN, MAIN)]
            if dx == 0 and dc == 0:
                pltpu.make_async_copy(src, dst, x_rs.at[k, a]).start()
            else:
                remote(src, dst, x_ss, x_rs.at[k, a], mate[dx, dc]).start()

    def z_send(p):
        for q in NEXT_HOP[p]:
            to = up_z if OFFSETS[q] < 0 else down_z
            remote(meta_all.at[p], meta_all.at[q], zm_ss, zm_rs.at[q - 1], to).start()
            remote(tok_all.at[p], tok_all.at[q], zt_ss, zt_rs.at[q - 1], to).start()

    def z_arrived(p):
        arrived(meta_all.at[p], zm_rs.at[p - 1])
        arrived(tok_all.at[p], zt_rs.at[p - 1])
        z_send(p)
        prepare(p)
        select(p)
        dispatch(p)

    def picks(n, b, axis):
        shape = (n * UROWS // CUT, n * UROWS) if axis == 0 else (n * UROWS, n * UROWS // CUT)
        few, many = lax.broadcasted_iota(jnp.int32, shape, axis), lax.broadcasted_iota(jnp.int32, shape, 1 - axis)
        return jnp.where(many == few * CUT + b, 1.0, 0.0).astype(BF16)

    def send_y(ref, recv, i, n, ss, rs):
        for d, to in enumerate((up_y, down_y)):
            part = pl.ds(0, n * UNIT)
            remote(ref.at[d, i, part], recv.at[d, i, part], ss, rs.at[d, i], to).start()

    def partials(i, n):
        for a in range(n):
            arrived(xin.at[i, pl.ds(a * UROWS, UROWS)], x_rs.at[i, a])
        rows, whole = n * UNIT, n * UROWS
        xrows[:whole] = xin[i, :whole, :width]
        for b in range(CUT):
            tail = jnp.dot(picks(n, b, 0), xin[i, :whole, width:], preferred_element_type=F32)
            xrows[whole:rows, b * block : (b + 1) * block] = tail.astype(BF16)

        def part(r, sink):
            for at in range(0, 2 * fq, TILE):
                cols = slice(2 * r * fq + at, 2 * r * fq + at + TILE)
                tile = jnp.dot(xrows[:rows], wgu[:, cols], preferred_element_type=F32)
                for which in range(2):
                    low, high = max(at, which * fq), min(at + TILE, (which + 1) * fq)
                    if low < high:
                        sink(which, slice(low - which * fq, high - which * fq), tile[:, low - at : high - at])

        def far(which, cols, tile):
            hop_s[which, i, :rows, cols] = tile.astype(BF16)

        def next_to(d):
            def sink(which, cols, tile):
                if which == d:
                    qf[d, :rows, cols] = tile
                else:
                    qs[d, i, :rows, which * fq + cols.start : which * fq + cols.stop] = tile.astype(BF16)

            return sink

        def keep(which, cols, tile):
            own[lax.rem(i, 2), :rows, which * fq + cols.start : which * fq + cols.stop] = tile

        part(2, far)
        send_y(hop_s, hop_r, i, n, hop_ss, hop_rs)
        part(1, next_to(0))
        part(3, next_to(1))
        part(0, keep)

    def blocks(rows):
        step = rows // 5
        return [slice(at, at + step) for at in range(0, rows, step)]

    def middle(i, n):
        rows = n * UNIT
        for d, to in enumerate((up_y, down_y)):
            arrived(hop_r.at[d, i, pl.ds(0, rows)], hop_rs.at[d, i])
            for rs in blocks(rows):
                total = qf[d, rs] + hop_r[d, i, rs].astype(F32)
                qs[d, i, rs, d * fq : (d + 1) * fq] = total.astype(BF16)
            part = pl.ds(0, rows)
            remote(qs.at[d, i, part], qr.at[d, i, part], q_ss, q_rs.at[d, i], to).start()

    def quarter(i, n, r):
        return hid.at[i, pl.ds(0, n * UNIT), pl.ds(r * fq, fq)]

    def half(i, n, r, h):
        first = -(-n * UNIT // 32) * 16
        at = pl.ds(0, first) if h == 0 else pl.ds(first, n * UNIT - first)
        return hid.at[i, at, pl.ds(r * fq, fq)]

    def activate(i, n):
        rows = n * UNIT
        for d in range(2):
            arrived(qr.at[d, i, pl.ds(0, rows)], q_rs.at[d, i])
        for rs in blocks(rows):

            def total(which):
                cols = slice(which * fq, (which + 1) * fq)
                return own[lax.rem(i, 2), rs, cols] + qr[0, i, rs, cols].astype(F32) + qr[1, i, rs, cols].astype(F32)

            gate = total(0)
            hid[i, rs, :fq] = (gate / (1.0 + jnp.exp(-gate)) * total(1)).astype(BF16)
        remote(quarter(i, n, 0), quarter(i, n, 3), ag_ss, ag_rs.at[0, i], up_y).start()
        remote(quarter(i, n, 0), quarter(i, n, 1), ag_ss, ag_rs.at[1, i], down_y).start()

    def forward(i, n):
        arrived(quarter(i, n, 3), ag_rs.at[0, i])
        remote(half(i, n, 3, 0), half(i, n, 2, 0), fw_ss, fw_rs.at[0, i], up_y).start()
        arrived(quarter(i, n, 1), ag_rs.at[1, i])
        remote(half(i, n, 1, 1), half(i, n, 2, 1), fw_ss, fw_rs.at[1, i], down_y).start()

    def send_back(k):
        todo = sorted((dx != 2, a, p, dx, dc) for a, (p, dx) in enumerate(ORDER[k]) for dc in range(NC))
        for _, a, p, dx, dc in todo:
            d = (NX - dx) % NX
            src = eout.at[k, pl.ds(a * UROWS + dc * MAIN, MAIN)]
            dst = back.at[p, pl.ds((d * NC + dc) * MAIN, MAIN)]
            if dx == 0 and dc == 0:
                pltpu.make_async_copy(src, dst, b_rs.at[p, d]).start()
            else:
                remote(src, dst, b_ss, b_rs.at[p, d], mate[dx, dc]).start()

    def down(i, n):
        arrived(half(i, n, 2, 0), fw_rs.at[0, i])
        arrived(half(i, n, 2, 1), fw_rs.at[1, i])
        rows, whole = n * UNIT, n * UROWS
        tail = jnp.zeros((whole, block), F32)
        for b in range(CUT):
            cols = slice(b * block, (b + 1) * block)
            part = jnp.dot(hid[i, :rows], wdn[:, cols], preferred_element_type=F32).astype(BF16)
            eout[i, :whole, cols] = part[:whole]
            tail += jnp.dot(picks(n, b, 1), part[whole:], preferred_element_type=F32)
        eout[i, :whole, width:] = tail.astype(BF16)
        for k in range(CHUNKS):
            if len(ORDER[k]) == n:
                pl.when(i == k)(lambda k=k: send_back(k))

    def combine(p):
        for d in range(NX):
            arrived(back.at[p, pl.ds(d * UROWS, UROWS)], b_rs.at[p, d])
        span = 2 * PLANE * MAIN
        last = back[p, :, width:]
        for b in range(CUT):
            cols = slice(b * block, (b + 1) * block)
            first = back[p, :, cols]
            weights = jnp.concatenate(
                [shares_all[p, :, :span], shares_all[p, :, (b + 1) * span : (b + 2) * span]], axis=1
            )
            rows = jnp.concatenate([first, first, last, last], axis=0)
            zp[p, :, cols] = jnp.dot(weights, rows, preferred_element_type=F32)

    def blocks4(rows):
        return [slice(at, at + rows // 4) for at in range(0, rows, rows // 4)]

    def leave(p):
        out, base, to = (LEFT_OUT, 0, down_z) if p in LEFT_OUT else (RIGHT_OUT, len(LEFT_OUT), up_z)
        h = base + out.index(p)
        if h > base:
            arrived(zr.at[h - 1], z_rs.at[h - 1])
        for rs in blocks4(tok):
            total = zp[p, rs]
            if h > base:
                total = total + zr[h - 1, rs].astype(F32)
            zs[h, rs] = total.astype(BF16)
        remote(zs.at[h], zr.at[h], z_ss, z_rs.at[h], to).start()

    ops = {PLANE_IN: z_arrived, COMBINE: combine, LEAVE: leave, SHARE: share}

    def one_of(s, steps):
        hit = s == steps[0]
        for t in steps[1:]:
            hit = jnp.logical_or(hit, s == t)
        return hit

    def perform(todo):
        for op, p in todo:
            ops[op](p)

    for load in inputs:
        load.wait()
    meta_all[0, 0:TOPK, :] = rt_own[...].astype(F32)
    prepare(0)
    select(0)
    pl.semaphore_wait(barrier, len(partners))
    z_send(0)
    dispatch(0)
    perform(FIRST)
    for load in loads:
        load.wait()

    def step(s, carry):
        for run, lag, steps, table in (
            (partials, 0, ALL_STEPS, AFTER_P),
            (activate, 1, EARLY_A, AFTER_EARLY_A),
            (middle, 0, EARLY_M, AFTER_EARLY_M),
            (forward, 1, EARLY_F, AFTER_EARLY_F),
            (down, 2, ALL_STEPS, AFTER_D),
            (activate, 1, LATE_A, AFTER_A),
            (middle, 0, LATE_M, AFTER_M),
            (forward, 1, LATE_F, AFTER_F),
        ):
            i = s - lag
            for n in (LARGE, SMALL):
                at = [t for t in steps if 0 <= t - lag < CHUNKS and len(ORDER[t - lag]) == n]
                if at:
                    pl.when(one_of(s, at))(lambda run=run, i=i, n=n: run(i, n))
            for at, todo in table.items():
                pl.when(s == at)(lambda todo=todo: perform(todo))
        return carry

    lax.fori_loop(0, CHUNKS + 2, step, 0)
    perform(LAST)
    last_left, last_right = len(LEFT_OUT) - 1, len(LEFT_OUT) + len(RIGHT_OUT) - 1
    arrived(zr.at[last_right], z_rs.at[last_right])
    arrived(zr.at[last_left], z_rs.at[last_left])
    for rs in blocks4(tok):
        out_ref[rs] = (zp[0, rs] + zr[last_left, rs].astype(F32) + zr[last_right, rs].astype(F32)).astype(BF16)

    sent(meta_all.at[pl.ds(1, NZ - 1)], zm_ss)
    sent(tok_all.at[pl.ds(1, NZ - 1)], zt_ss)
    sent(sel.at[:, pl.ds(MAIN, (PLANE - 1) * MAIN)], x_ss)
    sent(hop_s.at[:, pl.ds(0, NZ)], hop_ss)
    sent(qs.at[:, pl.ds(0, NZ)], q_ss)
    sent(hop_s.at[:, pl.ds(0, NZ)], ag_ss)
    sent(hop_s.at[0, pl.ds(0, NZ)], fw_ss)
    sent(sel.at[:, pl.ds(MAIN, (PLANE - 1) * MAIN)], b_ss)
    sent(zs, z_ss)


def shards(tokens, routes, combine_weight, gate_weight, up_weight, down_weight):
    tok, width = tokens.shape
    ff = gate_weight.shape[2]
    fq = ff // NY
    n = CHUNKS
    wide = width + width // CUT
    vm = pltpu.VMEM
    dma = pltpu.SemaphoreType.DMA
    any_space = pl.BlockSpec(memory_space=pl.ANY)
    return pl.pallas_call(
        body,
        out_shape=vm((tok, width), BF16),
        in_specs=[any_space] * 6,
        out_specs=pl.BlockSpec(memory_space=vm),
        scratch_shapes=[
            vm((TOPK, tok), jnp.int32),
            vm((NZ, tok, width), BF16),
            vm((NZ, 2 * TOPK, tok), F32),
            vm((NZ, PLANE, tok), F32),
            vm((NZ, PLANE, tok), F32),
            vm((NZ, tok, 2 * (1 + CUT) * PLANE * MAIN), BF16),
            vm((width, 2 * ff), BF16),
            vm((ff, width), BF16),
            vm((NZ, PLANE * MAIN, wide), BF16),
            vm((n, LARGE * UROWS, wide), BF16),
            vm((ROWS, width), BF16),
            vm((2, n, ROWS, fq), BF16),
            vm((2, n, ROWS, fq), BF16),
            vm((2, ROWS, fq), F32),
            vm((2, n, ROWS, 2 * fq), BF16),
            vm((2, n, ROWS, 2 * fq), BF16),
            vm((2, ROWS, 2 * fq), F32),
            vm((n, ROWS, ff), BF16),
            vm((n, LARGE * UROWS, wide), BF16),
            vm((NZ, PLANE * MAIN, wide), BF16),
            vm((NZ, tok, width), F32),
            vm((NZ - 1, tok, width), BF16),
            vm((NZ - 1, tok, width), BF16),
            dma((3,)),
            dma((3 * NY,)),
            dma,
            dma((NZ - 1,)),
            dma,
            dma((NZ - 1,)),
            dma,
            dma((n, LARGE)),
            dma,
            dma((2, n)),
            dma,
            dma((2, n)),
            dma,
            dma((2, n)),
            dma,
            dma((2, n)),
            dma,
            dma((NZ, NX)),
            dma,
            dma((NZ - 1,)),
        ],
        compiler_params=pltpu.CompilerParams(
            collective_id=0, has_side_effects=True, vmem_limit_bytes=60 * 1024 * 1024
        ),
        cost_estimate=pl.CostEstimate(flops=13 * 10**9, bytes_accessed=10 * 10**6, transcendentals=0),
    )(routes.T, combine_weight.T, tokens, gate_weight[0], up_weight[0], down_weight[0])


def solution(mesh):
    return jax.shard_map(
        shards,
        mesh=mesh,
        in_specs=(
            P("ep", "kv"),
            P("ep", None),
            P("ep", None),
            P("ep", "kv", None),
            P("ep", "kv", None),
            P("ep", None, "kv"),
        ),
        out_specs=P("ep", "kv"),
        check_vma=False,
    )
```

```python
import jax
import jax.numpy as jnp
from jax import lax
from jax.experimental import pallas as pl
from jax.experimental.pallas import tpu as pltpu
from jax.sharding import PartitionSpec as P

MESH = pl.DeviceIdType.MESH
F32, BF16 = jnp.float32, jnp.bfloat16
NZ, NX, NC, NY = 8, 4, 2, 4
PLANE = NX * NC
TOPK = 8

OFFSETS = (0, -1, 1, -2, 2, -3, 3, -4)
NEXT_HOP = {0: (1, 2), 1: (3,), 2: (4,), 3: (5,), 4: (6,), 5: (7,), 6: (), 7: ()}
LEFT_OUT = (7, 5, 3, 1)
RIGHT_OUT = (6, 4, 2)

MAIN, TAIL, CUT = 16, 4, 4

ORDER = tuple(
    tuple(divmod(unit, 10) for unit in chunk)
    for chunk in (
        (3, 0),
        (20, 10),
        (11, 23, 12, 13),
        (41, 31, 50, 43),
        (73, 60, 61, 62),
        (71, 72, 63, 32),
        (70, 51, 52, 53),
        (33, 40, 30, 42),
        (22, 21),
        (2, 1),
    )
)
CHUNKS, SMALL, LARGE = len(ORDER), 2, 4
POS = {unit: (k, a) for k, units in enumerate(ORDER) for a, unit in enumerate(units)}
UROWS = NC * MAIN
UNIT = NC * (MAIN + TAIL)
ROWS = LARGE * UNIT

FAR = (2, 1)
RELAYED = tuple(sorted(p for chunk in ORDER[:-2] for p, dx in chunk if dx == 2))

PLANE_IN, COMBINE, LEAVE, SHARE, RELAY_OUT, RELAY_BACK = range(6)
FIRST = ()
ALL_STEPS = tuple(range(CHUNKS + 2))
EARLY_A = (1, 2, 3, 4, 5, 6, 7, 8, 9, 10)
EARLY_M = (0, 1, 2, 3, 5, 7)
EARLY_F = (1,)
LATE_A = ()
LATE_M = (4, 6, 8, 9)
LATE_F = (2, 3, 4, 5, 6, 7, 8, 9, 10)
AFTER_P = {0: ((PLANE_IN, 1),), 2: ((RELAY_OUT, 0),), 3: ((SHARE, 3),), 5: ((RELAY_OUT, 2), (RELAY_OUT, 5)), 8: ((RELAY_BACK, 6),)}
AFTER_EARLY_A = {1: ((RELAY_OUT, 1),), 3: ((RELAY_OUT, 6),), 4: ((RELAY_OUT, 7),), 5: ((RELAY_BACK, 1),), 7: ((SHARE, 4),), 8: ((SHARE, 1), (RELAY_BACK, 7)), 9: ((RELAY_BACK, 3), (COMBINE, 5))}
AFTER_EARLY_M = {0: ((PLANE_IN, 2),), 1: ((PLANE_IN, 3), (PLANE_IN, 4)), 2: ((PLANE_IN, 5), (PLANE_IN, 6)), 3: ((PLANE_IN, 7), (SHARE, 7))}
AFTER_EARLY_F = {}
AFTER_D = {10: ((COMBINE, 3), (COMBINE, 4), (LEAVE, 4), (LEAVE, 3))}
AFTER_A = {}
AFTER_M = {8: ((COMBINE, 7), (LEAVE, 7), (COMBINE, 6), (SHARE, 0)), 9: ((LEAVE, 5), (RELAY_BACK, 4))}
AFTER_F = {3: ((RELAY_OUT, 3),), 4: ((RELAY_OUT, 4),), 6: ((SHARE, 2), (SHARE, 5), (SHARE, 6)), 8: ((RELAY_BACK, 5), (LEAVE, 6)), 10: ((COMBINE, 1),)}
LAST = ((COMBINE, 2), (LEAVE, 2), (LEAVE, 1), (COMBINE, 0))

def body(
    rt_ref, wt_ref, tok_ref, wg_ref, wu_ref, wd_ref, out_ref,
    rt_own, tok_all, meta_all, vv, ww, shares_all, wgu, wdn, sel, xin, xrows, hop_s, hop_r, qf, qs, qr, own, hid, erow, eout, back,
    zp, zs, zr, out_by, back_by,
    in_sem, w_sem, zt_ss, zt_rs, zm_ss, zm_rs, x_ss, x_rs, hop_ss, hop_rs, q_ss, q_rs, ag_ss, ag_rs,
    fw_ss, fw_rs, b_ss, b_rs, z_ss, z_rs, out_ss, out_rs, home_ss, home_rs,
):
    tok, width = tok_ref.shape
    ff = wg_ref.shape[1]
    fq = ff // NY
    block = width // CUT
    ep, y = lax.axis_index("ep"), lax.axis_index("kv")
    z, x, c = ep // PLANE, lax.rem(ep // NC, NX), lax.rem(ep, NC)

    def dev(dz=0, dx=0, dc=0, dy=0):
        zz, xx, cc = lax.rem(z + dz + NZ, NZ), lax.rem(x + dx, NX), lax.rem(c + dc, NC)
        return {"ep": (zz * NX + xx) * NC + cc, "kv": lax.rem(y + dy + NY, NY)}

    def remote(src, dst, ss, rs, to):
        return pltpu.make_async_remote_copy(
            src_ref=src, dst_ref=dst, send_sem=ss, recv_sem=rs, device_id=to, device_id_type=MESH
        )

    up_y, down_y = dev(dy=1), dev(dy=-1)
    up_z, down_z = dev(dz=1), dev(dz=-1)
    plane = [(dx, dc) for dx in range(NX) for dc in range(NC)]
    mate = {at: dev(dx=at[0], dc=at[1]) for at in plane}

    def arrived(dst, rs):
        remote(dst, dst, rs, rs, up_y).wait_recv()

    def sent(src, ss):
        remote(src, src, ss, ss, up_y).wait_send()

    barrier = pltpu.get_barrier_semaphore()
    partners = [up_y, down_y, up_z, down_z] + [mate[at] for at in plane[1:]]
    for partner in partners:
        pl.semaphore_signal(barrier, inc=1, device_id=partner, device_id_type=MESH)

    inputs = [
        pltpu.make_async_copy(rt_ref, rt_own, in_sem.at[0]),
        pltpu.make_async_copy(wt_ref, meta_all.at[0, pl.ds(TOPK, TOPK)], in_sem.at[1]),
        pltpu.make_async_copy(tok_ref, tok_all.at[0], in_sem.at[2]),
    ]
    for load in inputs:
        load.start()

    loads = []
    for r in range(NY):
        cols = pl.ds(pl.multiple_of(lax.rem(y + r, NY) * fq, 128), fq)
        loads += [
            pltpu.make_async_copy(wg_ref.at[:, cols], wgu.at[:, pl.ds(2 * r * fq, fq)], w_sem.at[3 * r]),
            pltpu.make_async_copy(wu_ref.at[:, cols], wgu.at[:, pl.ds((2 * r + 1) * fq, fq)], w_sem.at[3 * r + 1]),
            pltpu.make_async_copy(wd_ref.at[cols], wdn.at[pl.ds(r * fq, fq)], w_sem.at[3 * r + 2]),
        ]
    for load in loads:
        load.start()

    place = lax.rem(lax.broadcasted_iota(jnp.int32, (PLANE * MAIN, tok), 0), MAIN)
    main_slot = place.astype(F32)
    tail_slot = [
        jnp.where(lax.rem(place, CUT) == b, MAIN + place // CUT, -1).astype(F32) for b in range(CUT)
    ]

    def spread(rows):
        return jnp.concatenate([jnp.broadcast_to(rows[j : j + 1, :], (MAIN, tok)) for j in range(PLANE)], axis=0)

    def prepare(p):
        rt, wt = meta_all[p, 0:TOPK, :], meta_all[p, TOPK : 2 * TOPK, :]
        j = lax.broadcasted_iota(jnp.int32, (PLANE, tok), 0)
        expert = (z * NX + lax.rem(x + j // NC, NX)) * NC + lax.rem(c + lax.rem(j, NC), NC)
        expert = expert.astype(F32)
        hit = jnp.zeros((PLANE, tok), F32)
        share = jnp.zeros((PLANE, tok), F32)
        for k in range(TOPK):
            same = rt[k : k + 1, :] == expert
            hit += jnp.where(same, 1.0, 0.0)
            share += jnp.where(same, wt[k : k + 1, :], 0.0)
        earlier = lax.broadcasted_iota(jnp.int32, (tok, tok), 0) < lax.broadcasted_iota(jnp.int32, (tok, tok), 1)
        rank = jnp.dot(hit.astype(BF16), jnp.where(earlier, 1.0, 0.0).astype(BF16), preferred_element_type=F32)
        vv[p] = jnp.where(hit > 0.5, rank, -64.0)
        ww[p] = share

    def select(p):
        slot = spread(vv[p])
        tail = jnp.zeros((PLANE * MAIN, block), F32)
        first = jnp.where(slot == main_slot, 1.0, 0.0).astype(BF16)
        for b in range(CUT):
            cols = slice(b * block, (b + 1) * block)
            last = jnp.where(slot == tail_slot[b], 1.0, 0.0).astype(BF16)
            both = jnp.dot(jnp.concatenate([first, last], axis=0), tok_all[p, :, cols], preferred_element_type=F32)
            sel[p, :, cols] = both[: PLANE * MAIN].astype(BF16)
            tail += both[PLANE * MAIN :]
        sel[p, :, width:] = tail.astype(BF16)

    def share(p):
        expand = lax.broadcasted_iota(jnp.int32, (PLANE, PLANE * MAIN), 1) // MAIN
        expand = jnp.where(expand == lax.broadcasted_iota(jnp.int32, (PLANE, PLANE * MAIN), 0), 1.0, 0.0)

        def by_token(rows):
            return lax.dot_general(rows, expand, (((0,), (0,)), ((), ())), preferred_element_type=F32)

        weight = ww[p]
        high = weight.astype(BF16).astype(F32)
        slot, high, low = by_token(vv[p]), by_token(high), by_token(weight - high)
        lane = lax.rem(lax.broadcasted_iota(jnp.int32, (tok, PLANE * MAIN), 1), MAIN)
        wants = [lane] + [jnp.where(lax.rem(lane, CUT) == b, MAIN + lane // CUT, -1) for b in range(CUT)]
        for n, want in enumerate(wants):
            same = slot == want.astype(F32)
            both = jnp.concatenate([jnp.where(same, high, 0.0), jnp.where(same, low, 0.0)], axis=1)
            shares_all[p, :, 2 * n * PLANE * MAIN : 2 * (n + 1) * PLANE * MAIN] = both.astype(BF16)

    def dispatch(p):
        todo = []
        for dx, dc in plane:
            k, a = POS[p, (NX - dx) % NX]
            todo.append((k, dx != 2, dx, dc, a))
        for k, _, dx, dc, a in sorted(todo):
            src = sel.at[p, pl.ds((dx * NC + dc) * MAIN, MAIN)]
            dst = xin.at[k, pl.ds(a * UROWS + dc * MAIN, MAIN)]
            if dx == 0 and dc == 0:
                pltpu.make_async_copy(src, dst, x_rs.at[k, a]).start()
            elif (dx, dc) == FAR:
                remote(src, out_by.at[p], x_ss, out_rs.at[p], mate[3, 0]).start()
            else:
                remote(src, dst, x_ss, x_rs.at[k, a], mate[dx, dc]).start()

    def relay_out(p):
        k, a = POS[p, 2]
        arrived(out_by.at[p], out_rs.at[p])
        dst = xin.at[k, pl.ds(a * UROWS + MAIN, MAIN)]
        remote(out_by.at[p], dst, out_ss, x_rs.at[k, a], mate[3, 1]).start()

    def relay_back(p):
        arrived(back_by.at[p], home_rs.at[p])
        dst = back.at[p, pl.ds((2 * NC + 1) * MAIN, MAIN)]
        remote(back_by.at[p], dst, home_ss, b_rs.at[p, 2], mate[3, 1]).start()

    def z_send(p):
        for q in NEXT_HOP[p]:
            to = up_z if OFFSETS[q] < 0 else down_z
            remote(meta_all.at[p], meta_all.at[q], zm_ss, zm_rs.at[q - 1], to).start()
            remote(tok_all.at[p], tok_all.at[q], zt_ss, zt_rs.at[q - 1], to).start()

    def z_arrived(p):
        arrived(meta_all.at[p], zm_rs.at[p - 1])
        arrived(tok_all.at[p], zt_rs.at[p - 1])
        z_send(p)
        prepare(p)
        select(p)
        dispatch(p)

    def picks(n, b, axis):
        shape = (n * UROWS // CUT, n * UROWS) if axis == 0 else (n * UROWS, n * UROWS // CUT)
        few, many = lax.broadcasted_iota(jnp.int32, shape, axis), lax.broadcasted_iota(jnp.int32, shape, 1 - axis)
        return jnp.where(many == few * CUT + b, 1.0, 0.0).astype(BF16)

    def send_y(ref, recv, i, n, ss, rs):
        for d, to in enumerate((up_y, down_y)):
            part = pl.ds(0, n * UNIT)
            remote(ref.at[d, i, part], recv.at[d, i, part], ss, rs.at[d, i], to).start()

    def partials(i, n):
        for a in range(n):
            arrived(xin.at[i, pl.ds(a * UROWS, UROWS)], x_rs.at[i, a])
        rows, whole = n * UNIT, n * UROWS
        xrows[:whole] = xin[i, :whole, :width]
        for b in range(CUT):
            tail = jnp.dot(picks(n, b, 0), xin[i, :whole, width:], preferred_element_type=F32)
            xrows[whole:rows, b * block : (b + 1) * block] = tail.astype(BF16)

        def part(r):
            return jnp.dot(xrows[:rows], wgu[:, 2 * r * fq : 2 * (r + 1) * fq], preferred_element_type=F32)

        far = part(2)
        hop_s[0, i, :rows] = far[:, :fq].astype(BF16)
        hop_s[1, i, :rows] = far[:, fq:].astype(BF16)
        send_y(hop_s, hop_r, i, n, hop_ss, hop_rs)
        above = part(1)
        qf[0, :rows] = above[:, :fq]
        qs[0, i, :rows, fq:] = above[:, fq:].astype(BF16)
        below = part(3)
        qs[1, i, :rows, :fq] = below[:, :fq].astype(BF16)
        qf[1, :rows] = below[:, fq:]
        own[lax.rem(i, 2), :rows] = part(0)

    def middle(i, n):
        rows = n * UNIT
        for d, to in enumerate((up_y, down_y)):
            arrived(hop_r.at[d, i, pl.ds(0, rows)], hop_rs.at[d, i])
            total = qf[d, :rows] + hop_r[d, i, :rows].astype(F32)
            qs[d, i, :rows, d * fq : (d + 1) * fq] = total.astype(BF16)
            part = pl.ds(0, rows)
            remote(qs.at[d, i, part], qr.at[d, i, part], q_ss, q_rs.at[d, i], to).start()

    def quarter(i, n, r):
        return hid.at[i, pl.ds(0, n * UNIT), pl.ds(r * fq, fq)]

    def half(i, n, r, h):
        first = -(-n * UNIT // 32) * 16
        at = pl.ds(0, first) if h == 0 else pl.ds(first, n * UNIT - first)
        return hid.at[i, at, pl.ds(r * fq, fq)]

    def activate(i, n):
        rows = n * UNIT
        for d in range(2):
            arrived(qr.at[d, i, pl.ds(0, rows)], q_rs.at[d, i])
        total = own[lax.rem(i, 2), :rows] + qr[0, i, :rows].astype(F32) + qr[1, i, :rows].astype(F32)
        gate, up = total[:, :fq], total[:, fq:]
        hid[i, :rows, :fq] = (gate / (1.0 + jnp.exp(-gate)) * up).astype(BF16)
        remote(quarter(i, n, 0), quarter(i, n, 3), ag_ss, ag_rs.at[0, i], up_y).start()
        remote(quarter(i, n, 0), quarter(i, n, 1), ag_ss, ag_rs.at[1, i], down_y).start()

    def forward(i, n):
        arrived(quarter(i, n, 3), ag_rs.at[0, i])
        remote(half(i, n, 3, 0), half(i, n, 2, 0), fw_ss, fw_rs.at[0, i], up_y).start()
        arrived(quarter(i, n, 1), ag_rs.at[1, i])
        remote(half(i, n, 1, 1), half(i, n, 2, 1), fw_ss, fw_rs.at[1, i], down_y).start()

    def send_back(k):
        todo = sorted((dx != 2, a, p, dx, dc) for a, (p, dx) in enumerate(ORDER[k]) for dc in range(NC))
        for _, a, p, dx, dc in todo:
            d = (NX - dx) % NX
            src = eout.at[k, pl.ds(a * UROWS + dc * MAIN, MAIN)]
            dst = back.at[p, pl.ds((d * NC + dc) * MAIN, MAIN)]
            if dx == 0 and dc == 0:
                pltpu.make_async_copy(src, dst, b_rs.at[p, d]).start()
            elif (dx, dc) == FAR and p in RELAYED:
                remote(src, back_by.at[p], b_ss, home_rs.at[p], mate[3, 0]).start()
            else:
                remote(src, dst, b_ss, b_rs.at[p, d], mate[dx, dc]).start()

    def down(i, n):
        arrived(half(i, n, 2, 0), fw_rs.at[0, i])
        arrived(half(i, n, 2, 1), fw_rs.at[1, i])
        rows, whole = n * UNIT, n * UROWS
        erow[:rows] = jnp.dot(hid[i, :rows], wdn[...], preferred_element_type=F32).astype(BF16)
        eout[i, :whole, :width] = erow[:whole]
        tail = jnp.zeros((whole, block), F32)
        for b in range(CUT):
            last = erow[whole:rows, b * block : (b + 1) * block]
            tail += jnp.dot(picks(n, b, 1), last, preferred_element_type=F32)
        eout[i, :whole, width:] = tail.astype(BF16)
        for k in range(CHUNKS):
            if len(ORDER[k]) == n:
                pl.when(i == k)(lambda k=k: send_back(k))

    def combine(p):
        for d in range(NX):
            arrived(back.at[p, pl.ds(d * UROWS, UROWS)], b_rs.at[p, d])
        span = 2 * PLANE * MAIN
        last = back[p, :, width:]
        for b in range(CUT):
            cols = slice(b * block, (b + 1) * block)
            first = back[p, :, cols]
            weights = jnp.concatenate(
                [shares_all[p, :, :span], shares_all[p, :, (b + 1) * span : (b + 2) * span]], axis=1
            )
            rows = jnp.concatenate([first, first, last, last], axis=0)
            zp[p, :, cols] = jnp.dot(weights, rows, preferred_element_type=F32)

    def leave(p):
        out, base, to = (LEFT_OUT, 0, down_z) if p in LEFT_OUT else (RIGHT_OUT, len(LEFT_OUT), up_z)
        h = base + out.index(p)
        total = zp[p]
        if h > base:
            arrived(zr.at[h - 1], z_rs.at[h - 1])
            total = total + zr[h - 1].astype(F32)
        zs[h] = total.astype(BF16)
        remote(zs.at[h], zr.at[h], z_ss, z_rs.at[h], to).start()

    ops = {PLANE_IN: z_arrived, COMBINE: combine, LEAVE: leave, SHARE: share, RELAY_OUT: relay_out, RELAY_BACK: relay_back}

    def one_of(s, steps):
        hit = s == steps[0]
        for t in steps[1:]:
            hit = jnp.logical_or(hit, s == t)
        return hit

    def perform(todo):
        for op, p in todo:
            ops[op](p)

    for load in inputs:
        load.wait()
    meta_all[0, 0:TOPK, :] = rt_own[...].astype(F32)
    prepare(0)
    select(0)
    pl.semaphore_wait(barrier, len(partners))
    z_send(0)
    dispatch(0)
    perform(FIRST)
    for load in loads:
        load.wait()

    def step(s, carry):
        for run, lag, steps, table in (
            (partials, 0, ALL_STEPS, AFTER_P),
            (activate, 1, EARLY_A, AFTER_EARLY_A),
            (middle, 0, EARLY_M, AFTER_EARLY_M),
            (forward, 1, EARLY_F, AFTER_EARLY_F),
            (down, 2, ALL_STEPS, AFTER_D),
            (activate, 1, LATE_A, AFTER_A),
            (middle, 0, LATE_M, AFTER_M),
            (forward, 1, LATE_F, AFTER_F),
        ):
            i = s - lag
            for n in (LARGE, SMALL):
                at = [t for t in steps if 0 <= t - lag < CHUNKS and len(ORDER[t - lag]) == n]
                if at:
                    pl.when(one_of(s, at))(lambda run=run, i=i, n=n: run(i, n))
            for at, todo in table.items():
                pl.when(s == at)(lambda todo=todo: perform(todo))
        return carry

    lax.fori_loop(0, CHUNKS + 2, step, 0)
    perform(LAST)
    last_left, last_right = len(LEFT_OUT) - 1, len(LEFT_OUT) + len(RIGHT_OUT) - 1
    arrived(zr.at[last_right], z_rs.at[last_right])
    arrived(zr.at[last_left], z_rs.at[last_left])
    out_ref[...] = (zp[0] + zr[last_left].astype(F32) + zr[last_right].astype(F32)).astype(BF16)

    sent(meta_all.at[pl.ds(1, NZ - 1)], zm_ss)
    sent(tok_all.at[pl.ds(1, NZ - 1)], zt_ss)
    sent(sel.at[:, pl.ds(MAIN, (PLANE - 1) * MAIN)], x_ss)
    sent(hop_s.at[:, pl.ds(0, NZ)], hop_ss)
    sent(qs.at[:, pl.ds(0, NZ)], q_ss)
    sent(hop_s.at[:, pl.ds(0, NZ)], ag_ss)
    sent(hop_s.at[0, pl.ds(0, NZ)], fw_ss)
    sent(sel.at[:, pl.ds(MAIN, (PLANE - 1) * MAIN)], b_ss)
    sent(zs, z_ss)
    sent(out_by, out_ss)
    sent(back_by.at[pl.ds(0, len(RELAYED))], home_ss)


def shards(tokens, routes, combine_weight, gate_weight, up_weight, down_weight):
    tok, width = tokens.shape
    ff = gate_weight.shape[2]
    fq = ff // NY
    n = CHUNKS
    wide = width + width // CUT
    vm = pltpu.VMEM
    dma = pltpu.SemaphoreType.DMA
    any_space = pl.BlockSpec(memory_space=pl.ANY)
    return pl.pallas_call(
        body,
        out_shape=vm((tok, width), BF16),
        in_specs=[any_space] * 6,
        out_specs=pl.BlockSpec(memory_space=vm),
        scratch_shapes=[
            vm((TOPK, tok), jnp.int32),
            vm((NZ, tok, width), BF16),
            vm((NZ, 2 * TOPK, tok), F32),
            vm((NZ, PLANE, tok), F32),
            vm((NZ, PLANE, tok), F32),
            vm((NZ, tok, 2 * (1 + CUT) * PLANE * MAIN), BF16),
            vm((width, 2 * ff), BF16),
            vm((ff, width), BF16),
            vm((NZ, PLANE * MAIN, wide), BF16),
            vm((n, LARGE * UROWS, wide), BF16),
            vm((ROWS, width), BF16),
            vm((2, n, ROWS, fq), BF16),
            vm((2, n, ROWS, fq), BF16),
            vm((2, ROWS, fq), F32),
            vm((2, n, ROWS, 2 * fq), BF16),
            vm((2, n, ROWS, 2 * fq), BF16),
            vm((2, ROWS, 2 * fq), F32),
            vm((n, ROWS, ff), BF16),
            vm((ROWS, width), BF16),
            vm((n, LARGE * UROWS, wide), BF16),
            vm((NZ, PLANE * MAIN, wide), BF16),
            vm((NZ, tok, width), F32),
            vm((NZ - 1, tok, width), BF16),
            vm((NZ - 1, tok, width), BF16),
            vm((NZ, MAIN, wide), BF16),
            vm((NZ, MAIN, wide), BF16),
            dma((3,)),
            dma((3 * NY,)),
            dma,
            dma((NZ - 1,)),
            dma,
            dma((NZ - 1,)),
            dma,
            dma((n, LARGE)),
            dma,
            dma((2, n)),
            dma,
            dma((2, n)),
            dma,
            dma((2, n)),
            dma,
            dma((2, n)),
            dma,
            dma((NZ, NX)),
            dma,
            dma((NZ - 1,)),
            dma,
            dma((NZ,)),
            dma,
            dma((NZ,)),
        ],
        compiler_params=pltpu.CompilerParams(
            collective_id=0, has_side_effects=True, vmem_limit_bytes=60 * 1024 * 1024
        ),
        cost_estimate=pl.CostEstimate(flops=13 * 10**9, bytes_accessed=10 * 10**6, transcendentals=0),
    )(routes.T, combine_weight.T, tokens, gate_weight[0], up_weight[0], down_weight[0])


def solution(mesh):
    return jax.shard_map(
        shards,
        mesh=mesh,
        in_specs=(
            P("ep", "kv"),
            P("ep", None),
            P("ep", None),
            P("ep", "kv", None),
            P("ep", "kv", None),
            P("ep", None, "kv"),
        ),
        out_specs=P("ep", "kv"),
        check_vma=False,
    )
```

```python
import jax
import jax.numpy as jnp
from jax import lax
from jax.experimental import pallas as pl
from jax.experimental.pallas import tpu as pltpu
from jax.sharding import PartitionSpec as P

MESH = pl.DeviceIdType.MESH
F32, BF16 = jnp.float32, jnp.bfloat16
NZ, NX, NC, NY = 8, 4, 2, 4
PLANE = NX * NC
TOPK = 8

OFFSETS = (0, -1, 1, -2, 2, -3, 3, -4)
NEXT_HOP = {0: (1, 2), 1: (3,), 2: (4,), 3: (5,), 4: (6,), 5: (7,), 6: (), 7: ()}
LEFT_OUT = (7, 5, 3, 1)
RIGHT_OUT = (6, 4, 2)

MAIN, TAIL, CUT = 16, 4, 4

ORDER = tuple(
    tuple(divmod(unit, 10) for unit in chunk)
    for chunk in (
        (0, 3),
        (1, 10),
        (13, 11, 21, 12),
        (41, 60, 50, 51),
        (70, 63, 71, 61),
        (62, 53, 72, 73),
        (52, 31, 42, 43),
        (32, 40, 30, 33),
        (23, 22),
        (2, 20),
    )
)
CHUNKS, SMALL, LARGE = len(ORDER), 2, 4
POS = {unit: (k, a) for k, units in enumerate(ORDER) for a, unit in enumerate(units)}
UROWS = NC * MAIN
UNIT = NC * (MAIN + TAIL)
ROWS = LARGE * UNIT

PLANE_IN, COMBINE, LEAVE, SHARE = 0, 1, 2, 3
FIRST = ()
ALL_STEPS = tuple(range(CHUNKS + 2))
EARLY_A = (1, 2, 3, 4, 5, 6, 7, 8, 9, 10)
EARLY_M = (0, 1, 2, 3, 5, 8, 9)
EARLY_F = (1,)
LATE_A = ()
LATE_M = (4, 6, 7)
LATE_F = (2, 3, 4, 5, 6, 7, 8, 9, 10)
AFTER_P = {0: ((PLANE_IN, 1),), 6: ((SHARE, 3),), 7: ((SHARE, 7),), 8: ((COMBINE, 6),)}
AFTER_EARLY_A = {2: ((PLANE_IN, 5),), 3: ((SHARE, 2), (PLANE_IN, 7)), 8: ((COMBINE, 7), (LEAVE, 6), (LEAVE, 7)), 9: ((COMBINE, 5), (LEAVE, 5)), 10: ((LEAVE, 4),)}
AFTER_EARLY_M = {0: ((PLANE_IN, 2),), 1: ((PLANE_IN, 3), (PLANE_IN, 4)), 2: ((PLANE_IN, 6),), 5: ((SHARE, 1),)}
AFTER_EARLY_F = {}
AFTER_D = {10: ((COMBINE, 3), (LEAVE, 3))}
AFTER_A = {}
AFTER_M = {4: ((SHARE, 5),), 7: ((SHARE, 4), (SHARE, 6), (SHARE, 0))}
AFTER_F = {6: ((COMBINE, 1),), 9: ((COMBINE, 4),)}
LAST = ((COMBINE, 2), (LEAVE, 2), (LEAVE, 1), (COMBINE, 0))

def body(
    rt_ref, wt_ref, tok_ref, wg_ref, wu_ref, wd_ref, out_ref,
    rt_own, tok_all, meta_all, vv, ww, shares_all, wgu, wdn, sel, xin, xrows, hop_s, hop_r, qf, qs, qr, own, hid, erow, eout, back,
    zp, zs, zr,
    in_sem, w_sem, zt_ss, zt_rs, zm_ss, zm_rs, x_ss, x_rs, hop_ss, hop_rs, q_ss, q_rs, ag_ss, ag_rs,
    fw_ss, fw_rs, b_ss, b_rs, z_ss, z_rs,
):
    tok, width = tok_ref.shape
    ff = wg_ref.shape[1]
    fq = ff // NY
    block = width // CUT
    ep, y = lax.axis_index("ep"), lax.axis_index("kv")
    z, x, c = ep // PLANE, lax.rem(ep // NC, NX), lax.rem(ep, NC)

    def dev(dz=0, dx=0, dc=0, dy=0):
        zz, xx, cc = lax.rem(z + dz + NZ, NZ), lax.rem(x + dx, NX), lax.rem(c + dc, NC)
        return {"ep": (zz * NX + xx) * NC + cc, "kv": lax.rem(y + dy + NY, NY)}

    def remote(src, dst, ss, rs, to):
        return pltpu.make_async_remote_copy(
            src_ref=src, dst_ref=dst, send_sem=ss, recv_sem=rs, device_id=to, device_id_type=MESH
        )

    up_y, down_y = dev(dy=1), dev(dy=-1)
    up_z, down_z = dev(dz=1), dev(dz=-1)
    plane = [(dx, dc) for dx in range(NX) for dc in range(NC)]
    mate = {at: dev(dx=at[0], dc=at[1]) for at in plane}

    def arrived(dst, rs):
        remote(dst, dst, rs, rs, up_y).wait_recv()

    def sent(src, ss):
        remote(src, src, ss, ss, up_y).wait_send()

    barrier = pltpu.get_barrier_semaphore()
    partners = [up_y, down_y, up_z, down_z] + [mate[at] for at in plane[1:]]
    for partner in partners:
        pl.semaphore_signal(barrier, inc=1, device_id=partner, device_id_type=MESH)

    inputs = [
        pltpu.make_async_copy(rt_ref, rt_own, in_sem.at[0]),
        pltpu.make_async_copy(wt_ref, meta_all.at[0, pl.ds(TOPK, TOPK)], in_sem.at[1]),
        pltpu.make_async_copy(tok_ref, tok_all.at[0], in_sem.at[2]),
    ]
    for load in inputs:
        load.start()

    loads = []
    for r in range(NY):
        cols = pl.ds(pl.multiple_of(lax.rem(y + r, NY) * fq, 128), fq)
        loads += [
            pltpu.make_async_copy(wg_ref.at[:, cols], wgu.at[:, pl.ds(2 * r * fq, fq)], w_sem.at[3 * r]),
            pltpu.make_async_copy(wu_ref.at[:, cols], wgu.at[:, pl.ds((2 * r + 1) * fq, fq)], w_sem.at[3 * r + 1]),
            pltpu.make_async_copy(wd_ref.at[cols], wdn.at[pl.ds(r * fq, fq)], w_sem.at[3 * r + 2]),
        ]
    for load in loads:
        load.start()

    place = lax.rem(lax.broadcasted_iota(jnp.int32, (PLANE * MAIN, tok), 0), MAIN)
    main_slot = place.astype(F32)
    tail_slot = [
        jnp.where(lax.rem(place, CUT) == b, MAIN + place // CUT, -1).astype(F32) for b in range(CUT)
    ]

    def spread(rows):
        return jnp.concatenate([jnp.broadcast_to(rows[j : j + 1, :], (MAIN, tok)) for j in range(PLANE)], axis=0)

    def prepare(p):
        rt, wt = meta_all[p, 0:TOPK, :], meta_all[p, TOPK : 2 * TOPK, :]
        j = lax.broadcasted_iota(jnp.int32, (PLANE, tok), 0)
        expert = (z * NX + lax.rem(x + j // NC, NX)) * NC + lax.rem(c + lax.rem(j, NC), NC)
        expert = expert.astype(F32)
        hit = jnp.zeros((PLANE, tok), F32)
        share = jnp.zeros((PLANE, tok), F32)
        for k in range(TOPK):
            same = rt[k : k + 1, :] == expert
            hit += jnp.where(same, 1.0, 0.0)
            share += jnp.where(same, wt[k : k + 1, :], 0.0)
        earlier = lax.broadcasted_iota(jnp.int32, (tok, tok), 0) < lax.broadcasted_iota(jnp.int32, (tok, tok), 1)
        rank = jnp.dot(hit.astype(BF16), jnp.where(earlier, 1.0, 0.0).astype(BF16), preferred_element_type=F32)
        vv[p] = jnp.where(hit > 0.5, rank, -64.0)
        ww[p] = share

    def select(p):
        slot = spread(vv[p])
        tail = jnp.zeros((PLANE * MAIN, block), F32)
        first = jnp.where(slot == main_slot, 1.0, 0.0).astype(BF16)
        for b in range(CUT):
            cols = slice(b * block, (b + 1) * block)
            last = jnp.where(slot == tail_slot[b], 1.0, 0.0).astype(BF16)
            both = jnp.dot(jnp.concatenate([first, last], axis=0), tok_all[p, :, cols], preferred_element_type=F32)
            sel[p, :, cols] = both[: PLANE * MAIN].astype(BF16)
            tail += both[PLANE * MAIN :]
        sel[p, :, width:] = tail.astype(BF16)

    def share(p):
        expand = lax.broadcasted_iota(jnp.int32, (PLANE, PLANE * MAIN), 1) // MAIN
        expand = jnp.where(expand == lax.broadcasted_iota(jnp.int32, (PLANE, PLANE * MAIN), 0), 1.0, 0.0)

        def by_token(rows):
            return lax.dot_general(rows, expand, (((0,), (0,)), ((), ())), preferred_element_type=F32)

        weight = ww[p]
        high = weight.astype(BF16).astype(F32)
        slot, high, low = by_token(vv[p]), by_token(high), by_token(weight - high)
        lane = lax.rem(lax.broadcasted_iota(jnp.int32, (tok, PLANE * MAIN), 1), MAIN)
        wants = [lane] + [jnp.where(lax.rem(lane, CUT) == b, MAIN + lane // CUT, -1) for b in range(CUT)]
        for n, want in enumerate(wants):
            same = slot == want.astype(F32)
            both = jnp.concatenate([jnp.where(same, high, 0.0), jnp.where(same, low, 0.0)], axis=1)
            shares_all[p, :, 2 * n * PLANE * MAIN : 2 * (n + 1) * PLANE * MAIN] = both.astype(BF16)

    def dispatch(p):
        todo = []
        for dx, dc in plane:
            k, a = POS[p, (NX - dx) % NX]
            todo.append((k, dx != 2, dx, dc, a))
        for k, _, dx, dc, a in sorted(todo):
            src = sel.at[p, pl.ds((dx * NC + dc) * MAIN, MAIN)]
            dst = xin.at[k, pl.ds(a * UROWS + dc * MAIN, MAIN)]
            if dx == 0 and dc == 0:
                pltpu.make_async_copy(src, dst, x_rs.at[k, a]).start()
            else:
                remote(src, dst, x_ss, x_rs.at[k, a], mate[dx, dc]).start()

    def z_send(p):
        for q in NEXT_HOP[p]:
            to = up_z if OFFSETS[q] < 0 else down_z
            remote(meta_all.at[p], meta_all.at[q], zm_ss, zm_rs.at[q - 1], to).start()
            remote(tok_all.at[p], tok_all.at[q], zt_ss, zt_rs.at[q - 1], to).start()

    def z_arrived(p):
        arrived(meta_all.at[p], zm_rs.at[p - 1])
        arrived(tok_all.at[p], zt_rs.at[p - 1])
        z_send(p)
        prepare(p)
        select(p)
        dispatch(p)

    def picks(n, b, axis):
        shape = (n * UROWS // CUT, n * UROWS) if axis == 0 else (n * UROWS, n * UROWS // CUT)
        few, many = lax.broadcasted_iota(jnp.int32, shape, axis), lax.broadcasted_iota(jnp.int32, shape, 1 - axis)
        return jnp.where(many == few * CUT + b, 1.0, 0.0).astype(BF16)

    def parts(n):
        first = -(-n * UNIT // 32) * 16
        return [(0, first), (first, n * UNIT)]

    def partials(i, n):
        for a in range(n):
            arrived(xin.at[i, pl.ds(a * UROWS, UROWS)], x_rs.at[i, a])
        rows, whole = n * UNIT, n * UROWS
        xrows[:whole] = xin[i, :whole, :width]
        for b in range(CUT):
            tail = jnp.dot(picks(n, b, 0), xin[i, :whole, width:], preferred_element_type=F32)
            xrows[whole:rows, b * block : (b + 1) * block] = tail.astype(BF16)

        def part(r):
            return jnp.dot(xrows[:rows], wgu[:, 2 * r * fq : 2 * (r + 1) * fq], preferred_element_type=F32)

        far = part(2)
        hop_s[0, i, :rows] = far[:, :fq].astype(BF16)
        hop_s[1, i, :rows] = far[:, fq:].astype(BF16)
        for h, (low, high) in enumerate(parts(n)):
            at = pl.ds(low, high - low)
            for d, to in enumerate((up_y, down_y)):
                remote(hop_s.at[d, i, at], hop_r.at[d, i, at], hop_ss, hop_rs.at[d, i, h], to).start()
        above = part(1)
        qf[0, :rows] = above[:, :fq]
        qs[0, i, :rows, fq:] = above[:, fq:].astype(BF16)
        below = part(3)
        qs[1, i, :rows, :fq] = below[:, :fq].astype(BF16)
        qf[1, :rows] = below[:, fq:]
        own[lax.rem(i, 2), :rows] = part(0)

    def middle(i, n):
        for h, (low, high) in enumerate(parts(n)):
            at, rs = pl.ds(low, high - low), slice(low, high)
            for d, to in enumerate((up_y, down_y)):
                arrived(hop_r.at[d, i, at], hop_rs.at[d, i, h])
                total = qf[d, rs] + hop_r[d, i, rs].astype(F32)
                qs[d, i, rs, d * fq : (d + 1) * fq] = total.astype(BF16)
                remote(qs.at[d, i, at], qr.at[d, i, at], q_ss, q_rs.at[d, i, h], to).start()

    def half(i, n, r, h):
        low, high = parts(n)[h]
        return hid.at[i, pl.ds(low, high - low), pl.ds(r * fq, fq)]

    def activate(i, n):
        for h, (low, high) in enumerate(parts(n)):
            at, rs = pl.ds(low, high - low), slice(low, high)
            for d in range(2):
                arrived(qr.at[d, i, at], q_rs.at[d, i, h])
            total = own[lax.rem(i, 2), rs] + qr[0, i, rs].astype(F32) + qr[1, i, rs].astype(F32)
            gate, up = total[:, :fq], total[:, fq:]
            hid[i, rs, :fq] = (gate / (1.0 + jnp.exp(-gate)) * up).astype(BF16)
            remote(half(i, n, 0, h), half(i, n, 3, h), ag_ss, ag_rs.at[0, i, h], up_y).start()
            remote(half(i, n, 0, h), half(i, n, 1, h), ag_ss, ag_rs.at[1, i, h], down_y).start()

    def forward(i, n):
        arrived(half(i, n, 3, 0), ag_rs.at[0, i, 0])
        remote(half(i, n, 3, 0), half(i, n, 2, 0), fw_ss, fw_rs.at[0, i], up_y).start()
        arrived(half(i, n, 1, 1), ag_rs.at[1, i, 1])
        remote(half(i, n, 1, 1), half(i, n, 2, 1), fw_ss, fw_rs.at[1, i], down_y).start()

    def send_back(k):
        todo = sorted((dx != 2, a, p, dx, dc) for a, (p, dx) in enumerate(ORDER[k]) for dc in range(NC))
        for _, a, p, dx, dc in todo:
            d = (NX - dx) % NX
            src = eout.at[k, pl.ds(a * UROWS + dc * MAIN, MAIN)]
            dst = back.at[p, pl.ds((d * NC + dc) * MAIN, MAIN)]
            if dx == 0 and dc == 0:
                pltpu.make_async_copy(src, dst, b_rs.at[p, d]).start()
            else:
                remote(src, dst, b_ss, b_rs.at[p, d], mate[dx, dc]).start()

    def down(i, n):
        arrived(half(i, n, 3, 1), ag_rs.at[0, i, 1])
        arrived(half(i, n, 1, 0), ag_rs.at[1, i, 0])
        arrived(half(i, n, 2, 0), fw_rs.at[0, i])
        arrived(half(i, n, 2, 1), fw_rs.at[1, i])
        rows, whole = n * UNIT, n * UROWS
        erow[:rows] = jnp.dot(hid[i, :rows], wdn[...], preferred_element_type=F32).astype(BF16)
        eout[i, :whole, :width] = erow[:whole]
        tail = jnp.zeros((whole, block), F32)
        for b in range(CUT):
            last = erow[whole:rows, b * block : (b + 1) * block]
            tail += jnp.dot(picks(n, b, 1), last, preferred_element_type=F32)
        eout[i, :whole, width:] = tail.astype(BF16)
        for k in range(CHUNKS):
            if len(ORDER[k]) == n:
                pl.when(i == k)(lambda k=k: send_back(k))

    def combine(p):
        for d in range(NX):
            arrived(back.at[p, pl.ds(d * UROWS, UROWS)], b_rs.at[p, d])
        span = 2 * PLANE * MAIN
        last = back[p, :, width:]
        for b in range(CUT):
            cols = slice(b * block, (b + 1) * block)
            first = back[p, :, cols]
            weights = jnp.concatenate(
                [shares_all[p, :, :span], shares_all[p, :, (b + 1) * span : (b + 2) * span]], axis=1
            )
            rows = jnp.concatenate([first, first, last, last], axis=0)
            zp[p, :, cols] = jnp.dot(weights, rows, preferred_element_type=F32)

    def leave(p):
        out, base, to = (LEFT_OUT, 0, down_z) if p in LEFT_OUT else (RIGHT_OUT, len(LEFT_OUT), up_z)
        h = base + out.index(p)
        total = zp[p]
        if h > base:
            arrived(zr.at[h - 1], z_rs.at[h - 1])
            total = total + zr[h - 1].astype(F32)
        zs[h] = total.astype(BF16)
        remote(zs.at[h], zr.at[h], z_ss, z_rs.at[h], to).start()

    ops = {PLANE_IN: z_arrived, COMBINE: combine, LEAVE: leave, SHARE: share}

    def one_of(s, steps):
        hit = s == steps[0]
        for t in steps[1:]:
            hit = jnp.logical_or(hit, s == t)
        return hit

    def perform(todo):
        for op, p in todo:
            ops[op](p)

    for load in inputs:
        load.wait()
    meta_all[0, 0:TOPK, :] = rt_own[...].astype(F32)
    prepare(0)
    select(0)
    pl.semaphore_wait(barrier, len(partners))
    z_send(0)
    dispatch(0)
    perform(FIRST)
    for load in loads:
        load.wait()

    def step(s, carry):
        for run, lag, steps, table in (
            (partials, 0, ALL_STEPS, AFTER_P),
            (activate, 1, EARLY_A, AFTER_EARLY_A),
            (middle, 0, EARLY_M, AFTER_EARLY_M),
            (forward, 1, EARLY_F, AFTER_EARLY_F),
            (down, 2, ALL_STEPS, AFTER_D),
            (activate, 1, LATE_A, AFTER_A),
            (middle, 0, LATE_M, AFTER_M),
            (forward, 1, LATE_F, AFTER_F),
        ):
            i = s - lag
            for n in (LARGE, SMALL):
                at = [t for t in steps if 0 <= t - lag < CHUNKS and len(ORDER[t - lag]) == n]
                if at:
                    pl.when(one_of(s, at))(lambda run=run, i=i, n=n: run(i, n))
            for at, todo in table.items():
                pl.when(s == at)(lambda todo=todo: perform(todo))
        return carry

    lax.fori_loop(0, CHUNKS + 2, step, 0)
    perform(LAST)
    last_left, last_right = len(LEFT_OUT) - 1, len(LEFT_OUT) + len(RIGHT_OUT) - 1
    arrived(zr.at[last_right], z_rs.at[last_right])
    arrived(zr.at[last_left], z_rs.at[last_left])
    out_ref[...] = (zp[0] + zr[last_left].astype(F32) + zr[last_right].astype(F32)).astype(BF16)

    sent(meta_all.at[pl.ds(1, NZ - 1)], zm_ss)
    sent(tok_all.at[pl.ds(1, NZ - 1)], zt_ss)
    sent(sel.at[:, pl.ds(MAIN, (PLANE - 1) * MAIN)], x_ss)
    sent(hop_s.at[:, pl.ds(0, NZ)], hop_ss)
    sent(qs.at[:, pl.ds(0, NZ)], q_ss)
    sent(hop_s.at[:, pl.ds(0, NZ)], ag_ss)
    sent(hop_s.at[0, pl.ds(0, NZ)], fw_ss)
    sent(sel.at[:, pl.ds(MAIN, (PLANE - 1) * MAIN)], b_ss)
    sent(zs, z_ss)


def shards(tokens, routes, combine_weight, gate_weight, up_weight, down_weight):
    tok, width = tokens.shape
    ff = gate_weight.shape[2]
    fq = ff // NY
    n = CHUNKS
    wide = width + width // CUT
    vm = pltpu.VMEM
    dma = pltpu.SemaphoreType.DMA
    any_space = pl.BlockSpec(memory_space=pl.ANY)
    return pl.pallas_call(
        body,
        out_shape=vm((tok, width), BF16),
        in_specs=[any_space] * 6,
        out_specs=pl.BlockSpec(memory_space=vm),
        scratch_shapes=[
            vm((TOPK, tok), jnp.int32),
            vm((NZ, tok, width), BF16),
            vm((NZ, 2 * TOPK, tok), F32),
            vm((NZ, PLANE, tok), F32),
            vm((NZ, PLANE, tok), F32),
            vm((NZ, tok, 2 * (1 + CUT) * PLANE * MAIN), BF16),
            vm((width, 2 * ff), BF16),
            vm((ff, width), BF16),
            vm((NZ, PLANE * MAIN, wide), BF16),
            vm((n, LARGE * UROWS, wide), BF16),
            vm((ROWS, width), BF16),
            vm((2, n, ROWS, fq), BF16),
            vm((2, n, ROWS, fq), BF16),
            vm((2, ROWS, fq), F32),
            vm((2, n, ROWS, 2 * fq), BF16),
            vm((2, n, ROWS, 2 * fq), BF16),
            vm((2, ROWS, 2 * fq), F32),
            vm((n, ROWS, ff), BF16),
            vm((ROWS, width), BF16),
            vm((n, LARGE * UROWS, wide), BF16),
            vm((NZ, PLANE * MAIN, wide), BF16),
            vm((NZ, tok, width), F32),
            vm((NZ - 1, tok, width), BF16),
            vm((NZ - 1, tok, width), BF16),
            dma((3,)),
            dma((3 * NY,)),
            dma,
            dma((NZ - 1,)),
            dma,
            dma((NZ - 1,)),
            dma,
            dma((n, LARGE)),
            dma,
            dma((2, n, 2)),
            dma,
            dma((2, n, 2)),
            dma,
            dma((2, n, 2)),
            dma,
            dma((2, n)),
            dma,
            dma((NZ, NX)),
            dma,
            dma((NZ - 1,)),
        ],
        compiler_params=pltpu.CompilerParams(
            collective_id=0, has_side_effects=True, vmem_limit_bytes=60 * 1024 * 1024
        ),
        cost_estimate=pl.CostEstimate(flops=13 * 10**9, bytes_accessed=10 * 10**6, transcendentals=0),
    )(routes.T, combine_weight.T, tokens, gate_weight[0], up_weight[0], down_weight[0])


def solution(mesh):
    return jax.shard_map(
        shards,
        mesh=mesh,
        in_specs=(
            P("ep", "kv"),
            P("ep", None),
            P("ep", None),
            P("ep", "kv", None),
            P("ep", "kv", None),
            P("ep", None, "kv"),
        ),
        out_specs=P("ep", "kv"),
        check_vma=False,
    )
```

```python
import jax
import jax.numpy as jnp
from jax import lax
from jax.experimental import pallas as pl
from jax.experimental.pallas import tpu as pltpu
from jax.sharding import PartitionSpec as P

MESH = pl.DeviceIdType.MESH
F32, BF16 = jnp.float32, jnp.bfloat16
NZ, NX, NC, NY = 8, 4, 2, 4
PLANE = NX * NC
TOPK = 8

OFFSETS = (0, -1, 1, -2, 2, -3, 3, -4)
NEXT_HOP = {0: (1, 2), 1: (3,), 2: (4,), 3: (5,), 4: (6,), 5: (7,), 6: (), 7: ()}
LEFT_OUT = (7, 5, 3, 1)
RIGHT_OUT = (6, 4, 2)

MAIN, TAIL, CUT = 16, 4, 4

ORDER = tuple(
    tuple(divmod(unit, 10) for unit in chunk)
    for chunk in (
        (1, 0),
        (2, 20),
        (23, 11, 21, 12),
        (22, 31, 60, 41),
        (70, 42, 62, 61),
        (72, 63, 71, 73),
        (51, 53, 43, 52),
        (32, 40, 50, 33),
        (13, 30),
        (10, 3),
    )
)
CHUNKS, SMALL, LARGE = len(ORDER), 2, 4
POS = {unit: (k, a) for k, units in enumerate(ORDER) for a, unit in enumerate(units)}
UROWS = NC * MAIN
UNIT = NC * (MAIN + TAIL)
ROWS = LARGE * UNIT

PLANE_IN, COMBINE, LEAVE, SHARE = 0, 1, 2, 3
FIRST = ()
ALL_STEPS = tuple(range(CHUNKS + 2))
EARLY_A = (1, 2, 3, 4, 5, 6, 7, 8, 9, 10)
EARLY_M = (0, 1, 2, 3, 4, 5, 6, 8, 9)
EARLY_F = (1, 3, 4, 5, 6)
LATE_A = ()
LATE_M = (7,)
LATE_F = (2, 7, 8, 9, 10)
AFTER_P = {0: ((PLANE_IN, 1),), 2: ((SHARE, 3),)}
AFTER_EARLY_A = {1: ((SHARE, 1), (SHARE, 2)), 5: ((SHARE, 6),), 8: ((COMBINE, 6), (LEAVE, 6), (COMBINE, 7), (LEAVE, 7)), 10: ((COMBINE, 4), (LEAVE, 4))}
AFTER_EARLY_M = {0: ((PLANE_IN, 2),), 1: ((PLANE_IN, 3),), 2: ((PLANE_IN, 5), (PLANE_IN, 6)), 3: ((PLANE_IN, 7),), 4: ((SHARE, 7), (SHARE, 5))}
AFTER_EARLY_F = {1: ((PLANE_IN, 4),)}
AFTER_D = {}
AFTER_A = {}
AFTER_M = {}
AFTER_F = {7: ((SHARE, 0),), 9: ((COMBINE, 5), (LEAVE, 5), (SHARE, 4)), 10: ((COMBINE, 3), (LEAVE, 3))}
LAST = ((COMBINE, 2), (LEAVE, 2), (COMBINE, 1), (LEAVE, 1), (COMBINE, 0))

def body(
    rt_ref, wt_ref, tok_ref, wg_ref, wu_ref, wd_ref, out_ref,
    rt_own, tok_all, meta_all, vv, ww, shares_all, wgu, wdn, sel, xin, xrows, hop_s, hop_r, qf, qs, qr, own, hid, erow, eout, back,
    zp, zs, zr,
    in_sem, w_sem, zt_ss, zt_rs, zm_ss, zm_rs, x_ss, x_rs, hop_ss, hop_rs, q_ss, q_rs, ag_ss, ag_rs,
    fw_ss, fw_rs, b_ss, b_rs, z_ss, z_rs,
):
    tok, width = tok_ref.shape
    ff = wg_ref.shape[1]
    fq = ff // NY
    block = width // CUT
    ep, y = lax.axis_index("ep"), lax.axis_index("kv")
    z, x, c = ep // PLANE, lax.rem(ep // NC, NX), lax.rem(ep, NC)

    def dev(dz=0, dx=0, dc=0, dy=0):
        zz, xx, cc = lax.rem(z + dz + NZ, NZ), lax.rem(x + dx, NX), lax.rem(c + dc, NC)
        return {"ep": (zz * NX + xx) * NC + cc, "kv": lax.rem(y + dy + NY, NY)}

    def remote(src, dst, ss, rs, to):
        return pltpu.make_async_remote_copy(
            src_ref=src, dst_ref=dst, send_sem=ss, recv_sem=rs, device_id=to, device_id_type=MESH
        )

    up_y, down_y = dev(dy=1), dev(dy=-1)
    up_z, down_z = dev(dz=1), dev(dz=-1)
    plane = [(dx, dc) for dx in range(NX) for dc in range(NC)]
    mate = {at: dev(dx=at[0], dc=at[1]) for at in plane}

    def arrived(dst, rs):
        remote(dst, dst, rs, rs, up_y).wait_recv()

    def sent(src, ss):
        remote(src, src, ss, ss, up_y).wait_send()

    barrier = pltpu.get_barrier_semaphore()
    partners = [up_y, down_y, up_z, down_z] + [mate[at] for at in plane[1:]]
    for partner in partners:
        pl.semaphore_signal(barrier, inc=1, device_id=partner, device_id_type=MESH)

    inputs = [
        pltpu.make_async_copy(rt_ref, rt_own, in_sem.at[0]),
        pltpu.make_async_copy(wt_ref, meta_all.at[0, pl.ds(TOPK, TOPK)], in_sem.at[1]),
        pltpu.make_async_copy(tok_ref, tok_all.at[0], in_sem.at[2]),
    ]
    for load in inputs:
        load.start()

    loads = []
    for r in range(NY):
        cols = pl.ds(pl.multiple_of(lax.rem(y + r, NY) * fq, 128), fq)
        loads += [
            pltpu.make_async_copy(wg_ref.at[:, cols], wgu.at[:, pl.ds(2 * r * fq, fq)], w_sem.at[3 * r]),
            pltpu.make_async_copy(wu_ref.at[:, cols], wgu.at[:, pl.ds((2 * r + 1) * fq, fq)], w_sem.at[3 * r + 1]),
            pltpu.make_async_copy(wd_ref.at[cols], wdn.at[pl.ds(r * fq, fq)], w_sem.at[3 * r + 2]),
        ]
    for load in loads:
        load.start()

    place = lax.rem(lax.broadcasted_iota(jnp.int32, (PLANE * MAIN, tok), 0), MAIN)
    main_slot = place.astype(F32)
    tail_slot = [
        jnp.where(lax.rem(place, CUT) == b, MAIN + place // CUT, -1).astype(F32) for b in range(CUT)
    ]

    def spread(rows):
        return jnp.concatenate([jnp.broadcast_to(rows[j : j + 1, :], (MAIN, tok)) for j in range(PLANE)], axis=0)

    def prepare(p):
        rt, wt = meta_all[p, 0:TOPK, :], meta_all[p, TOPK : 2 * TOPK, :]
        j = lax.broadcasted_iota(jnp.int32, (PLANE, tok), 0)
        expert = (z * NX + lax.rem(x + j // NC, NX)) * NC + lax.rem(c + lax.rem(j, NC), NC)
        expert = expert.astype(F32)
        hit = jnp.zeros((PLANE, tok), F32)
        share = jnp.zeros((PLANE, tok), F32)
        for k in range(TOPK):
            same = rt[k : k + 1, :] == expert
            hit += jnp.where(same, 1.0, 0.0)
            share += jnp.where(same, wt[k : k + 1, :], 0.0)
        earlier = lax.broadcasted_iota(jnp.int32, (tok, tok), 0) < lax.broadcasted_iota(jnp.int32, (tok, tok), 1)
        rank = jnp.dot(hit.astype(BF16), jnp.where(earlier, 1.0, 0.0).astype(BF16), preferred_element_type=F32)
        vv[p] = jnp.where(hit > 0.5, rank, -64.0)
        ww[p] = share

    def select(p):
        slot = spread(vv[p])
        tail = jnp.zeros((PLANE * MAIN, block), F32)
        first = jnp.where(slot == main_slot, 1.0, 0.0).astype(BF16)
        for b in range(CUT):
            cols = slice(b * block, (b + 1) * block)
            last = jnp.where(slot == tail_slot[b], 1.0, 0.0).astype(BF16)
            both = jnp.dot(jnp.concatenate([first, last], axis=0), tok_all[p, :, cols], preferred_element_type=F32)
            sel[p, :, cols] = both[: PLANE * MAIN].astype(BF16)
            tail += both[PLANE * MAIN :]
        sel[p, :, width:] = tail.astype(BF16)

    def share(p):
        expand = lax.broadcasted_iota(jnp.int32, (PLANE, PLANE * MAIN), 1) // MAIN
        expand = jnp.where(expand == lax.broadcasted_iota(jnp.int32, (PLANE, PLANE * MAIN), 0), 1.0, 0.0)

        def by_token(rows):
            return lax.dot_general(rows, expand, (((0,), (0,)), ((), ())), preferred_element_type=F32)

        weight = ww[p]
        high = weight.astype(BF16).astype(F32)
        slot, high, low = by_token(vv[p]), by_token(high), by_token(weight - high)
        lane = lax.rem(lax.broadcasted_iota(jnp.int32, (tok, PLANE * MAIN), 1), MAIN)
        wants = [lane] + [jnp.where(lax.rem(lane, CUT) == b, MAIN + lane // CUT, -1) for b in range(CUT)]
        for n, want in enumerate(wants):
            same = slot == want.astype(F32)
            both = jnp.concatenate([jnp.where(same, high, 0.0), jnp.where(same, low, 0.0)], axis=1)
            shares_all[p, :, 2 * n * PLANE * MAIN : 2 * (n + 1) * PLANE * MAIN] = both.astype(BF16)

    def dispatch(p):
        todo = []
        for dx, dc in plane:
            k, a = POS[p, (NX - dx) % NX]
            todo.append((k, dx != 2, dx, dc, a))
        for k, _, dx, dc, a in sorted(todo):
            src = sel.at[p, pl.ds((dx * NC + dc) * MAIN, MAIN)]
            dst = xin.at[k, pl.ds(a * UROWS + dc * MAIN, MAIN)]
            if dx == 0 and dc == 0:
                pltpu.make_async_copy(src, dst, x_rs.at[k, a]).start()
            else:
                remote(src, dst, x_ss, x_rs.at[k, a], mate[dx, dc]).start()

    def z_send(p):
        for q in NEXT_HOP[p]:
            to = up_z if OFFSETS[q] < 0 else down_z
            remote(meta_all.at[p], meta_all.at[q], zm_ss, zm_rs.at[q - 1], to).start()
            remote(tok_all.at[p], tok_all.at[q], zt_ss, zt_rs.at[q - 1], to).start()

    def z_arrived(p):
        arrived(meta_all.at[p], zm_rs.at[p - 1])
        arrived(tok_all.at[p], zt_rs.at[p - 1])
        z_send(p)
        prepare(p)
        select(p)
        dispatch(p)

    def picks(n, b, axis):
        shape = (n * UROWS // CUT, n * UROWS) if axis == 0 else (n * UROWS, n * UROWS // CUT)
        few, many = lax.broadcasted_iota(jnp.int32, shape, axis), lax.broadcasted_iota(jnp.int32, shape, 1 - axis)
        return jnp.where(many == few * CUT + b, 1.0, 0.0).astype(BF16)

    def parts(n):
        first = -(-n * UNIT // 32) * 16
        return [(0, first), (first, n * UNIT)]

    def partials(i, n):
        for a in range(n):
            arrived(xin.at[i, pl.ds(a * UROWS, UROWS)], x_rs.at[i, a])
        rows, whole = n * UNIT, n * UROWS
        xrows[:whole] = xin[i, :whole, :width]
        for b in range(CUT):
            tail = jnp.dot(picks(n, b, 0), xin[i, :whole, width:], preferred_element_type=F32)
            xrows[whole:rows, b * block : (b + 1) * block] = tail.astype(BF16)

        def part(r):
            return jnp.dot(xrows[:rows], wgu[:, 2 * r * fq : 2 * (r + 1) * fq], preferred_element_type=F32)

        far = part(2)
        hop_s[0, i, :rows] = far[:, :fq].astype(BF16)
        hop_s[1, i, :rows] = far[:, fq:].astype(BF16)
        for h, (low, high) in enumerate(parts(n)):
            at = pl.ds(low, high - low)
            for d, to in enumerate((up_y, down_y)):
                remote(hop_s.at[d, i, at], hop_r.at[d, i, at], hop_ss, hop_rs.at[d, i, h], to).start()
        above = part(1)
        qf[0, :rows] = above[:, :fq]
        qs[0, i, :rows, fq:] = above[:, fq:].astype(BF16)
        below = part(3)
        qs[1, i, :rows, :fq] = below[:, :fq].astype(BF16)
        qf[1, :rows] = below[:, fq:]
        own[lax.rem(i, 2), :rows] = part(0)

    def middle(i, n):
        for h, (low, high) in enumerate(parts(n)):
            at, rs = pl.ds(low, high - low), slice(low, high)
            for d, to in enumerate((up_y, down_y)):
                arrived(hop_r.at[d, i, at], hop_rs.at[d, i, h])
                total = qf[d, rs] + hop_r[d, i, rs].astype(F32)
                qs[d, i, rs, d * fq : (d + 1) * fq] = total.astype(BF16)
                remote(qs.at[d, i, at], qr.at[d, i, at], q_ss, q_rs.at[d, i, h], to).start()

    def half(i, n, r, h):
        low, high = parts(n)[h]
        return hid.at[i, pl.ds(low, high - low), pl.ds(r * fq, fq)]

    def activate(i, n):
        for h, (low, high) in enumerate(parts(n)):
            at, rs = pl.ds(low, high - low), slice(low, high)
            for d in range(2):
                arrived(qr.at[d, i, at], q_rs.at[d, i, h])
            total = own[lax.rem(i, 2), rs] + qr[0, i, rs].astype(F32) + qr[1, i, rs].astype(F32)
            gate, up = total[:, :fq], total[:, fq:]
            hid[i, rs, :fq] = (gate / (1.0 + jnp.exp(-gate)) * up).astype(BF16)
            remote(half(i, n, 0, h), half(i, n, 3, h), ag_ss, ag_rs.at[0, i, h], up_y).start()
            remote(half(i, n, 0, h), half(i, n, 1, h), ag_ss, ag_rs.at[1, i, h], down_y).start()

    def forward(i, n):
        arrived(half(i, n, 3, 0), ag_rs.at[0, i, 0])
        remote(half(i, n, 3, 0), half(i, n, 2, 0), fw_ss, fw_rs.at[0, i], up_y).start()
        arrived(half(i, n, 1, 1), ag_rs.at[1, i, 1])
        remote(half(i, n, 1, 1), half(i, n, 2, 1), fw_ss, fw_rs.at[1, i], down_y).start()

    def send_back(k):
        todo = sorted((dx != 2, a, p, dx, dc) for a, (p, dx) in enumerate(ORDER[k]) for dc in range(NC))
        for _, a, p, dx, dc in todo:
            d = (NX - dx) % NX
            src = eout.at[k, pl.ds(a * UROWS + dc * MAIN, MAIN)]
            dst = back.at[p, pl.ds((d * NC + dc) * MAIN, MAIN)]
            if dx == 0 and dc == 0:
                pltpu.make_async_copy(src, dst, b_rs.at[p, d]).start()
            else:
                remote(src, dst, b_ss, b_rs.at[p, d], mate[dx, dc]).start()

    def down(i, n):
        arrived(half(i, n, 3, 1), ag_rs.at[0, i, 1])
        arrived(half(i, n, 1, 0), ag_rs.at[1, i, 0])
        arrived(half(i, n, 2, 0), fw_rs.at[0, i])
        arrived(half(i, n, 2, 1), fw_rs.at[1, i])
        rows, whole = n * UNIT, n * UROWS
        erow[:rows] = jnp.dot(hid[i, :rows], wdn[...], preferred_element_type=F32).astype(BF16)
        eout[i, :whole, :width] = erow[:whole]
        tail = jnp.zeros((whole, block), F32)
        for b in range(CUT):
            last = erow[whole:rows, b * block : (b + 1) * block]
            tail += jnp.dot(picks(n, b, 1), last, preferred_element_type=F32)
        eout[i, :whole, width:] = tail.astype(BF16)
        for k in range(CHUNKS):
            if len(ORDER[k]) == n:
                pl.when(i == k)(lambda k=k: send_back(k))

    def combine(p):
        for d in range(NX):
            arrived(back.at[p, pl.ds(d * UROWS, UROWS)], b_rs.at[p, d])
        span = 2 * PLANE * MAIN
        last = back[p, :, width:]
        for b in range(CUT):
            cols = slice(b * block, (b + 1) * block)
            first = back[p, :, cols]
            weights = jnp.concatenate(
                [shares_all[p, :, :span], shares_all[p, :, (b + 1) * span : (b + 2) * span]], axis=1
            )
            rows = jnp.concatenate([first, first, last, last], axis=0)
            zp[p, :, cols] = jnp.dot(weights, rows, preferred_element_type=F32)

    z_parts = [pl.ds(0, tok // 2), pl.ds(tok // 2, tok // 2)]

    def leave(p):
        out, base, to = (LEFT_OUT, 0, down_z) if p in LEFT_OUT else (RIGHT_OUT, len(LEFT_OUT), up_z)
        h = base + out.index(p)
        for part, rows in enumerate(z_parts):
            at = slice(rows.start, rows.start + rows.size)
            total = zp[p, at]
            if h > base:
                arrived(zr.at[h - 1, rows], z_rs.at[h - 1, part])
                total = total + zr[h - 1, at].astype(F32)
            zs[h, at] = total.astype(BF16)
            remote(zs.at[h, rows], zr.at[h, rows], z_ss, z_rs.at[h, part], to).start()

    ops = {PLANE_IN: z_arrived, COMBINE: combine, LEAVE: leave, SHARE: share}

    def one_of(s, steps):
        hit = s == steps[0]
        for t in steps[1:]:
            hit = jnp.logical_or(hit, s == t)
        return hit

    def perform(todo):
        for op, p in todo:
            ops[op](p)

    for load in inputs:
        load.wait()
    meta_all[0, 0:TOPK, :] = rt_own[...].astype(F32)
    prepare(0)
    select(0)
    pl.semaphore_wait(barrier, len(partners))
    z_send(0)
    dispatch(0)
    perform(FIRST)
    for load in loads:
        load.wait()

    def step(s, carry):
        for run, lag, steps, table in (
            (partials, 0, ALL_STEPS, AFTER_P),
            (activate, 1, EARLY_A, AFTER_EARLY_A),
            (middle, 0, EARLY_M, AFTER_EARLY_M),
            (forward, 1, EARLY_F, AFTER_EARLY_F),
            (down, 2, ALL_STEPS, AFTER_D),
            (activate, 1, LATE_A, AFTER_A),
            (middle, 0, LATE_M, AFTER_M),
            (forward, 1, LATE_F, AFTER_F),
        ):
            i = s - lag
            for n in (LARGE, SMALL):
                at = [t for t in steps if 0 <= t - lag < CHUNKS and len(ORDER[t - lag]) == n]
                if at:
                    pl.when(one_of(s, at))(lambda run=run, i=i, n=n: run(i, n))
            for at, todo in table.items():
                pl.when(s == at)(lambda todo=todo: perform(todo))
        return carry

    lax.fori_loop(0, CHUNKS + 2, step, 0)
    perform(LAST)
    last_left, last_right = len(LEFT_OUT) - 1, len(LEFT_OUT) + len(RIGHT_OUT) - 1
    for part, rows in enumerate(z_parts):
        at = slice(rows.start, rows.start + rows.size)
        arrived(zr.at[last_right, rows], z_rs.at[last_right, part])
        arrived(zr.at[last_left, rows], z_rs.at[last_left, part])
        out_ref[at] = (zp[0, at] + zr[last_left, at].astype(F32) + zr[last_right, at].astype(F32)).astype(BF16)

    sent(meta_all.at[pl.ds(1, NZ - 1)], zm_ss)
    sent(tok_all.at[pl.ds(1, NZ - 1)], zt_ss)
    sent(sel.at[:, pl.ds(MAIN, (PLANE - 1) * MAIN)], x_ss)
    sent(hop_s.at[:, pl.ds(0, NZ)], hop_ss)
    sent(qs.at[:, pl.ds(0, NZ)], q_ss)
    sent(hop_s.at[:, pl.ds(0, NZ)], ag_ss)
    sent(hop_s.at[0, pl.ds(0, NZ)], fw_ss)
    sent(sel.at[:, pl.ds(MAIN, (PLANE - 1) * MAIN)], b_ss)
    sent(zs, z_ss)


def shards(tokens, routes, combine_weight, gate_weight, up_weight, down_weight):
    tok, width = tokens.shape
    ff = gate_weight.shape[2]
    fq = ff // NY
    n = CHUNKS
    wide = width + width // CUT
    vm = pltpu.VMEM
    dma = pltpu.SemaphoreType.DMA
    any_space = pl.BlockSpec(memory_space=pl.ANY)
    return pl.pallas_call(
        body,
        out_shape=vm((tok, width), BF16),
        in_specs=[any_space] * 6,
        out_specs=pl.BlockSpec(memory_space=vm),
        scratch_shapes=[
            vm((TOPK, tok), jnp.int32),
            vm((NZ, tok, width), BF16),
            vm((NZ, 2 * TOPK, tok), F32),
            vm((NZ, PLANE, tok), F32),
            vm((NZ, PLANE, tok), F32),
            vm((NZ, tok, 2 * (1 + CUT) * PLANE * MAIN), BF16),
            vm((width, 2 * ff), BF16),
            vm((ff, width), BF16),
            vm((NZ, PLANE * MAIN, wide), BF16),
            vm((n, LARGE * UROWS, wide), BF16),
            vm((ROWS, width), BF16),
            vm((2, n, ROWS, fq), BF16),
            vm((2, n, ROWS, fq), BF16),
            vm((2, ROWS, fq), F32),
            vm((2, n, ROWS, 2 * fq), BF16),
            vm((2, n, ROWS, 2 * fq), BF16),
            vm((2, ROWS, 2 * fq), F32),
            vm((n, ROWS, ff), BF16),
            vm((ROWS, width), BF16),
            vm((n, LARGE * UROWS, wide), BF16),
            vm((NZ, PLANE * MAIN, wide), BF16),
            vm((NZ, tok, width), F32),
            vm((NZ - 1, tok, width), BF16),
            vm((NZ - 1, tok, width), BF16),
            dma((3,)),
            dma((3 * NY,)),
            dma,
            dma((NZ - 1,)),
            dma,
            dma((NZ - 1,)),
            dma,
            dma((n, LARGE)),
            dma,
            dma((2, n, 2)),
            dma,
            dma((2, n, 2)),
            dma,
            dma((2, n, 2)),
            dma,
            dma((2, n)),
            dma,
            dma((NZ, NX)),
            dma,
            dma((NZ - 1, 2)),
        ],
        compiler_params=pltpu.CompilerParams(
            collective_id=0, has_side_effects=True, vmem_limit_bytes=60 * 1024 * 1024
        ),
        cost_estimate=pl.CostEstimate(flops=13 * 10**9, bytes_accessed=10 * 10**6, transcendentals=0),
    )(routes.T, combine_weight.T, tokens, gate_weight[0], up_weight[0], down_weight[0])


def solution(mesh):
    return jax.shard_map(
        shards,
        mesh=mesh,
        in_specs=(
            P("ep", "kv"),
            P("ep", None),
            P("ep", None),
            P("ep", "kv", None),
            P("ep", "kv", None),
            P("ep", None, "kv"),
        ),
        out_specs=P("ep", "kv"),
        check_vma=False,
    )
```

```python
import jax
import jax.numpy as jnp
from jax import lax
from jax.experimental import pallas as pl
from jax.experimental.pallas import tpu as pltpu
from jax.sharding import PartitionSpec as P

MESH = pl.DeviceIdType.MESH
F32, BF16 = jnp.float32, jnp.bfloat16
NZ, NX, NC, NY = 8, 4, 2, 4
PLANE = NX * NC
TOPK = 8

OFFSETS = (0, -1, 1, -2, 2, -3, 3, -4)
NEXT_HOP = {0: (1, 2), 1: (3,), 2: (4,), 3: (5,), 4: (6,), 5: (7,), 6: (), 7: ()}
LEFT_OUT = (7, 5, 3, 1)
RIGHT_OUT = (6, 4, 2)

MAIN, TAIL, CUT = 16, 4, 4

ORDER = tuple(
    tuple(divmod(unit, 10) for unit in chunk)
    for chunk in (
        (1, 0),
        (2, 20),
        (23, 11, 21, 12),
        (22, 31, 60, 41),
        (70, 42, 62, 61),
        (72, 63, 71, 73),
        (51, 53, 43, 52),
        (32, 40, 50, 33),
        (13, 30),
        (10, 3),
    )
)
CHUNKS, SMALL, LARGE = len(ORDER), 2, 4
POS = {unit: (k, a) for k, units in enumerate(ORDER) for a, unit in enumerate(units)}
UROWS = NC * MAIN
UNIT = NC * (MAIN + TAIL)
ROWS = LARGE * UNIT

PLANE_IN, COMBINE, LEAVE, SHARE = 0, 1, 2, 3
FIRST = ()
ALL_STEPS = tuple(range(CHUNKS + 2))
EARLY_A = (1, 2, 3, 4, 5, 6, 7, 8, 9, 10)
EARLY_M = (0, 1, 2, 3, 4, 5, 6, 8, 9)
EARLY_F = (1, 3, 4, 5, 6)
LATE_A = ()
LATE_M = (7,)
LATE_F = (2, 7, 8, 9, 10)
AFTER_P = {0: ((PLANE_IN, 1),), 2: ((SHARE, 3),)}
AFTER_EARLY_A = {1: ((SHARE, 1), (SHARE, 2)), 5: ((SHARE, 6),), 8: ((COMBINE, 6), (LEAVE, 6), (COMBINE, 7), (LEAVE, 7)), 10: ((COMBINE, 4), (LEAVE, 4))}
AFTER_EARLY_M = {0: ((PLANE_IN, 2),), 1: ((PLANE_IN, 3),), 2: ((PLANE_IN, 5), (PLANE_IN, 6)), 3: ((PLANE_IN, 7),), 4: ((SHARE, 7), (SHARE, 5))}
AFTER_EARLY_F = {1: ((PLANE_IN, 4),)}
AFTER_D = {}
AFTER_A = {}
AFTER_M = {}
AFTER_F = {7: ((SHARE, 0),), 9: ((COMBINE, 5), (LEAVE, 5), (SHARE, 4)), 10: ((COMBINE, 3), (LEAVE, 3))}
LAST = ((COMBINE, 2), (LEAVE, 2), (COMBINE, 1), (LEAVE, 1), (COMBINE, 0))

def body(
    rt_ref, wt_ref, tok_ref, wg_ref, wu_ref, wd_ref, out_ref,
    rt_own, tok_all, meta_all, vv, ww, shares_all, wgu, wdn, sel, xin, xrows, hop_s, hop_r, qf, qs, qr, own, hid, erow, eout, back,
    zp, zs, zr,
    in_sem, w_sem, zt_ss, zt_rs, zm_ss, zm_rs, x_ss, x_rs, hop_ss, hop_rs, q_ss, q_rs, ag_ss, ag_rs,
    fw_ss, fw_rs, b_ss, b_rs, z_ss, z_rs,
):
    tok, width = tok_ref.shape
    ff = wg_ref.shape[1]
    fq = ff // NY
    block = width // CUT
    ep, y = lax.axis_index("ep"), lax.axis_index("kv")
    z, x, c = ep // PLANE, lax.rem(ep // NC, NX), lax.rem(ep, NC)

    def dev(dz=0, dx=0, dc=0, dy=0):
        zz, xx, cc = lax.rem(z + dz + NZ, NZ), lax.rem(x + dx, NX), lax.rem(c + dc, NC)
        return {"ep": (zz * NX + xx) * NC + cc, "kv": lax.rem(y + dy + NY, NY)}

    def remote(src, dst, ss, rs, to):
        return pltpu.make_async_remote_copy(
            src_ref=src, dst_ref=dst, send_sem=ss, recv_sem=rs, device_id=to, device_id_type=MESH
        )

    up_y, down_y = dev(dy=1), dev(dy=-1)
    up_z, down_z = dev(dz=1), dev(dz=-1)
    plane = [(dx, dc) for dx in range(NX) for dc in range(NC)]
    mate = {at: dev(dx=at[0], dc=at[1]) for at in plane}

    def arrived(dst, rs):
        remote(dst, dst, rs, rs, up_y).wait_recv()

    def sent(src, ss):
        remote(src, src, ss, ss, up_y).wait_send()

    barrier = pltpu.get_barrier_semaphore()
    partners = [up_y, down_y, up_z, down_z] + [mate[at] for at in plane[1:]]
    for partner in partners:
        pl.semaphore_signal(barrier, inc=1, device_id=partner, device_id_type=MESH)

    inputs = [
        pltpu.make_async_copy(rt_ref, rt_own, in_sem.at[0]),
        pltpu.make_async_copy(wt_ref, meta_all.at[0, pl.ds(TOPK, TOPK)], in_sem.at[1]),
        pltpu.make_async_copy(tok_ref, tok_all.at[0], in_sem.at[2]),
    ]
    for load in inputs:
        load.start()

    loads = []
    for r in (2, 1, 3, 0):
        cols = pl.ds(pl.multiple_of(lax.rem(y + r, NY) * fq, 128), fq)
        loads += [
            pltpu.make_async_copy(wg_ref.at[:, cols], wgu.at[:, pl.ds(2 * r * fq, fq)], w_sem.at[3 * r]),
            pltpu.make_async_copy(wu_ref.at[:, cols], wgu.at[:, pl.ds((2 * r + 1) * fq, fq)], w_sem.at[3 * r + 1]),
            pltpu.make_async_copy(wd_ref.at[cols], wdn.at[pl.ds(r * fq, fq)], w_sem.at[3 * r + 2]),
        ]
    place = lax.rem(lax.broadcasted_iota(jnp.int32, (PLANE * MAIN, tok), 0), MAIN)
    main_slot = place.astype(F32)
    tail_slot = [
        jnp.where(lax.rem(place, CUT) == b, MAIN + place // CUT, -1).astype(F32) for b in range(CUT)
    ]

    def spread(rows):
        return jnp.concatenate([jnp.broadcast_to(rows[j : j + 1, :], (MAIN, tok)) for j in range(PLANE)], axis=0)

    def prepare(p):
        rt, wt = meta_all[p, 0:TOPK, :], meta_all[p, TOPK : 2 * TOPK, :]
        j = lax.broadcasted_iota(jnp.int32, (PLANE, tok), 0)
        expert = (z * NX + lax.rem(x + j // NC, NX)) * NC + lax.rem(c + lax.rem(j, NC), NC)
        expert = expert.astype(F32)
        hit = jnp.zeros((PLANE, tok), F32)
        share = jnp.zeros((PLANE, tok), F32)
        for k in range(TOPK):
            same = rt[k : k + 1, :] == expert
            hit += jnp.where(same, 1.0, 0.0)
            share += jnp.where(same, wt[k : k + 1, :], 0.0)
        earlier = lax.broadcasted_iota(jnp.int32, (tok, tok), 0) < lax.broadcasted_iota(jnp.int32, (tok, tok), 1)
        rank = jnp.dot(hit.astype(BF16), jnp.where(earlier, 1.0, 0.0).astype(BF16), preferred_element_type=F32)
        vv[p] = jnp.where(hit > 0.5, rank, -64.0)
        ww[p] = share

    def select(p):
        slot = spread(vv[p])
        tail = jnp.zeros((PLANE * MAIN, block), F32)
        first = jnp.where(slot == main_slot, 1.0, 0.0).astype(BF16)
        for b in range(CUT):
            cols = slice(b * block, (b + 1) * block)
            last = jnp.where(slot == tail_slot[b], 1.0, 0.0).astype(BF16)
            both = jnp.dot(jnp.concatenate([first, last], axis=0), tok_all[p, :, cols], preferred_element_type=F32)
            sel[p, :, cols] = both[: PLANE * MAIN].astype(BF16)
            tail += both[PLANE * MAIN :]
        sel[p, :, width:] = tail.astype(BF16)

    def share(p):
        expand = lax.broadcasted_iota(jnp.int32, (PLANE, PLANE * MAIN), 1) // MAIN
        expand = jnp.where(expand == lax.broadcasted_iota(jnp.int32, (PLANE, PLANE * MAIN), 0), 1.0, 0.0)

        def by_token(rows):
            return lax.dot_general(rows, expand, (((0,), (0,)), ((), ())), preferred_element_type=F32)

        weight = ww[p]
        high = weight.astype(BF16).astype(F32)
        slot, high, low = by_token(vv[p]), by_token(high), by_token(weight - high)
        lane = lax.rem(lax.broadcasted_iota(jnp.int32, (tok, PLANE * MAIN), 1), MAIN)
        wants = [lane] + [jnp.where(lax.rem(lane, CUT) == b, MAIN + lane // CUT, -1) for b in range(CUT)]
        for n, want in enumerate(wants):
            same = slot == want.astype(F32)
            both = jnp.concatenate([jnp.where(same, high, 0.0), jnp.where(same, low, 0.0)], axis=1)
            shares_all[p, :, 2 * n * PLANE * MAIN : 2 * (n + 1) * PLANE * MAIN] = both.astype(BF16)

    def dispatch(p):
        todo = []
        for dx, dc in plane:
            k, a = POS[p, (NX - dx) % NX]
            todo.append((k, dx != 2, dx, dc, a))
        for k, _, dx, dc, a in sorted(todo):
            src = sel.at[p, pl.ds((dx * NC + dc) * MAIN, MAIN)]
            dst = xin.at[k, pl.ds(a * UROWS + dc * MAIN, MAIN)]
            if dx == 0 and dc == 0:
                pltpu.make_async_copy(src, dst, x_rs.at[k, a]).start()
            else:
                remote(src, dst, x_ss, x_rs.at[k, a], mate[dx, dc]).start()

    def z_send(p):
        for q in NEXT_HOP[p]:
            to = up_z if OFFSETS[q] < 0 else down_z
            remote(meta_all.at[p], meta_all.at[q], zm_ss, zm_rs.at[q - 1], to).start()
            remote(tok_all.at[p], tok_all.at[q], zt_ss, zt_rs.at[q - 1], to).start()

    def z_arrived(p):
        arrived(meta_all.at[p], zm_rs.at[p - 1])
        arrived(tok_all.at[p], zt_rs.at[p - 1])
        z_send(p)
        prepare(p)
        select(p)
        dispatch(p)

    def picks(n, b, axis):
        shape = (n * UROWS // CUT, n * UROWS) if axis == 0 else (n * UROWS, n * UROWS // CUT)
        few, many = lax.broadcasted_iota(jnp.int32, shape, axis), lax.broadcasted_iota(jnp.int32, shape, 1 - axis)
        return jnp.where(many == few * CUT + b, 1.0, 0.0).astype(BF16)

    def parts(n):
        first = -(-n * UNIT // 32) * 16
        return [(0, first), (first, n * UNIT)]

    def partials(i, n):
        for a in range(n):
            arrived(xin.at[i, pl.ds(a * UROWS, UROWS)], x_rs.at[i, a])
        rows, whole = n * UNIT, n * UROWS
        xrows[:whole] = xin[i, :whole, :width]
        for b in range(CUT):
            tail = jnp.dot(picks(n, b, 0), xin[i, :whole, width:], preferred_element_type=F32)
            xrows[whole:rows, b * block : (b + 1) * block] = tail.astype(BF16)

        def part(r):
            return jnp.dot(xrows[:rows], wgu[:, 2 * r * fq : 2 * (r + 1) * fq], preferred_element_type=F32)

        far = part(2)
        hop_s[0, i, :rows] = far[:, :fq].astype(BF16)
        hop_s[1, i, :rows] = far[:, fq:].astype(BF16)
        for h, (low, high) in enumerate(parts(n)):
            at = pl.ds(low, high - low)
            for d, to in enumerate((up_y, down_y)):
                remote(hop_s.at[d, i, at], hop_r.at[d, i, at], hop_ss, hop_rs.at[d, i, h], to).start()
        above = part(1)
        qf[0, :rows] = above[:, :fq]
        qs[0, i, :rows, fq:] = above[:, fq:].astype(BF16)
        below = part(3)
        qs[1, i, :rows, :fq] = below[:, :fq].astype(BF16)
        qf[1, :rows] = below[:, fq:]
        own[lax.rem(i, 2), :rows] = part(0)

    def middle(i, n):
        for h, (low, high) in enumerate(parts(n)):
            at, rs = pl.ds(low, high - low), slice(low, high)
            for d, to in enumerate((up_y, down_y)):
                arrived(hop_r.at[d, i, at], hop_rs.at[d, i, h])
                total = qf[d, rs] + hop_r[d, i, rs].astype(F32)
                qs[d, i, rs, d * fq : (d + 1) * fq] = total.astype(BF16)
                remote(qs.at[d, i, at], qr.at[d, i, at], q_ss, q_rs.at[d, i, h], to).start()

    def half(i, n, r, h):
        low, high = parts(n)[h]
        return hid.at[i, r, pl.ds(low, high - low)]

    def activate(i, n):
        for h, (low, high) in enumerate(parts(n)):
            at, rs = pl.ds(low, high - low), slice(low, high)
            for d in range(2):
                arrived(qr.at[d, i, at], q_rs.at[d, i, h])
            total = own[lax.rem(i, 2), rs] + qr[0, i, rs].astype(F32) + qr[1, i, rs].astype(F32)
            gate, up = total[:, :fq], total[:, fq:]
            hid[i, 0, rs] = (gate / (1.0 + jnp.exp(-gate)) * up).astype(BF16)
            remote(half(i, n, 0, h), half(i, n, 3, h), ag_ss, ag_rs.at[0, i, h], up_y).start()
            remote(half(i, n, 0, h), half(i, n, 1, h), ag_ss, ag_rs.at[1, i, h], down_y).start()

    def forward(i, n):
        arrived(half(i, n, 3, 0), ag_rs.at[0, i, 0])
        remote(half(i, n, 3, 0), half(i, n, 2, 0), fw_ss, fw_rs.at[0, i], up_y).start()
        arrived(half(i, n, 1, 1), ag_rs.at[1, i, 1])
        remote(half(i, n, 1, 1), half(i, n, 2, 1), fw_ss, fw_rs.at[1, i], down_y).start()

    def send_back(k):
        todo = sorted((dx != 2, a, p, dx, dc) for a, (p, dx) in enumerate(ORDER[k]) for dc in range(NC))
        for _, a, p, dx, dc in todo:
            d = (NX - dx) % NX
            src = eout.at[k, pl.ds(a * UROWS + dc * MAIN, MAIN)]
            dst = back.at[p, pl.ds((d * NC + dc) * MAIN, MAIN)]
            if dx == 0 and dc == 0:
                pltpu.make_async_copy(src, dst, b_rs.at[p, d]).start()
            else:
                remote(src, dst, b_ss, b_rs.at[p, d], mate[dx, dc]).start()

    def down(i, n):
        arrived(half(i, n, 3, 1), ag_rs.at[0, i, 1])
        arrived(half(i, n, 1, 0), ag_rs.at[1, i, 0])
        arrived(half(i, n, 2, 0), fw_rs.at[0, i])
        arrived(half(i, n, 2, 1), fw_rs.at[1, i])
        rows, whole = n * UNIT, n * UROWS
        hidden = jnp.concatenate([hid[i, r, :rows] for r in range(NY)], axis=1)
        erow[:rows] = jnp.dot(hidden, wdn[...], preferred_element_type=F32).astype(BF16)
        eout[i, :whole, :width] = erow[:whole]
        tail = jnp.zeros((whole, block), F32)
        for b in range(CUT):
            last = erow[whole:rows, b * block : (b + 1) * block]
            tail += jnp.dot(picks(n, b, 1), last, preferred_element_type=F32)
        eout[i, :whole, width:] = tail.astype(BF16)
        for k in range(CHUNKS):
            if len(ORDER[k]) == n:
                pl.when(i == k)(lambda k=k: send_back(k))

    def combine(p):
        for d in range(NX):
            arrived(back.at[p, pl.ds(d * UROWS, UROWS)], b_rs.at[p, d])
        span = 2 * PLANE * MAIN
        last = back[p, :, width:]
        for b in range(CUT):
            cols = slice(b * block, (b + 1) * block)
            first = back[p, :, cols]
            weights = jnp.concatenate(
                [shares_all[p, :, :span], shares_all[p, :, (b + 1) * span : (b + 2) * span]], axis=1
            )
            rows = jnp.concatenate([first, first, last, last], axis=0)
            zp[p, :, cols] = jnp.dot(weights, rows, preferred_element_type=F32)

    z_parts = [pl.ds(0, tok // 2), pl.ds(tok // 2, tok // 2)]

    def leave(p):
        out, base, to = (LEFT_OUT, 0, down_z) if p in LEFT_OUT else (RIGHT_OUT, len(LEFT_OUT), up_z)
        h = base + out.index(p)
        for part, rows in enumerate(z_parts):
            at = slice(rows.start, rows.start + rows.size)
            total = zp[p, at]
            if h > base:
                arrived(zr.at[h - 1, rows], z_rs.at[h - 1, part])
                total = total + zr[h - 1, at].astype(F32)
            zs[h, at] = total.astype(BF16)
            remote(zs.at[h, rows], zr.at[h, rows], z_ss, z_rs.at[h, part], to).start()

    ops = {PLANE_IN: z_arrived, COMBINE: combine, LEAVE: leave, SHARE: share}

    def one_of(s, steps):
        hit = s == steps[0]
        for t in steps[1:]:
            hit = jnp.logical_or(hit, s == t)
        return hit

    def perform(todo):
        for op, p in todo:
            ops[op](p)

    for load in inputs:
        load.wait()
    meta_all[0, 0:TOPK, :] = rt_own[...].astype(F32)
    prepare(0)
    select(0)
    pl.semaphore_wait(barrier, len(partners))
    z_send(0)
    dispatch(0)
    for load in loads:
        load.start()
    perform(FIRST)
    for load in loads:
        load.wait()

    def step(s, carry):
        for run, lag, steps, table in (
            (partials, 0, ALL_STEPS, AFTER_P),
            (activate, 1, EARLY_A, AFTER_EARLY_A),
            (middle, 0, EARLY_M, AFTER_EARLY_M),
            (forward, 1, EARLY_F, AFTER_EARLY_F),
            (down, 2, ALL_STEPS, AFTER_D),
            (activate, 1, LATE_A, AFTER_A),
            (middle, 0, LATE_M, AFTER_M),
            (forward, 1, LATE_F, AFTER_F),
        ):
            i = s - lag
            for n in (LARGE, SMALL):
                at = [t for t in steps if 0 <= t - lag < CHUNKS and len(ORDER[t - lag]) == n]
                if at:
                    pl.when(one_of(s, at))(lambda run=run, i=i, n=n: run(i, n))
            for at, todo in table.items():
                pl.when(s == at)(lambda todo=todo: perform(todo))
        return carry

    lax.fori_loop(0, CHUNKS + 2, step, 0)
    perform(LAST)
    last_left, last_right = len(LEFT_OUT) - 1, len(LEFT_OUT) + len(RIGHT_OUT) - 1
    for part, rows in enumerate(z_parts):
        at = slice(rows.start, rows.start + rows.size)
        arrived(zr.at[last_right, rows], z_rs.at[last_right, part])
        arrived(zr.at[last_left, rows], z_rs.at[last_left, part])
        out_ref[at] = (zp[0, at] + zr[last_left, at].astype(F32) + zr[last_right, at].astype(F32)).astype(BF16)

    sent(meta_all.at[pl.ds(1, NZ - 1)], zm_ss)
    sent(tok_all.at[pl.ds(1, NZ - 1)], zt_ss)
    sent(sel.at[:, pl.ds(MAIN, (PLANE - 1) * MAIN)], x_ss)
    sent(hop_s.at[:, pl.ds(0, NZ)], hop_ss)
    sent(qs.at[:, pl.ds(0, NZ)], q_ss)
    sent(hop_s.at[:, pl.ds(0, NZ)], ag_ss)
    sent(hop_s.at[0, pl.ds(0, NZ)], fw_ss)
    sent(sel.at[:, pl.ds(MAIN, (PLANE - 1) * MAIN)], b_ss)
    sent(zs, z_ss)


def shards(tokens, routes, combine_weight, gate_weight, up_weight, down_weight):
    tok, width = tokens.shape
    ff = gate_weight.shape[2]
    fq = ff // NY
    n = CHUNKS
    wide = width + width // CUT
    vm = pltpu.VMEM
    dma = pltpu.SemaphoreType.DMA
    any_space = pl.BlockSpec(memory_space=pl.ANY)
    return pl.pallas_call(
        body,
        out_shape=vm((tok, width), BF16),
        in_specs=[any_space] * 6,
        out_specs=pl.BlockSpec(memory_space=vm),
        scratch_shapes=[
            vm((TOPK, tok), jnp.int32),
            vm((NZ, tok, width), BF16),
            vm((NZ, 2 * TOPK, tok), F32),
            vm((NZ, PLANE, tok), F32),
            vm((NZ, PLANE, tok), F32),
            vm((NZ, tok, 2 * (1 + CUT) * PLANE * MAIN), BF16),
            vm((width, 2 * ff), BF16),
            vm((ff, width), BF16),
            vm((NZ, PLANE * MAIN, wide), BF16),
            vm((n, LARGE * UROWS, wide), BF16),
            vm((ROWS, width), BF16),
            vm((2, n, ROWS, fq), BF16),
            vm((2, n, ROWS, fq), BF16),
            vm((2, ROWS, fq), F32),
            vm((2, n, ROWS, 2 * fq), BF16),
            vm((2, n, ROWS, 2 * fq), BF16),
            vm((2, ROWS, 2 * fq), F32),
            vm((n, NY, ROWS, fq), BF16),
            vm((ROWS, width), BF16),
            vm((n, LARGE * UROWS, wide), BF16),
            vm((NZ, PLANE * MAIN, wide), BF16),
            vm((NZ, tok, width), F32),
            vm((NZ - 1, tok, width), BF16),
            vm((NZ - 1, tok, width), BF16),
            dma((3,)),
            dma((3 * NY,)),
            dma,
            dma((NZ - 1,)),
            dma,
            dma((NZ - 1,)),
            dma,
            dma((n, LARGE)),
            dma,
            dma((2, n, 2)),
            dma,
            dma((2, n, 2)),
            dma,
            dma((2, n, 2)),
            dma,
            dma((2, n)),
            dma,
            dma((NZ, NX)),
            dma,
            dma((NZ - 1, 2)),
        ],
        compiler_params=pltpu.CompilerParams(
            collective_id=0, has_side_effects=True, vmem_limit_bytes=60 * 1024 * 1024
        ),
        cost_estimate=pl.CostEstimate(flops=13 * 10**9, bytes_accessed=10 * 10**6, transcendentals=0),
    )(routes.T, combine_weight.T, tokens, gate_weight[0], up_weight[0], down_weight[0])


def solution(mesh):
    return jax.shard_map(
        shards,
        mesh=mesh,
        in_specs=(
            P("ep", "kv"),
            P("ep", None),
            P("ep", None),
            P("ep", "kv", None),
            P("ep", "kv", None),
            P("ep", None, "kv"),
        ),
        out_specs=P("ep", "kv"),
        check_vma=False,
    )
```

```python
import jax
import jax.numpy as jnp
from jax import lax
from jax.experimental import pallas as pl
from jax.experimental.pallas import tpu as pltpu
from jax.sharding import PartitionSpec as P

MESH = pl.DeviceIdType.MESH
F32, BF16 = jnp.float32, jnp.bfloat16
NZ, NX, NC, NY = 8, 4, 2, 4
PLANE = NX * NC
TOPK = 8

OFFSETS = (0, -1, 1, -2, 2, -3, 3, -4)
NEXT_HOP = {0: (1, 2), 1: (3,), 2: (4,), 3: (5,), 4: (6,), 5: (7,), 6: (), 7: ()}
LEFT_OUT = (7, 5, 3, 1)
RIGHT_OUT = (6, 4, 2)

MAIN, TAIL, CUT = 16, 4, 4

ORDER = tuple(
    tuple(divmod(unit, 10) for unit in chunk)
    for chunk in (
        (3, 0),
        (10, 20),
        (21, 30, 12, 22),
        (51, 41, 50, 60),
        (70, 62, 71, 61),
        (72, 73, 63, 52),
        (31, 53, 42, 43),
        (40, 32, 23, 33),
        (13, 11),
        (2, 1),
    )
)
CHUNKS, SMALL, LARGE = len(ORDER), 2, 4
POS = {unit: (k, a) for k, units in enumerate(ORDER) for a, unit in enumerate(units)}
UROWS = NC * MAIN
UNIT = NC * (MAIN + TAIL)
ROWS = LARGE * UNIT

PLANE_IN, COMBINE, LEAVE, SHARE = 0, 1, 2, 3
FIRST = ()
ALL_STEPS = tuple(range(CHUNKS + 2))
EARLY_A = (1, 2, 3, 4, 5, 6, 7, 8, 9, 10)
EARLY_M = (0, 1, 2, 3, 4, 5, 6, 8, 9)
EARLY_F = (1, 2, 4, 5)
LATE_A = ()
LATE_M = (7,)
LATE_F = (3, 6, 7, 8, 9, 10)
AFTER_P = {0: ((PLANE_IN, 1), (SHARE, 1), (PLANE_IN, 2)), 7: ((SHARE, 7),), 8: ((SHARE, 5), (SHARE, 0), (COMBINE, 7), (COMBINE, 6), (LEAVE, 6))}
AFTER_EARLY_A = {1: ((PLANE_IN, 3),), 2: ((PLANE_IN, 5),), 3: ((PLANE_IN, 7), (SHARE, 4)), 8: ((LEAVE, 7),), 10: ((LEAVE, 4),)}
AFTER_EARLY_M = {1: ((SHARE, 3), (PLANE_IN, 4), (SHARE, 2)), 2: ((PLANE_IN, 6),)}
AFTER_EARLY_F = {}
AFTER_D = {}
AFTER_A = {}
AFTER_M = {}
AFTER_F = {6: ((SHARE, 6),), 9: ((COMBINE, 5), (LEAVE, 5), (COMBINE, 4)), 10: ((COMBINE, 2), (COMBINE, 3), (LEAVE, 3))}
LAST = ((COMBINE, 1), (LEAVE, 2), (LEAVE, 1), (COMBINE, 0))

def body(
    rt_ref, wt_ref, tok_ref, wg_ref, wu_ref, wd_ref, out_ref,
    rt_own, tok_all, meta_all, vv, ww, shares_all, wgu, wdn, sel, xin, xrows, hop_s, hop_r, qf, qs, qr, own, hid, erow, eout, back,
    zp, zs, zr,
    in_sem, w_sem, zt_ss, zt_rs, zm_ss, zm_rs, x_ss, x_rs, hop_ss, hop_rs, q_ss, q_rs, ag_ss, ag_rs,
    fw_ss, fw_rs, b_ss, b_rs, z_ss, z_rs,
):
    tok, width = tok_ref.shape
    ff = wg_ref.shape[1]
    fq = ff // NY
    block = width // CUT
    ep, y = lax.axis_index("ep"), lax.axis_index("kv")
    z, x, c = ep // PLANE, lax.rem(ep // NC, NX), lax.rem(ep, NC)

    def dev(dz=0, dx=0, dc=0, dy=0):
        zz, xx, cc = lax.rem(z + dz + NZ, NZ), lax.rem(x + dx, NX), lax.rem(c + dc, NC)
        return {"ep": (zz * NX + xx) * NC + cc, "kv": lax.rem(y + dy + NY, NY)}

    def remote(src, dst, ss, rs, to):
        return pltpu.make_async_remote_copy(
            src_ref=src, dst_ref=dst, send_sem=ss, recv_sem=rs, device_id=to, device_id_type=MESH
        )

    up_y, down_y = dev(dy=1), dev(dy=-1)
    up_z, down_z = dev(dz=1), dev(dz=-1)
    plane = [(dx, dc) for dx in range(NX) for dc in range(NC)]
    mate = {at: dev(dx=at[0], dc=at[1]) for at in plane}

    def arrived(dst, rs):
        remote(dst, dst, rs, rs, up_y).wait_recv()

    def sent(src, ss):
        remote(src, src, ss, ss, up_y).wait_send()

    barrier = pltpu.get_barrier_semaphore()
    partners = [up_y, down_y, up_z, down_z] + [mate[at] for at in plane[1:]]
    for partner in partners:
        pl.semaphore_signal(barrier, inc=1, device_id=partner, device_id_type=MESH)

    inputs = [
        pltpu.make_async_copy(rt_ref, rt_own, in_sem.at[0]),
        pltpu.make_async_copy(wt_ref, meta_all.at[0, pl.ds(TOPK, TOPK)], in_sem.at[1]),
        pltpu.make_async_copy(tok_ref, tok_all.at[0], in_sem.at[2]),
    ]
    for load in inputs:
        load.start()

    gate_up, to_width = {}, []
    for r in (2, 1, 3, 0):
        cols = pl.ds(pl.multiple_of(lax.rem(y + r, NY) * fq, 128), fq)
        gate_up[r] = [
            pltpu.make_async_copy(wg_ref.at[:, cols], wgu.at[:, pl.ds(2 * r * fq, fq)], w_sem.at[3 * r]),
            pltpu.make_async_copy(wu_ref.at[:, cols], wgu.at[:, pl.ds((2 * r + 1) * fq, fq)], w_sem.at[3 * r + 1]),
        ]
        to_width.append(pltpu.make_async_copy(wd_ref.at[cols], wdn.at[pl.ds(r * fq, fq)], w_sem.at[3 * r + 2]))

    place = lax.rem(lax.broadcasted_iota(jnp.int32, (PLANE * MAIN, tok), 0), MAIN)
    main_slot = place.astype(F32)
    tail_slot = [
        jnp.where(lax.rem(place, CUT) == b, MAIN + place // CUT, -1).astype(F32) for b in range(CUT)
    ]

    def spread(rows):
        return jnp.concatenate([jnp.broadcast_to(rows[j : j + 1, :], (MAIN, tok)) for j in range(PLANE)], axis=0)

    def prepare(p):
        rt, wt = meta_all[p, 0:TOPK, :], meta_all[p, TOPK : 2 * TOPK, :]
        j = lax.broadcasted_iota(jnp.int32, (PLANE, tok), 0)
        expert = (z * NX + lax.rem(x + j // NC, NX)) * NC + lax.rem(c + lax.rem(j, NC), NC)
        expert = expert.astype(F32)
        hit = jnp.zeros((PLANE, tok), F32)
        share = jnp.zeros((PLANE, tok), F32)
        for k in range(TOPK):
            same = rt[k : k + 1, :] == expert
            hit += jnp.where(same, 1.0, 0.0)
            share += jnp.where(same, wt[k : k + 1, :], 0.0)
        earlier = lax.broadcasted_iota(jnp.int32, (tok, tok), 0) < lax.broadcasted_iota(jnp.int32, (tok, tok), 1)
        rank = jnp.dot(hit.astype(BF16), jnp.where(earlier, 1.0, 0.0).astype(BF16), preferred_element_type=F32)
        vv[p] = jnp.where(hit > 0.5, rank, -64.0)
        ww[p] = share

    def select(p):
        slot = spread(vv[p])
        tail = jnp.zeros((PLANE * MAIN, block), F32)
        first = jnp.where(slot == main_slot, 1.0, 0.0).astype(BF16)
        for b in range(CUT):
            cols = slice(b * block, (b + 1) * block)
            last = jnp.where(slot == tail_slot[b], 1.0, 0.0).astype(BF16)
            both = jnp.dot(jnp.concatenate([first, last], axis=0), tok_all[p, :, cols], preferred_element_type=F32)
            sel[p, :, cols] = both[: PLANE * MAIN].astype(BF16)
            tail += both[PLANE * MAIN :]
        sel[p, :, width:] = tail.astype(BF16)

    def share(p):
        expand = lax.broadcasted_iota(jnp.int32, (PLANE, PLANE * MAIN), 1) // MAIN
        expand = jnp.where(expand == lax.broadcasted_iota(jnp.int32, (PLANE, PLANE * MAIN), 0), 1.0, 0.0)

        def by_token(rows):
            return lax.dot_general(rows, expand, (((0,), (0,)), ((), ())), preferred_element_type=F32)

        weight = ww[p]
        high = weight.astype(BF16).astype(F32)
        slot, high, low = by_token(vv[p]), by_token(high), by_token(weight - high)
        lane = lax.rem(lax.broadcasted_iota(jnp.int32, (tok, PLANE * MAIN), 1), MAIN)
        wants = [lane] + [jnp.where(lax.rem(lane, CUT) == b, MAIN + lane // CUT, -1) for b in range(CUT)]
        for n, want in enumerate(wants):
            same = slot == want.astype(F32)
            both = jnp.concatenate([jnp.where(same, high, 0.0), jnp.where(same, low, 0.0)], axis=1)
            shares_all[p, :, 2 * n * PLANE * MAIN : 2 * (n + 1) * PLANE * MAIN] = both.astype(BF16)

    def dispatch(p):
        todo = []
        for dx, dc in plane:
            k, a = POS[p, (NX - dx) % NX]
            todo.append((k, dx != 2, dx, dc, a))
        for k, _, dx, dc, a in sorted(todo):
            src = sel.at[p, pl.ds((dx * NC + dc) * MAIN, MAIN)]
            dst = xin.at[k, pl.ds(a * UROWS + dc * MAIN, MAIN)]
            if dx == 0 and dc == 0:
                pltpu.make_async_copy(src, dst, x_rs.at[k, a]).start()
            else:
                remote(src, dst, x_ss, x_rs.at[k, a], mate[dx, dc]).start()

    def z_send(p):
        for q in NEXT_HOP[p]:
            to = up_z if OFFSETS[q] < 0 else down_z
            remote(meta_all.at[p], meta_all.at[q], zm_ss, zm_rs.at[q - 1], to).start()
            remote(tok_all.at[p], tok_all.at[q], zt_ss, zt_rs.at[q - 1], to).start()

    def z_arrived(p):
        arrived(meta_all.at[p], zm_rs.at[p - 1])
        arrived(tok_all.at[p], zt_rs.at[p - 1])
        z_send(p)
        prepare(p)
        select(p)
        dispatch(p)

    def picks(n, b, axis):
        shape = (n * UROWS // CUT, n * UROWS) if axis == 0 else (n * UROWS, n * UROWS // CUT)
        few, many = lax.broadcasted_iota(jnp.int32, shape, axis), lax.broadcasted_iota(jnp.int32, shape, 1 - axis)
        return jnp.where(many == few * CUT + b, 1.0, 0.0).astype(BF16)

    def parts(n):
        first = -(-n * UNIT // 32) * 16
        return [(0, first), (first, n * UNIT)]

    def partials(i, n):
        for a in range(n):
            arrived(xin.at[i, pl.ds(a * UROWS, UROWS)], x_rs.at[i, a])
        rows, whole = n * UNIT, n * UROWS
        xrows[:whole] = xin[i, :whole, :width]
        for b in range(CUT):
            tail = jnp.dot(picks(n, b, 0), xin[i, :whole, width:], preferred_element_type=F32)
            xrows[whole:rows, b * block : (b + 1) * block] = tail.astype(BF16)

        def part(r):
            if len(ORDER[0]) == n:

                @pl.when(i == 0)
                def _():
                    for load in gate_up[r]:
                        load.wait()

            return jnp.dot(xrows[:rows], wgu[:, 2 * r * fq : 2 * (r + 1) * fq], preferred_element_type=F32)

        far = part(2)
        hop_s[0, i, :rows] = far[:, :fq].astype(BF16)
        hop_s[1, i, :rows] = far[:, fq:].astype(BF16)
        for h, (low, high) in enumerate(parts(n)):
            at = pl.ds(low, high - low)
            for d, to in enumerate((up_y, down_y)):
                remote(hop_s.at[d, i, at], hop_r.at[d, i, at], hop_ss, hop_rs.at[d, i, h], to).start()
        above = part(1)
        qf[0, :rows] = above[:, :fq]
        qs[0, i, :rows, fq:] = above[:, fq:].astype(BF16)
        below = part(3)
        qs[1, i, :rows, :fq] = below[:, :fq].astype(BF16)
        qf[1, :rows] = below[:, fq:]
        own[lax.rem(i, 2), :rows] = part(0)

    def middle(i, n):
        for h, (low, high) in enumerate(parts(n)):
            at, rs = pl.ds(low, high - low), slice(low, high)
            for d, to in enumerate((up_y, down_y)):
                arrived(hop_r.at[d, i, at], hop_rs.at[d, i, h])
                total = qf[d, rs] + hop_r[d, i, rs].astype(F32)
                qs[d, i, rs, d * fq : (d + 1) * fq] = total.astype(BF16)
                remote(qs.at[d, i, at], qr.at[d, i, at], q_ss, q_rs.at[d, i, h], to).start()

    def half(i, n, r, h):
        low, high = parts(n)[h]
        return hid.at[i, r, pl.ds(low, high - low)]

    def activate(i, n):
        for h, (low, high) in enumerate(parts(n)):
            at, rs = pl.ds(low, high - low), slice(low, high)
            for d in range(2):
                arrived(qr.at[d, i, at], q_rs.at[d, i, h])
            total = own[lax.rem(i, 2), rs] + qr[0, i, rs].astype(F32) + qr[1, i, rs].astype(F32)
            gate, up = total[:, :fq], total[:, fq:]
            hid[i, 0, rs] = (gate / (1.0 + jnp.exp(-gate)) * up).astype(BF16)
            remote(half(i, n, 0, h), half(i, n, 3, h), ag_ss, ag_rs.at[0, i, h], up_y).start()
            remote(half(i, n, 0, h), half(i, n, 1, h), ag_ss, ag_rs.at[1, i, h], down_y).start()

    def forward(i, n):
        arrived(half(i, n, 3, 0), ag_rs.at[0, i, 0])
        remote(half(i, n, 3, 0), half(i, n, 2, 0), fw_ss, fw_rs.at[0, i], up_y).start()
        arrived(half(i, n, 1, 1), ag_rs.at[1, i, 1])
        remote(half(i, n, 1, 1), half(i, n, 2, 1), fw_ss, fw_rs.at[1, i], down_y).start()

    def send_back(k):
        todo = sorted((dx != 2, a, p, dx, dc) for a, (p, dx) in enumerate(ORDER[k]) for dc in range(NC))
        for _, a, p, dx, dc in todo:
            d = (NX - dx) % NX
            src = eout.at[k, pl.ds(a * UROWS + dc * MAIN, MAIN)]
            dst = back.at[p, pl.ds((d * NC + dc) * MAIN, MAIN)]
            if dx == 0 and dc == 0:
                pltpu.make_async_copy(src, dst, b_rs.at[p, d]).start()
            else:
                remote(src, dst, b_ss, b_rs.at[p, d], mate[dx, dc]).start()

    def down(i, n):
        arrived(half(i, n, 3, 1), ag_rs.at[0, i, 1])
        arrived(half(i, n, 1, 0), ag_rs.at[1, i, 0])
        arrived(half(i, n, 2, 0), fw_rs.at[0, i])
        arrived(half(i, n, 2, 1), fw_rs.at[1, i])
        rows, whole = n * UNIT, n * UROWS
        if len(ORDER[0]) == n:

            @pl.when(i == 0)
            def _():
                for load in to_width:
                    load.wait()

        hidden = jnp.concatenate([hid[i, r, :rows] for r in range(NY)], axis=1)
        erow[:rows] = jnp.dot(hidden, wdn[...], preferred_element_type=F32).astype(BF16)
        eout[i, :whole, :width] = erow[:whole]
        tail = jnp.zeros((whole, block), F32)
        for b in range(CUT):
            last = erow[whole:rows, b * block : (b + 1) * block]
            tail += jnp.dot(picks(n, b, 1), last, preferred_element_type=F32)
        eout[i, :whole, width:] = tail.astype(BF16)
        for k in range(CHUNKS):
            if len(ORDER[k]) == n:
                pl.when(i == k)(lambda k=k: send_back(k))

    def combine(p):
        for d in range(NX):
            arrived(back.at[p, pl.ds(d * UROWS, UROWS)], b_rs.at[p, d])
        span = 2 * PLANE * MAIN
        last = back[p, :, width:]
        for b in range(CUT):
            cols = slice(b * block, (b + 1) * block)
            first = back[p, :, cols]
            weights = jnp.concatenate(
                [shares_all[p, :, :span], shares_all[p, :, (b + 1) * span : (b + 2) * span]], axis=1
            )
            rows = jnp.concatenate([first, first, last, last], axis=0)
            zp[p, :, cols] = jnp.dot(weights, rows, preferred_element_type=F32)

    z_parts = [pl.ds(0, tok // 2), pl.ds(tok // 2, tok // 2)]

    def leave(p):
        out, base, to = (LEFT_OUT, 0, down_z) if p in LEFT_OUT else (RIGHT_OUT, len(LEFT_OUT), up_z)
        h = base + out.index(p)
        for part, rows in enumerate(z_parts):
            at = slice(rows.start, rows.start + rows.size)
            total = zp[p, at]
            if h > base:
                arrived(zr.at[h - 1, rows], z_rs.at[h - 1, part])
                total = total + zr[h - 1, at].astype(F32)
            zs[h, at] = total.astype(BF16)
            remote(zs.at[h, rows], zr.at[h, rows], z_ss, z_rs.at[h, part], to).start()

    ops = {PLANE_IN: z_arrived, COMBINE: combine, LEAVE: leave, SHARE: share}

    def one_of(s, steps):
        hit = s == steps[0]
        for t in steps[1:]:
            hit = jnp.logical_or(hit, s == t)
        return hit

    def perform(todo):
        for op, p in todo:
            ops[op](p)

    for load in inputs:
        load.wait()
    meta_all[0, 0:TOPK, :] = rt_own[...].astype(F32)
    prepare(0)
    select(0)
    pl.semaphore_wait(barrier, len(partners))
    z_send(0)
    dispatch(0)
    for load in [*gate_up[2], *gate_up[1], *gate_up[3], *gate_up[0], *to_width]:
        load.start()
    perform(FIRST)

    def step(s, carry):
        for run, lag, steps, table in (
            (partials, 0, ALL_STEPS, AFTER_P),
            (activate, 1, EARLY_A, AFTER_EARLY_A),
            (middle, 0, EARLY_M, AFTER_EARLY_M),
            (forward, 1, EARLY_F, AFTER_EARLY_F),
            (down, 2, ALL_STEPS, AFTER_D),
            (activate, 1, LATE_A, AFTER_A),
            (middle, 0, LATE_M, AFTER_M),
            (forward, 1, LATE_F, AFTER_F),
        ):
            i = s - lag
            for n in (LARGE, SMALL):
                at = [t for t in steps if 0 <= t - lag < CHUNKS and len(ORDER[t - lag]) == n]
                if at:
                    pl.when(one_of(s, at))(lambda run=run, i=i, n=n: run(i, n))
            for at, todo in table.items():
                pl.when(s == at)(lambda todo=todo: perform(todo))
        return carry

    lax.fori_loop(0, CHUNKS + 2, step, 0)
    perform(LAST)
    last_left, last_right = len(LEFT_OUT) - 1, len(LEFT_OUT) + len(RIGHT_OUT) - 1
    for part, rows in enumerate(z_parts):
        at = slice(rows.start, rows.start + rows.size)
        arrived(zr.at[last_right, rows], z_rs.at[last_right, part])
        arrived(zr.at[last_left, rows], z_rs.at[last_left, part])
        out_ref[at] = (zp[0, at] + zr[last_left, at].astype(F32) + zr[last_right, at].astype(F32)).astype(BF16)

    sent(meta_all.at[pl.ds(1, NZ - 1)], zm_ss)
    sent(tok_all.at[pl.ds(1, NZ - 1)], zt_ss)
    sent(sel.at[:, pl.ds(MAIN, (PLANE - 1) * MAIN)], x_ss)
    sent(hop_s.at[:, pl.ds(0, NZ)], hop_ss)
    sent(qs.at[:, pl.ds(0, NZ)], q_ss)
    sent(hop_s.at[:, pl.ds(0, NZ)], ag_ss)
    sent(hop_s.at[0, pl.ds(0, NZ)], fw_ss)
    sent(sel.at[:, pl.ds(MAIN, (PLANE - 1) * MAIN)], b_ss)
    sent(zs, z_ss)


def shards(tokens, routes, combine_weight, gate_weight, up_weight, down_weight):
    tok, width = tokens.shape
    ff = gate_weight.shape[2]
    fq = ff // NY
    n = CHUNKS
    wide = width + width // CUT
    vm = pltpu.VMEM
    dma = pltpu.SemaphoreType.DMA
    any_space = pl.BlockSpec(memory_space=pl.ANY)
    return pl.pallas_call(
        body,
        out_shape=vm((tok, width), BF16),
        in_specs=[any_space] * 6,
        out_specs=pl.BlockSpec(memory_space=vm),
        scratch_shapes=[
            vm((TOPK, tok), jnp.int32),
            vm((NZ, tok, width), BF16),
            vm((NZ, 2 * TOPK, tok), F32),
            vm((NZ, PLANE, tok), F32),
            vm((NZ, PLANE, tok), F32),
            vm((NZ, tok, 2 * (1 + CUT) * PLANE * MAIN), BF16),
            vm((width, 2 * ff), BF16),
            vm((ff, width), BF16),
            vm((NZ, PLANE * MAIN, wide), BF16),
            vm((n, LARGE * UROWS, wide), BF16),
            vm((ROWS, width), BF16),
            vm((2, n, ROWS, fq), BF16),
            vm((2, n, ROWS, fq), BF16),
            vm((2, ROWS, fq), F32),
            vm((2, n, ROWS, 2 * fq), BF16),
            vm((2, n, ROWS, 2 * fq), BF16),
            vm((2, ROWS, 2 * fq), F32),
            vm((n, NY, ROWS, fq), BF16),
            vm((ROWS, width), BF16),
            vm((n, LARGE * UROWS, wide), BF16),
            vm((NZ, PLANE * MAIN, wide), BF16),
            vm((NZ, tok, width), F32),
            vm((NZ - 1, tok, width), BF16),
            vm((NZ - 1, tok, width), BF16),
            dma((3,)),
            dma((3 * NY,)),
            dma,
            dma((NZ - 1,)),
            dma,
            dma((NZ - 1,)),
            dma,
            dma((n, LARGE)),
            dma,
            dma((2, n, 2)),
            dma,
            dma((2, n, 2)),
            dma,
            dma((2, n, 2)),
            dma,
            dma((2, n)),
            dma,
            dma((NZ, NX)),
            dma,
            dma((NZ - 1, 2)),
        ],
        compiler_params=pltpu.CompilerParams(
            collective_id=0, has_side_effects=True, vmem_limit_bytes=60 * 1024 * 1024
        ),
        cost_estimate=pl.CostEstimate(flops=13 * 10**9, bytes_accessed=10 * 10**6, transcendentals=0),
    )(routes.T, combine_weight.T, tokens, gate_weight[0], up_weight[0], down_weight[0])


def solution(mesh):
    return jax.shard_map(
        shards,
        mesh=mesh,
        in_specs=(
            P("ep", "kv"),
            P("ep", None),
            P("ep", None),
            P("ep", "kv", None),
            P("ep", "kv", None),
            P("ep", None, "kv"),
        ),
        out_specs=P("ep", "kv"),
        check_vma=False,
    )
```

```python
import jax
import jax.numpy as jnp
from jax import lax
from jax.experimental import pallas as pl
from jax.experimental.pallas import tpu as pltpu
from jax.sharding import PartitionSpec as P

MESH = pl.DeviceIdType.MESH
F32, BF16 = jnp.float32, jnp.bfloat16
NZ, NX, NC, NY = 8, 4, 2, 4
PLANE = NX * NC
TOPK = 8

OFFSETS = (0, -1, 1, -2, 2, -3, 3, -4)
NEXT_HOP = {0: (1, 2), 1: (3,), 2: (4,), 3: (5,), 4: (6,), 5: (7,), 6: (), 7: ()}
LEFT_OUT = (7, 5, 3, 1)
RIGHT_OUT = (6, 4, 2)

MAIN, TAIL, CUT = 16, 4, 4

ORDER = tuple(
    tuple(divmod(unit, 10) for unit in chunk)
    for chunk in (
        (1, 0),
        (2, 20),
        (23, 11, 21, 12),
        (22, 31, 60, 41),
        (70, 42, 62, 61),
        (72, 63, 71, 73),
        (51, 53, 43, 52),
        (32, 40, 50, 33),
        (13, 30),
        (10, 3),
    )
)
CHUNKS, SMALL, LARGE = len(ORDER), 2, 4
POS = {unit: (k, a) for k, units in enumerate(ORDER) for a, unit in enumerate(units)}
UROWS = NC * MAIN
UNIT = NC * (MAIN + TAIL)
ROWS = LARGE * UNIT

PLANE_IN, COMBINE, LEAVE, SHARE = 0, 1, 2, 3
FIRST = ()
ALL_STEPS = tuple(range(CHUNKS + 2))
EARLY_A = (1, 2, 3, 4, 5, 6, 7, 8, 9, 10)
EARLY_M = (0, 1, 2, 3, 4, 5, 6, 8, 9)
EARLY_F = (1, 3, 4, 5, 6)
LATE_A = ()
LATE_M = (7,)
LATE_F = (2, 7, 8, 9, 10)
AFTER_P = {0: ((PLANE_IN, 1),), 2: ((SHARE, 3),)}
AFTER_EARLY_A = {1: ((SHARE, 1), (SHARE, 2)), 5: ((SHARE, 6),), 8: ((COMBINE, 6), (LEAVE, 6), (COMBINE, 7), (LEAVE, 7)), 10: ((COMBINE, 4), (LEAVE, 4))}
AFTER_EARLY_M = {0: ((PLANE_IN, 2),), 1: ((PLANE_IN, 3),), 2: ((PLANE_IN, 5), (PLANE_IN, 6)), 3: ((PLANE_IN, 7),), 4: ((SHARE, 7), (SHARE, 5))}
AFTER_EARLY_F = {1: ((PLANE_IN, 4),)}
AFTER_D = {}
AFTER_A = {}
AFTER_M = {}
AFTER_F = {7: ((SHARE, 0),), 9: ((COMBINE, 5), (LEAVE, 5), (SHARE, 4)), 10: ((COMBINE, 3), (LEAVE, 3))}
LAST = ((COMBINE, 2), (LEAVE, 2), (COMBINE, 1), (LEAVE, 1), (COMBINE, 0))

def body(
    rt_ref, wt_ref, tok_ref, wg_ref, wu_ref, wd_ref, out_ref,
    rt_own, tok_all, meta_all, vv, ww, shares_all, wgu, wdn, sel, xin, xrows, hop_s, hop_r, qf, qs, qr, own, hid, erow, eout, back,
    zp, zs, zr,
    in_sem, w_sem, zt_ss, zt_rs, zm_ss, zm_rs, x_ss, x_rs, hop_ss, hop_rs, q_ss, q_rs, ag_ss, ag_rs,
    fw_ss, fw_rs, b_ss, b_rs, z_ss, z_rs,
):
    tok, width = tok_ref.shape
    ff = wg_ref.shape[1]
    fq = ff // NY
    block = width // CUT
    ep, y = lax.axis_index("ep"), lax.axis_index("kv")
    z, x, c = ep // PLANE, lax.rem(ep // NC, NX), lax.rem(ep, NC)

    def dev(dz=0, dx=0, dc=0, dy=0):
        zz, xx, cc = lax.rem(z + dz + NZ, NZ), lax.rem(x + dx, NX), lax.rem(c + dc, NC)
        return {"ep": (zz * NX + xx) * NC + cc, "kv": lax.rem(y + dy + NY, NY)}

    def remote(src, dst, ss, rs, to):
        return pltpu.make_async_remote_copy(
            src_ref=src, dst_ref=dst, send_sem=ss, recv_sem=rs, device_id=to, device_id_type=MESH
        )

    up_y, down_y = dev(dy=1), dev(dy=-1)
    up_z, down_z = dev(dz=1), dev(dz=-1)
    plane = [(dx, dc) for dx in range(NX) for dc in range(NC)]
    mate = {at: dev(dx=at[0], dc=at[1]) for at in plane}

    def arrived(dst, rs):
        remote(dst, dst, rs, rs, up_y).wait_recv()

    def sent(src, ss):
        remote(src, src, ss, ss, up_y).wait_send()

    barrier = pltpu.get_barrier_semaphore()
    partners = [up_y, down_y, up_z, down_z] + [mate[at] for at in plane[1:]]
    for partner in partners:
        pl.semaphore_signal(barrier, inc=1, device_id=partner, device_id_type=MESH)

    inputs = [
        pltpu.make_async_copy(rt_ref, rt_own, in_sem.at[0]),
        pltpu.make_async_copy(wt_ref, meta_all.at[0, pl.ds(TOPK, TOPK)], in_sem.at[1]),
        pltpu.make_async_copy(tok_ref, tok_all.at[0], in_sem.at[2]),
    ]
    for load in inputs:
        load.start()

    gate_up, to_width = {}, []
    for r in (2, 1, 3, 0):
        cols = pl.ds(pl.multiple_of(lax.rem(y + r, NY) * fq, 128), fq)
        gate_up[r] = [
            pltpu.make_async_copy(wg_ref.at[:, cols], wgu.at[:, pl.ds(2 * r * fq, fq)], w_sem.at[3 * r]),
            pltpu.make_async_copy(wu_ref.at[:, cols], wgu.at[:, pl.ds((2 * r + 1) * fq, fq)], w_sem.at[3 * r + 1]),
        ]
        to_width.append(pltpu.make_async_copy(wd_ref.at[cols], wdn.at[pl.ds(r * fq, fq)], w_sem.at[3 * r + 2]))

    place = lax.rem(lax.broadcasted_iota(jnp.int32, (PLANE * MAIN, tok), 0), MAIN)
    main_slot = place.astype(F32)
    tail_slot = [
        jnp.where(lax.rem(place, CUT) == b, MAIN + place // CUT, -1).astype(F32) for b in range(CUT)
    ]

    def spread(rows):
        return jnp.concatenate([jnp.broadcast_to(rows[j : j + 1, :], (MAIN, tok)) for j in range(PLANE)], axis=0)

    def prepare(p):
        rt, wt = meta_all[p, 0:TOPK, :], meta_all[p, TOPK : 2 * TOPK, :]
        j = lax.broadcasted_iota(jnp.int32, (PLANE, tok), 0)
        expert = (z * NX + lax.rem(x + j // NC, NX)) * NC + lax.rem(c + lax.rem(j, NC), NC)
        expert = expert.astype(F32)
        hit = jnp.zeros((PLANE, tok), F32)
        share = jnp.zeros((PLANE, tok), F32)
        for k in range(TOPK):
            same = rt[k : k + 1, :] == expert
            hit += jnp.where(same, 1.0, 0.0)
            share += jnp.where(same, wt[k : k + 1, :], 0.0)
        earlier = lax.broadcasted_iota(jnp.int32, (tok, tok), 0) < lax.broadcasted_iota(jnp.int32, (tok, tok), 1)
        rank = jnp.dot(hit.astype(BF16), jnp.where(earlier, 1.0, 0.0).astype(BF16), preferred_element_type=F32)
        vv[p] = jnp.where(hit > 0.5, rank, -64.0)
        ww[p] = share

    def select(p):
        slot = spread(vv[p])
        tail = jnp.zeros((PLANE * MAIN, block), F32)
        first = jnp.where(slot == main_slot, 1.0, 0.0).astype(BF16)
        for b in range(CUT):
            cols = slice(b * block, (b + 1) * block)
            last = jnp.where(slot == tail_slot[b], 1.0, 0.0).astype(BF16)
            both = jnp.dot(jnp.concatenate([first, last], axis=0), tok_all[p, :, cols], preferred_element_type=F32)
            sel[p, :, cols] = both[: PLANE * MAIN].astype(BF16)
            tail += both[PLANE * MAIN :]
        sel[p, :, width:] = tail.astype(BF16)

    def share(p):
        expand = lax.broadcasted_iota(jnp.int32, (PLANE, PLANE * MAIN), 1) // MAIN
        expand = jnp.where(expand == lax.broadcasted_iota(jnp.int32, (PLANE, PLANE * MAIN), 0), 1.0, 0.0)

        def by_token(rows):
            return lax.dot_general(rows, expand, (((0,), (0,)), ((), ())), preferred_element_type=F32)

        weight = ww[p]
        high = weight.astype(BF16).astype(F32)
        slot, high, low = by_token(vv[p]), by_token(high), by_token(weight - high)
        lane = lax.rem(lax.broadcasted_iota(jnp.int32, (tok, PLANE * MAIN), 1), MAIN)
        wants = [lane] + [jnp.where(lax.rem(lane, CUT) == b, MAIN + lane // CUT, -1) for b in range(CUT)]
        for n, want in enumerate(wants):
            same = slot == want.astype(F32)
            both = jnp.concatenate([jnp.where(same, high, 0.0), jnp.where(same, low, 0.0)], axis=1)
            shares_all[p, :, 2 * n * PLANE * MAIN : 2 * (n + 1) * PLANE * MAIN] = both.astype(BF16)

    def dispatch(p):
        todo = []
        for dx, dc in plane:
            k, a = POS[p, (NX - dx) % NX]
            todo.append((k, dx != 2, dx, dc, a))
        for k, _, dx, dc, a in sorted(todo):
            src = sel.at[p, pl.ds((dx * NC + dc) * MAIN, MAIN)]
            dst = xin.at[k, pl.ds(a * UROWS + dc * MAIN, MAIN)]
            if dx == 0 and dc == 0:
                pltpu.make_async_copy(src, dst, x_rs.at[k, a]).start()
            else:
                remote(src, dst, x_ss, x_rs.at[k, a], mate[dx, dc]).start()

    def z_send(p):
        for q in NEXT_HOP[p]:
            to = up_z if OFFSETS[q] < 0 else down_z
            remote(meta_all.at[p], meta_all.at[q], zm_ss, zm_rs.at[q - 1], to).start()
            remote(tok_all.at[p], tok_all.at[q], zt_ss, zt_rs.at[q - 1], to).start()

    def z_arrived(p):
        arrived(meta_all.at[p], zm_rs.at[p - 1])
        arrived(tok_all.at[p], zt_rs.at[p - 1])
        z_send(p)
        prepare(p)
        select(p)
        dispatch(p)

    def picks(n, b, axis):
        shape = (n * UROWS // CUT, n * UROWS) if axis == 0 else (n * UROWS, n * UROWS // CUT)
        few, many = lax.broadcasted_iota(jnp.int32, shape, axis), lax.broadcasted_iota(jnp.int32, shape, 1 - axis)
        return jnp.where(many == few * CUT + b, 1.0, 0.0).astype(BF16)

    def parts(n):
        first = -(-n * UNIT // 32) * 16
        return [(0, first), (first, n * UNIT)]

    def partials(i, n):
        for a in range(n):
            arrived(xin.at[i, pl.ds(a * UROWS, UROWS)], x_rs.at[i, a])
        rows, whole = n * UNIT, n * UROWS
        xrows[:whole] = xin[i, :whole, :width]
        for b in range(CUT):
            tail = jnp.dot(picks(n, b, 0), xin[i, :whole, width:], preferred_element_type=F32)
            xrows[whole:rows, b * block : (b + 1) * block] = tail.astype(BF16)

        def part(r):
            if len(ORDER[0]) == n:

                @pl.when(i == 0)
                def _():
                    for load in gate_up[r]:
                        load.wait()

            return jnp.dot(xrows[:rows], wgu[:, 2 * r * fq : 2 * (r + 1) * fq], preferred_element_type=F32)

        far = part(2)
        hop_s[0, i, :rows] = far[:, :fq].astype(BF16)
        hop_s[1, i, :rows] = far[:, fq:].astype(BF16)
        for h, (low, high) in enumerate(parts(n)):
            at = pl.ds(low, high - low)
            for d, to in enumerate((up_y, down_y)):
                remote(hop_s.at[d, i, at], hop_r.at[d, i, at], hop_ss, hop_rs.at[d, i, h], to).start()
        above = part(1)
        qf[0, :rows] = above[:, :fq]
        qs[0, i, :rows, fq:] = above[:, fq:].astype(BF16)
        below = part(3)
        qs[1, i, :rows, :fq] = below[:, :fq].astype(BF16)
        qf[1, :rows] = below[:, fq:]
        own[lax.rem(i, 2), :rows] = part(0)

    def middle(i, n):
        for h, (low, high) in enumerate(parts(n)):
            at, rs = pl.ds(low, high - low), slice(low, high)
            for d, to in enumerate((up_y, down_y)):
                arrived(hop_r.at[d, i, at], hop_rs.at[d, i, h])
                total = qf[d, rs] + hop_r[d, i, rs].astype(F32)
                qs[d, i, rs, d * fq : (d + 1) * fq] = total.astype(BF16)
                remote(qs.at[d, i, at], qr.at[d, i, at], q_ss, q_rs.at[d, i, h], to).start()

    def half(i, n, r, h):
        low, high = parts(n)[h]
        return hid.at[i, r, pl.ds(low, high - low)]

    def activate(i, n):
        for h, (low, high) in enumerate(parts(n)):
            at, rs = pl.ds(low, high - low), slice(low, high)
            for d in range(2):
                arrived(qr.at[d, i, at], q_rs.at[d, i, h])
            total = own[lax.rem(i, 2), rs] + qr[0, i, rs].astype(F32) + qr[1, i, rs].astype(F32)
            gate, up = total[:, :fq], total[:, fq:]
            hid[i, 0, rs] = (gate / (1.0 + jnp.exp(-gate)) * up).astype(BF16)
            remote(half(i, n, 0, h), half(i, n, 3, h), ag_ss, ag_rs.at[0, i, h], up_y).start()
            remote(half(i, n, 0, h), half(i, n, 1, h), ag_ss, ag_rs.at[1, i, h], down_y).start()

    def forward(i, n):
        arrived(half(i, n, 3, 0), ag_rs.at[0, i, 0])
        remote(half(i, n, 3, 0), half(i, n, 2, 0), fw_ss, fw_rs.at[0, i], up_y).start()
        arrived(half(i, n, 1, 1), ag_rs.at[1, i, 1])
        remote(half(i, n, 1, 1), half(i, n, 2, 1), fw_ss, fw_rs.at[1, i], down_y).start()

    def send_back(k):
        todo = sorted((dx != 2, a, p, dx, dc) for a, (p, dx) in enumerate(ORDER[k]) for dc in range(NC))
        for _, a, p, dx, dc in todo:
            d = (NX - dx) % NX
            src = eout.at[k, pl.ds(a * UROWS + dc * MAIN, MAIN)]
            dst = back.at[p, pl.ds((d * NC + dc) * MAIN, MAIN)]
            if dx == 0 and dc == 0:
                pltpu.make_async_copy(src, dst, b_rs.at[p, d]).start()
            else:
                remote(src, dst, b_ss, b_rs.at[p, d], mate[dx, dc]).start()

    def down(i, n):
        arrived(half(i, n, 3, 1), ag_rs.at[0, i, 1])
        arrived(half(i, n, 1, 0), ag_rs.at[1, i, 0])
        arrived(half(i, n, 2, 0), fw_rs.at[0, i])
        arrived(half(i, n, 2, 1), fw_rs.at[1, i])
        rows, whole = n * UNIT, n * UROWS
        if len(ORDER[0]) == n:

            @pl.when(i == 0)
            def _():
                for load in to_width:
                    load.wait()

        hidden = jnp.concatenate([hid[i, r, :rows] for r in range(NY)], axis=1)
        erow[:rows] = jnp.dot(hidden, wdn[...], preferred_element_type=F32).astype(BF16)
        eout[i, :whole, :width] = erow[:whole]
        tail = jnp.zeros((whole, block), F32)
        for b in range(CUT):
            last = erow[whole:rows, b * block : (b + 1) * block]
            tail += jnp.dot(picks(n, b, 1), last, preferred_element_type=F32)
        eout[i, :whole, width:] = tail.astype(BF16)
        for k in range(CHUNKS):
            if len(ORDER[k]) == n:
                pl.when(i == k)(lambda k=k: send_back(k))

    def combine(p):
        for d in range(NX):
            arrived(back.at[p, pl.ds(d * UROWS, UROWS)], b_rs.at[p, d])
        span = 2 * PLANE * MAIN
        last = back[p, :, width:]
        for b in range(CUT):
            cols = slice(b * block, (b + 1) * block)
            first = back[p, :, cols]
            weights = jnp.concatenate(
                [shares_all[p, :, :span], shares_all[p, :, (b + 1) * span : (b + 2) * span]], axis=1
            )
            rows = jnp.concatenate([first, first, last, last], axis=0)
            zp[p, :, cols] = jnp.dot(weights, rows, preferred_element_type=F32)

    z_parts = [pl.ds(0, tok // 2), pl.ds(tok // 2, tok // 2)]

    def leave(p):
        out, base, to = (LEFT_OUT, 0, down_z) if p in LEFT_OUT else (RIGHT_OUT, len(LEFT_OUT), up_z)
        h = base + out.index(p)
        for part, rows in enumerate(z_parts):
            at = slice(rows.start, rows.start + rows.size)
            total = zp[p, at]
            if h > base:
                arrived(zr.at[h - 1, rows], z_rs.at[h - 1, part])
                total = total + zr[h - 1, at].astype(F32)
            zs[h, at] = total.astype(BF16)
            remote(zs.at[h, rows], zr.at[h, rows], z_ss, z_rs.at[h, part], to).start()

    ops = {PLANE_IN: z_arrived, COMBINE: combine, LEAVE: leave, SHARE: share}

    def one_of(s, steps):
        hit = s == steps[0]
        for t in steps[1:]:
            hit = jnp.logical_or(hit, s == t)
        return hit

    def perform(todo):
        for op, p in todo:
            ops[op](p)

    for load in inputs:
        load.wait()
    meta_all[0, 0:TOPK, :] = rt_own[...].astype(F32)
    prepare(0)
    select(0)
    pl.semaphore_wait(barrier, len(partners))
    z_send(0)
    dispatch(0)
    for load in [*gate_up[2], *gate_up[1], *gate_up[3], *gate_up[0], *to_width]:
        load.start()
    perform(FIRST)

    def step(s, carry):
        for run, lag, steps, table in (
            (partials, 0, ALL_STEPS, AFTER_P),
            (activate, 1, EARLY_A, AFTER_EARLY_A),
            (middle, 0, EARLY_M, AFTER_EARLY_M),
            (forward, 1, EARLY_F, AFTER_EARLY_F),
            (down, 2, ALL_STEPS, AFTER_D),
            (activate, 1, LATE_A, AFTER_A),
            (middle, 0, LATE_M, AFTER_M),
            (forward, 1, LATE_F, AFTER_F),
        ):
            i = s - lag
            for n in (LARGE, SMALL):
                at = [t for t in steps if 0 <= t - lag < CHUNKS and len(ORDER[t - lag]) == n]
                if at:
                    pl.when(one_of(s, at))(lambda run=run, i=i, n=n: run(i, n))
            for at, todo in table.items():
                pl.when(s == at)(lambda todo=todo: perform(todo))
        return carry

    lax.fori_loop(0, CHUNKS + 2, step, 0)
    perform(LAST)
    last_left, last_right = len(LEFT_OUT) - 1, len(LEFT_OUT) + len(RIGHT_OUT) - 1
    for part, rows in enumerate(z_parts):
        at = slice(rows.start, rows.start + rows.size)
        arrived(zr.at[last_right, rows], z_rs.at[last_right, part])
        arrived(zr.at[last_left, rows], z_rs.at[last_left, part])
        out_ref[at] = (zp[0, at] + zr[last_left, at].astype(F32) + zr[last_right, at].astype(F32)).astype(BF16)

    sent(meta_all.at[pl.ds(1, NZ - 1)], zm_ss)
    sent(tok_all.at[pl.ds(1, NZ - 1)], zt_ss)
    sent(sel.at[:, pl.ds(MAIN, (PLANE - 1) * MAIN)], x_ss)
    sent(hop_s.at[:, pl.ds(0, NZ)], hop_ss)
    sent(qs.at[:, pl.ds(0, NZ)], q_ss)
    sent(hop_s.at[:, pl.ds(0, NZ)], ag_ss)
    sent(hop_s.at[0, pl.ds(0, NZ)], fw_ss)
    sent(sel.at[:, pl.ds(MAIN, (PLANE - 1) * MAIN)], b_ss)
    sent(zs, z_ss)


def shards(tokens, routes, combine_weight, gate_weight, up_weight, down_weight):
    tok, width = tokens.shape
    ff = gate_weight.shape[2]
    fq = ff // NY
    n = CHUNKS
    wide = width + width // CUT
    vm = pltpu.VMEM
    dma = pltpu.SemaphoreType.DMA
    any_space = pl.BlockSpec(memory_space=pl.ANY)
    return pl.pallas_call(
        body,
        out_shape=vm((tok, width), BF16),
        in_specs=[any_space] * 6,
        out_specs=pl.BlockSpec(memory_space=vm),
        scratch_shapes=[
            vm((TOPK, tok), jnp.int32),
            vm((NZ, tok, width), BF16),
            vm((NZ, 2 * TOPK, tok), F32),
            vm((NZ, PLANE, tok), F32),
            vm((NZ, PLANE, tok), F32),
            vm((NZ, tok, 2 * (1 + CUT) * PLANE * MAIN), BF16),
            vm((width, 2 * ff), BF16),
            vm((ff, width), BF16),
            vm((NZ, PLANE * MAIN, wide), BF16),
            vm((n, LARGE * UROWS, wide), BF16),
            vm((ROWS, width), BF16),
            vm((2, n, ROWS, fq), BF16),
            vm((2, n, ROWS, fq), BF16),
            vm((2, ROWS, fq), F32),
            vm((2, n, ROWS, 2 * fq), BF16),
            vm((2, n, ROWS, 2 * fq), BF16),
            vm((2, ROWS, 2 * fq), F32),
            vm((n, NY, ROWS, fq), BF16),
            vm((ROWS, width), BF16),
            vm((n, LARGE * UROWS, wide), BF16),
            vm((NZ, PLANE * MAIN, wide), BF16),
            vm((NZ, tok, width), F32),
            vm((NZ - 1, tok, width), BF16),
            vm((NZ - 1, tok, width), BF16),
            dma((3,)),
            dma((3 * NY,)),
            dma,
            dma((NZ - 1,)),
            dma,
            dma((NZ - 1,)),
            dma,
            dma((n, LARGE)),
            dma,
            dma((2, n, 2)),
            dma,
            dma((2, n, 2)),
            dma,
            dma((2, n, 2)),
            dma,
            dma((2, n)),
            dma,
            dma((NZ, NX)),
            dma,
            dma((NZ - 1, 2)),
        ],
        compiler_params=pltpu.CompilerParams(
            collective_id=0, has_side_effects=True, vmem_limit_bytes=60 * 1024 * 1024
        ),
        cost_estimate=pl.CostEstimate(flops=13 * 10**9, bytes_accessed=10 * 10**6, transcendentals=0),
    )(routes.T, combine_weight.T, tokens, gate_weight[0], up_weight[0], down_weight[0])


def solution(mesh):
    return jax.shard_map(
        shards,
        mesh=mesh,
        in_specs=(
            P("ep", "kv"),
            P("ep", None),
            P("ep", None),
            P("ep", "kv", None),
            P("ep", "kv", None),
            P("ep", None, "kv"),
        ),
        out_specs=P("ep", "kv"),
        check_vma=False,
    )
```
